256 devices in a mesh: lon: 16 (over z, core), lat: 8 (over y, x_hi), tp: 2 (over x_lo).
Axes of the slice: x: 4 (x_hi: 2, x_lo: 2; x = x_hi * 2 + x_lo), y: 4, z: 8, core: 2. Of those that a mesh axis runs over, the one named last changes fastest.
Arguments:
- latent: bfloat16 [192, 96, 4, 512], P('lon', 'lat'), may hold values from -6 to 6
- cotangent: bfloat16 [192, 96, 4, 512], P('lon', 'lat'), may hold values from -6 to 6
- ln_gain: float32 [512], replicated, may hold values from 0.1 to 1.9
- w_qkv: bfloat16 [3, 512, 512], P(None, None, 'tp'), may hold values from -0.25 to 0.25
- w_out: bfloat16 [512, 512], P('tp'), may hold values from -0.25 to 0.25
- bias_table: float32 [16, 2, 8, 3312], P('lat', None, 'tp'), may hold values from -3 to 360
Outputs:
- output: bfloat16 [192, 96, 4, 512], P('lon', 'lat')
- grad_latent: bfloat16 [192, 96, 4, 512], P('lon', 'lat')
- grad_gain: float32 [512], replicated
- grad_wqkv: float32 [3, 512, 512], P(None, None, 'tp')
- grad_wout: float32 [512, 512], P('tp')
- grad_bias: float32 [16, 2, 8, 3312], P('lat', None, 'tp')
The draws below stay inside these ranges and needn't reach their ends.
All inputs are finite; a program needn't handle non-finite values.
Results may differ from the reference program's by a relative error of at most 0.023.
Values may be sent and summed in bfloat16 or wider, within the bound.
No kernel may reach another device: no remote copies, remote signals or barrier semaphores. Data moves between devices by JAX's collectives and lax.ppermute only.
A program may use at most 128 MiB of HBM per device.

```python
import math
import jax
import jax.numpy as jnp
import numpy as np
from jax import lax

D = 512
HEADS = 8
HD = 64
WLON = 12
WLAT = 6
WLEV = 2
LEV = 4
NLON = 192
NLAT = 96
WTOK = 144
NREL = 3312
LATWIN = 16
LEVWIN = 2
N_TP = 2


def draw_bias_table(key, part):
    key = jax.random.fold_in(key, 7)
    shape = (LATWIN, LEVWIN, HEADS, WLEV * WLEV, WLAT * WLAT, 2 * WLON - 1)
    base = jnp.clip(0.5 * jax.random.normal(key, shape, jnp.float32), -3.0, 3.0)
    return base.reshape(LATWIN, LEVWIN, HEADS, NREL).astype(jnp.float32)


def block_scale(own_key, shape, shards, low, high):
    gain = 1.0
    for dim, parts in shards:
        steps = jax.random.uniform(jax.random.fold_in(jax.random.fold_in(own_key, 6), dim), (parts,), jnp.float32, low / len(shards), high / len(shards))
        gain = gain * jnp.repeat(jnp.exp(steps), shape[dim] // parts).reshape((-1,) + (1,) * (len(shape) - 1 - dim))
    return gain


def bell_draw(rng, extent, width, most, shards=(), dtype=jnp.bfloat16):
    drawn = jax.random.normal(rng, extent, jnp.float32) * width
    if len(shards) > 0:
        drawn = block_scale(rng, extent, shards, -0.22, 0.18) * drawn
    return jnp.clip(drawn, min=-most, max=most).astype(dtype)


def setup_inputs(seed: int = 0) -> dict:
    arg_keys = jax.random.split(jax.random.key(seed), 7)
    return {
        "latent": bell_draw(arg_keys[0], (NLON, NLAT, LEV, D), 1.0, 6.0, ((0, 16), (1, 8))),
        "cotangent": bell_draw(arg_keys[1], (NLON, NLAT, LEV, D), 1.0, 6.0, ((0, 16), (1, 8))),
        "ln_gain": jnp.clip(1.0 + 0.18 * jax.random.normal(arg_keys[2], (D,), jnp.float32), 0.1, 1.9),
        "w_qkv": bell_draw(arg_keys[3], (3, D, D), D ** -0.5, 0.25, ((2, 2),)),
        "w_out": bell_draw(arg_keys[4], (D, D), D ** -0.5, 0.25, ((0, 2),)),
        "bias_table": draw_bias_table(jax.random.fold_in(arg_keys[6], 71), 0),
    }


def pair_layout():
    position = np.arange(WTOK)
    lon_pos = position // (WLAT * WLEV)
    lat_pos = position // WLEV % WLAT
    lev_pos = position % WLEV
    relative = lon_pos[None, :] - lon_pos[:, None] + WLON - 1
    entries = ((lev_pos[:, None] * WLEV + lev_pos[None, :]) * WLAT * WLAT + lat_pos[:, None] * WLAT + lat_pos[None, :]) * (2 * WLON - 1) + relative
    return (entries.astype(np.int32), lat_pos, lev_pos)

def to_windows(values):
    lon_cells, lat_cells, lev_cells, channels = values.shape
    blocks = values.reshape(lon_cells // WLON, WLON, lat_cells // WLAT, WLAT, lev_cells // WLEV, WLEV, channels)
    blocks = blocks.transpose(2, 4, 0, 1, 3, 5, 6)
    return blocks.reshape(lat_cells // WLAT, lev_cells // WLEV, lon_cells // WLON, WTOK, channels)

def from_windows(values):
    lat_bands, lev_bands, lon_bands, window_len, channels = values.shape
    blocks = values.reshape(lat_bands, lev_bands, lon_bands, WLON, WLAT, WLEV, channels)
    blocks = blocks.transpose(2, 3, 0, 4, 1, 5, 6)
    return blocks.reshape(lon_bands * WLON, lat_bands * WLAT, lev_bands * WLEV, channels)

def allowed_pairs(last_lat, lev_bands, lat_pos, lev_pos):
    lat_edge = jnp.asarray(lat_pos >= WLAT - WLAT // 2)
    lev_edge = jnp.asarray(lev_pos >= WLEV - WLEV // 2)
    lev_last = jnp.arange(lev_bands) == lev_bands - 1
    lat_region = last_lat[:, None] & lat_edge[None, :]
    lev_region = lev_last[:, None] & lev_edge[None, :]
    same_lat = lat_region[:, :, None] == lat_region[:, None, :]
    same_lev = lev_region[:, :, None] == lev_region[:, None, :]
    return same_lat[:, None] & same_lev[None, :]

def layer_norm(values, scale_gain):
    values = values.astype(jnp.float32)
    centre = lax.optimization_barrier(jnp.mean(values, -1, keepdims=True))
    shifted = values - centre
    inv_std = lax.rsqrt(lax.optimization_barrier(jnp.mean(shifted * shifted, -1, keepdims=True)) + 1e-05)
    normed = shifted * inv_std
    return (normed, inv_std, (normed * scale_gain).astype(jnp.bfloat16))

def rounded_sum(partials):
    total = jnp.zeros(partials[0].shape, jnp.float32)
    for partial_value in partials:
        total = total + lax.optimization_barrier(partial_value.astype(jnp.bfloat16)).astype(jnp.float32)
    return total.astype(jnp.bfloat16)

def reference(latent, cotangent, ln_gain, w_qkv, w_out, bias_table):
    entries, lat_pos, lev_pos = pair_layout()
    entry_ids = jnp.asarray(entries)
    shifts = (-(WLON // 2), -(WLAT // 2), -(WLEV // 2))
    scale_gain = ln_gain.astype(jnp.float32)
    inv_scale = 1.0 / math.sqrt(HD)
    group_width = D // N_TP

    def bands_of(values):
        rolled = jnp.roll(values, shifts, axis=(0, 1, 2))
        return rolled.reshape(NLON, LATWIN, WLAT, LEV, D).transpose(1, 0, 2, 3, 4)

    def band_step(carry, band):
        grad_qkv, grad_out, grad_gain = carry
        latent_band, cot_band, table_band, band_number = band
        latent_win = to_windows(latent_band)
        cot_win = to_windows(cot_band)
        lev_bands = latent_win.shape[1]
        lon_bands = latent_win.shape[2]
        last_lat = jnp.reshape(band_number == LATWIN - 1, (1,))
        allowed = allowed_pairs(last_lat, lev_bands, lat_pos, lev_pos)
        bias_full = jnp.take(table_band, entry_ids, axis=2)[None]
        normed, inv_std, hidden = layer_norm(latent_win, scale_gain)
        hidden_flat = hidden.reshape(-1, D)
        head_shape = (1, lev_bands, lon_bands, WTOK, HEADS, HD)
        projected = [jnp.dot(hidden_flat, w_qkv[member], preferred_element_type=jnp.float32).astype(jnp.bfloat16) for member in range(3)]
        queries, key_rows, value_rows = [matrix.reshape(head_shape).astype(jnp.float32) for matrix in projected]
        scores = jnp.einsum('abwqhe,abwkhe->abwhqk', queries, key_rows) * inv_scale + bias_full[:, :, None]
        scores = jnp.where(allowed[:, :, None, None], scores, -jnp.inf)
        row_max = lax.optimization_barrier(jnp.max(scores, -1, keepdims=True))
        expsum = jnp.exp(scores - row_max)
        attn_weights = expsum / lax.optimization_barrier(jnp.sum(expsum, -1, keepdims=True))
        attn_low = attn_weights.astype(jnp.bfloat16)
        attended = jnp.einsum('abwhqk,abwkhe->abwqhe', attn_low.astype(jnp.float32), value_rows).astype(jnp.bfloat16)
        attended_flat = attended.reshape(-1, D)
        out_terms = [jnp.dot(attended_flat[:, group * group_width:(group + 1) * group_width], w_out[group * group_width:(group + 1) * group_width], preferred_element_type=jnp.float32) for group in range(N_TP)]
        attn_out = rounded_sum(out_terms)
        result = (latent_win.reshape(-1, D).astype(jnp.float32) + attn_out.astype(jnp.float32)).astype(jnp.bfloat16)
        cot_flat = cot_win.reshape(-1, D)
        grad_out = grad_out + jnp.dot(attended_flat.T, cot_flat, preferred_element_type=jnp.float32)
        down_heads = jnp.dot(cot_flat, w_out.T, preferred_element_type=jnp.float32).astype(jnp.bfloat16).reshape(head_shape).astype(jnp.float32)
        down_scores = jnp.einsum('abwqhe,abwkhe->abwhqk', down_heads, value_rows)
        grad_values = jnp.einsum('abwhqk,abwqhe->abwkhe', attn_low.astype(jnp.float32), down_heads).astype(jnp.bfloat16)
        centred = lax.optimization_barrier(jnp.sum(down_scores * attn_weights, -1, keepdims=True))
        grad_scores = attn_weights * (down_scores - centred)
        bias_terms = lax.optimization_barrier(jnp.sum(grad_scores, 2))
        grad_table = jax.ops.segment_sum(bias_terms.reshape(-1, WTOK * WTOK).T, entry_ids.reshape(-1), num_segments=NREL).T
        grad_table = grad_table.reshape(table_band.shape)
        scores_low = grad_scores.astype(jnp.bfloat16).astype(jnp.float32)
        grad_queries = (jnp.einsum('abwhqk,abwkhe->abwqhe', scores_low, key_rows) * inv_scale).astype(jnp.bfloat16)
        grad_keys = (jnp.einsum('abwhqk,abwqhe->abwkhe', scores_low, queries) * inv_scale).astype(jnp.bfloat16)
        grads_proj = [matrix.reshape(-1, D) for matrix in (grad_queries, grad_keys, grad_values)]
        grad_qkv = grad_qkv + jnp.stack([jnp.dot(hidden_flat.T, matrix, preferred_element_type=jnp.float32) for matrix in grads_proj])
        hidden_terms = []
        for group in range(N_TP):
            columns = slice(group * group_width, (group + 1) * group_width)
            partial_value = jnp.zeros((hidden_flat.shape[0], D), jnp.float32)
            for member in range(3):
                partial_value = partial_value + jnp.dot(grads_proj[member][:, columns], w_qkv[member][:, columns].T, preferred_element_type=jnp.float32)
            hidden_terms.append(partial_value)
        grad_hidden = rounded_sum(hidden_terms).astype(jnp.float32)
        normed_flat = normed.reshape(-1, D)
        inv_flat = inv_std.reshape(-1, 1)
        scaled = grad_hidden * scale_gain
        grad_in = cot_flat.astype(jnp.float32) + inv_flat * (scaled - lax.optimization_barrier(jnp.mean(scaled, -1, keepdims=True)) - normed_flat * lax.optimization_barrier(jnp.mean(scaled * normed_flat, -1, keepdims=True)))
        grad_gain = grad_gain + lax.optimization_barrier(jnp.sum(grad_hidden * normed_flat, 0))
        win_shape = latent_win.shape
        result_band = from_windows(result.reshape(win_shape))
        grad_band = from_windows(grad_in.astype(jnp.bfloat16).reshape(win_shape))
        return ((grad_qkv, grad_out, grad_gain), (result_band, grad_band, grad_table))
    init = (jnp.zeros((3, D, D), jnp.float32), jnp.zeros((D, D), jnp.float32), jnp.zeros((D,), jnp.float32))
    band_ids = jnp.arange(LATWIN).astype(jnp.int32)
    carry, stacked = lax.scan(band_step, init, (bands_of(latent), bands_of(cotangent), bias_table, band_ids))
    grad_wqkv, grad_wout, grad_gain = carry
    result_bands, grad_bands, grad_bias = stacked

    def unbands(values):
        whole = values.transpose(1, 0, 2, 3, 4).reshape(NLON, NLAT, LEV, D)
        return jnp.roll(whole, (WLON // 2, WLAT // 2, WLEV // 2), axis=(0, 1, 2))
    return (unbands(result_bands), unbands(grad_bands), grad_gain, grad_wqkv, grad_wout, grad_bias)
```

```python
import jax
import jax.numpy as jnp
import numpy as np
from jax import lax
from jax.experimental import pallas as pl
from jax.experimental.pallas import tpu as pltpu
from jax.sharding import PartitionSpec as P

BF = jnp.bfloat16
F32 = jnp.float32
WTOK = 144
OFFS = 23
NT = (((1,), (1,)), ((), ()))
TN = (((0,), (0,)), ((), ()))
SECTIONS = (216, 216, 72, 72)


def section_rows(lon, lat, lev, low):
    lon_first, lat_first = lon < 6, lat < 9
    if low:
        lon_first, lat_first = lon >= 6, lat >= 3
        lon_at = lon - 6 if lon_first else lon
        lat_at = lat - 3 if lat_first else lat
    else:
        lon_at = lon if lon_first else lon - 6
        lat_at = lat if lat_first else lat - 9
    section = (0 if lon_first else 1) + (0 if lat_first else 2)
    return section, (lon_at * (9 if lat_first else 3) + lat_at) * 4 + lev


def placements():
    to_window = [np.zeros((576, n), np.float32) for n in SECTIONS]
    to_owner = [np.zeros((576, n), np.float32) for n in SECTIONS]
    for a in range(2):
        for b in range(2):
            for p in range(12):
                for s in range(2):
                    for r in range(6):
                        row = (a * 2 + b) * WTOK + p * 12 + s * 6 + r
                        section, at = section_rows(p, a * 6 + r, (b * 2 + s + 1) % 4, False)
                        to_window[section][row, at] = 1
    for lon in range(12):
        for lat in range(12):
            for lev in range(4):
                section, at = section_rows(lon, lat, lev, True)
                to_owner[section][(lon * 12 + lat) * 4 + lev, at] = 1
    return to_window, to_owner


def offset_matrix():
    spread = np.zeros((12, 12 * OFFS, WTOK), np.float32)
    for p_t in range(12):
        for p_u in range(12):
            for rs in range(12):
                spread[p_t, rs * OFFS + p_u - p_t + 11, p_u * 12 + rs] = 1
    return spread


TO_WINDOW, TO_OWNER = placements()
SPREAD = offset_matrix()


def dot(a, b, dims=(((1,), (0,)), ((), ()))):
    return lax.dot_general(a, b, dims, preferred_element_type=F32)


def call(body, outs, args, scratch=(), smem=1):
    vmem = pl.BlockSpec(memory_space=pltpu.VMEM)
    return pl.pallas_call(
        body,
        out_shape=[jax.ShapeDtypeStruct(s, t) for s, t in outs],
        in_specs=[pl.BlockSpec(memory_space=pltpu.SMEM)] * smem + [vmem] * (len(args) - smem),
        out_specs=[vmem] * len(outs),
        scratch_shapes=list(scratch),
        compiler_params=pltpu.CompilerParams(vmem_limit_bytes=50 * 1024 * 1024),
    )(*args)


def bias_kernel(info, table, spread, bias):
    full = table[...]
    high = full.astype(BF)
    rest = full - high.astype(F32)
    mid = rest.astype(BF)
    low = (rest - mid.astype(F32)).astype(BF)
    row = lax.broadcasted_iota(jnp.int32, (192, WTOK), 0)
    col = lax.broadcasted_iota(jnp.int32, (192, WTOK), 1)
    rs_t, rs_u = row % 12, col % 12
    s_t, s_u = (rs_t >= 6).astype(jnp.int32), (rs_u >= 6).astype(jnp.int32)
    edge_t = (rs_t - s_t * 6 >= 3).astype(jnp.int32)
    edge_u = (rs_u - s_u * 6 >= 3).astype(jnp.int32)
    last_lat = (row >= 96).astype(jnp.int32) * info[0]
    last_lev = ((row % 96) >= 48).astype(jnp.int32)
    barred = (last_lat * (edge_t - edge_u) != 0) | (last_lev * (s_t - s_u) != 0)
    for p in range(12):
        at = dot(low, spread[p]) + dot(mid, spread[p])
        at = at + dot(high, spread[p])
        at = jnp.where(barred, -jnp.inf, at)
        for i in range(16):
            bias[i * WTOK + p * 12 : i * WTOK + p * 12 + 12, :] = at[i * 12 : i * 12 + 12]


def main_kernel(info, own, lon, lat, cor, t0, t1, t2, t3, b0, b1, b2, b3, gain, w_qkv, w_out, bias,
                o_own, o_lon, o_lat, o_cor, keep, send, o_ds, att_s, gq_s, gk_s, gv_s):
    def gathered(which):
        return dot(t0[...], own[which]) + dot(t1[...], lon[which]) + dot(t2[...], lat[which]) + dot(t3[...], cor[which])

    values = gathered(0)
    cot = gathered(1).astype(BF)
    shifted = values - jnp.mean(values, -1, keepdims=True)
    normed = shifted * lax.rsqrt(jnp.mean(shifted * shifted, -1, keepdims=True) + 1e-05)
    hidden = (normed * gain[...]).astype(BF)
    q, k, v = [dot(hidden, w_qkv[j]).astype(BF) for j in range(3)]
    down = dot(cot, w_out[...], NT).astype(BF)
    head = lax.broadcasted_iota(jnp.int32, (WTOK, 256), 1) // 64

    def stacked(rows):
        return jnp.concatenate([jnp.where(head == h, rows, jnp.zeros_like(rows)) for h in range(4)], 0)

    def unstacked(rows):
        total = jnp.zeros((WTOK, 256), F32)
        for h in range(4):
            total = jnp.where(head == h, rows[h * WTOK : (h + 1) * WTOK], total)
        return total

    for w in range(4):
        rows = slice(w * WTOK, (w + 1) * WTOK)
        four = slice(w * 576, (w + 1) * 576)
        qs, ds_ = stacked(q[rows]), stacked(down[rows])
        scores = dot(qs, k[rows], NT) * 0.125 + bias[four, :]
        exps = jnp.exp(scores - jnp.max(scores, -1, keepdims=True))
        probs = exps / jnp.sum(exps, -1, keepdims=True)
        probs_low = probs.astype(BF)
        att_s[rows, :] = unstacked(dot(probs_low, v[rows])).astype(BF)
        dp = dot(ds_, v[rows], NT)
        gv_s[rows, :] = dot(probs_low, ds_, TN).astype(BF)
        grad = probs * (dp - jnp.sum(dp * probs, -1, keepdims=True))
        o_ds[four, :] = grad
        grad_low = grad.astype(BF)
        gq_s[rows, :] = unstacked(dot(grad_low, k[rows]) * 0.125).astype(BF)
        gk_s[rows, :] = (dot(grad_low, qs, TN) * 0.125).astype(BF)

    att, gq, gk, gv = att_s[...], gq_s[...], gk_s[...], gv_s[...]
    out_part = dot(att, w_out[...]).astype(BF)
    hid_part = (dot(gq, w_qkv[0], NT) + dot(gk, w_qkv[1], NT) + dot(gv, w_qkv[2], NT)).astype(BF)
    for back, ref in ((b0, o_own), (b1, o_lon), (b2, o_lat), (b3, o_cor)):
        ref[0] = dot(back[...], out_part).astype(BF)
        ref[1] = dot(back[...], hid_part).astype(BF)
    wo = dot(att, cot, TN)
    first = [dot(hidden, gq, TN), dot(hidden, gk, TN)]
    second = [dot(hidden, gv, TN), jnp.concatenate([wo[:, :256], wo[:, 256:]], 0)]
    core = info[1]
    for j in range(2):
        rows = slice(j * 512, (j + 1) * 512)
        keep[rows, :] = jnp.where(core == 0, first[j], second[j])
        send[rows, :] = jnp.where(core == 0, second[j], first[j]).astype(BF)

def core_sum_kernel(keep, recv, total):
    total[...] = (keep[...] + recv[...].astype(F32)).astype(BF)


def chip_sum_kernel(parts, out):
    total = parts[0].astype(F32)
    for j in range(1, 64):
        total = total + parts[j].astype(F32)
    total = total.astype(BF)
    for j in range(64):
        out[j] = total


def weights_kernel(info, mine, other, w_qkv, wqkv, wout, gain):
    first = jnp.where(info[1] == 0, mine[...], other[...]).astype(F32)
    second = jnp.where(info[1] == 0, other[...], mine[...]).astype(F32)
    wqkv[0] = first[:512]
    wqkv[1] = first[512:]
    wqkv[2] = second[:512]
    wout[:, 0:256] = second[512:768]
    wout[:, 256:512] = second[768:]
    total = first[:512] * w_qkv[0].astype(F32)
    total = total + first[512:] * w_qkv[1].astype(F32)
    total = total + second[:512] * w_qkv[2].astype(F32)
    gain[...] = jnp.sum(total, -1, keepdims=True)


def bias_grad_kernel(info, ds, spread, keep, send, part):
    total = jnp.zeros((192, 12 * OFFS), F32)
    for p in range(12):
        for i in range(16):
            part[i * 12 : i * 12 + 12, :] = ds[i * WTOK + p * 12 : i * WTOK + p * 12 + 12, :]
        rows = part[...]
        high = rows.astype(BF)
        low = (rows - high.astype(F32)).astype(BF)
        total = total + dot(high, spread[p], NT) + dot(low, spread[p], NT)
    keep[...] = jnp.where(info[1] == 0, total[:96], total[96:])
    send[...] = jnp.where(info[1] == 0, total[96:], total[:96]).astype(BF)


def pair_sum_kernel(a1, a2, a3, b1, b2, b3, o1, o2, o3):
    for a, b, o in ((a1, b1, o1), (a2, b2, o2), (a3, b3, o3)):
        o[...] = (a[...].astype(F32) + b[...].astype(F32)).astype(BF)


def final_kernel(latent, cot, gain, own_a, own_b, lon, lat, cor, t0, t1, t2, t3, output, grad):
    own = [(own_a[j].astype(F32) + own_b[j].astype(F32)).astype(BF) for j in range(2)]

    def placed(which):
        return dot(t0[...], own[which]) + dot(t1[...], lon[which]) + dot(t2[...], lat[which]) + dot(t3[...], cor[which])

    values = latent[...].astype(F32)
    output[...] = (values + placed(0)).astype(BF)
    shifted = values - jnp.mean(values, -1, keepdims=True)
    inv_std = lax.rsqrt(jnp.mean(shifted * shifted, -1, keepdims=True) + 1e-05)
    normed = shifted * inv_std
    scaled = placed(1) * gain[...]
    inner = scaled - jnp.mean(scaled, -1, keepdims=True) - normed * jnp.mean(scaled * normed, -1, keepdims=True)
    grad[...] = (cot[...].astype(F32) + inv_std * inner).astype(BF)


def moved(value, by_lon, by_lat):
    n_lon, n_lat = lax.axis_size("lon"), lax.axis_size("lat")
    pairs = [
        (i * n_lat + j, (i + by_lon) % n_lon * n_lat + (j + by_lat) % n_lat)
        for i in range(n_lon)
        for j in range(n_lat)
    ]
    return lax.ppermute(value, ("lon", "lat"), pairs)


def swapped(value, lon_bits, lat_bits):
    n_lon, n_lat = lax.axis_size("lon"), lax.axis_size("lat")
    pairs = [(i * n_lat + j, (i ^ lon_bits) * n_lat + (j ^ lat_bits)) for i in range(n_lon) for j in range(n_lat)]
    return lax.ppermute(value, ("lon", "lat"), pairs)


def chip_groups():
    n_lon, n_lat = lax.axis_size("lon"), lax.axis_size("lat")
    return [[i * n_lat + j for i in range(core, n_lon, 2) for j in range(n_lat)] for core in range(2)]


def other_group(value):
    return lax.ppermute(value, "tp", [(0, 1), (1, 0)])


def on_device(latent, cotangent, ln_gain, w_qkv, w_out, bias_table):
    to_window = [jnp.asarray(m, BF) for m in TO_WINDOW]
    to_section = [jnp.asarray(m.T, BF) for m in TO_WINDOW]
    to_owner = [jnp.asarray(m, BF) for m in TO_OWNER]
    spread = jnp.asarray(SPREAD, BF)
    i_lon, i_lat = lax.axis_index("lon"), lax.axis_index("lat")
    last = (i_lat == lax.axis_size("lat") - 1).astype(jnp.int32)
    core = i_lon % 2
    info = jnp.stack([last, core]).astype(jnp.int32)
    gain = ln_gain.reshape(1, 512)

    def section(lon, lat):
        return jnp.stack([latent[lon, lat].reshape(-1, 512), cotangent[lon, lat].reshape(-1, 512)])

    low_lon, low_lat, high_lon, high_lat = slice(0, 6), slice(0, 3), slice(6, 12), slice(3, 12)
    in_lon = moved(section(low_lon, high_lat), -1, 0)
    in_lat = moved(section(high_lon, low_lat), 0, -1)
    in_cor = moved(section(low_lon, low_lat), -1, -1)
    in_own = section(high_lon, high_lat)

    table = bias_table.reshape(16, 2, 2, 6, 6 * OFFS).transpose(0, 1, 3, 2, 4).reshape(192, 12 * OFFS)
    (bias,) = call(bias_kernel, [((16 * WTOK, WTOK), F32)], [info, table, spread])

    part = lambda n: ((2, n, 512), BF)
    p_own, p_lon, p_lat, p_cor, keep, send, ds = call(
        main_kernel,
        [part(216), part(216), part(72), part(72), ((1024, 256), F32), ((1024, 256), BF), ((16 * WTOK, WTOK), F32)],
        [info, in_own, in_lon, in_lat, in_cor, *to_window, *to_section, gain, w_qkv, w_out, bias],
        [pltpu.VMEM((576, 256), BF)] * 4,
    )

    recv = swapped(send, 1, 0)
    (total,) = call(core_sum_kernel, [((1024, 256), BF)], [keep, recv], smem=0)
    groups = chip_groups()
    parts = lax.all_to_all(total.reshape(64, 16, 256), ("lon", "lat"), 0, 0, axis_index_groups=groups)
    (copies,) = call(chip_sum_kernel, [((64, 16, 256), BF)], [parts], smem=0)
    mine = lax.all_to_all(copies, ("lon", "lat"), 0, 0, axis_index_groups=groups).reshape(1024, 256)
    grad_wqkv, grad_wout, gain_part = call(
        weights_kernel,
        [((3, 512, 256), F32), ((256, 512), F32), ((512, 1), F32)],
        [info, mine, swapped(mine, 1, 0), w_qkv],
    )
    gain_part = gain_part.reshape(512)
    grad_gain = (gain_part + other_group(gain_part)) / ln_gain

    b_keep, b_send = call(
        bias_grad_kernel,
        [((96, 12 * OFFS), F32), ((96, 12 * OFFS), BF)],
        [info, ds, spread],
        [pltpu.VMEM((192, WTOK), F32)],
    )
    b_sum = (b_keep + swapped(b_send, 1, 0).astype(F32)).astype(BF)
    for bits in (2, 4, 8):
        b_sum = (b_sum.astype(F32) + swapped(b_sum, bits, 0).astype(F32)).astype(BF)
    b_other = swapped(b_sum, 1, 0)
    b_all = jnp.where(core == 0, jnp.stack([b_sum, b_other]), jnp.stack([b_other, b_sum]))
    grad_bias = b_all.reshape(16, 2, 6, 2, 6 * OFFS).transpose(0, 1, 3, 2, 4).astype(F32)
    grad_bias = grad_bias.reshape(bias_table.shape)

    halves = [p_lon, p_lat, p_cor]
    others = [other_group(p) for p in halves]
    own_other = other_group(p_own)
    s_lon, s_lat, s_cor = call(pair_sum_kernel, [part(216), part(72), part(72)], halves + others, smem=0)
    r_lon, r_lat, r_cor = moved(s_lon, 1, 0), moved(s_lat, 0, 1), moved(s_cor, 1, 1)
    output, grad_latent = call(
        final_kernel,
        [((576, 512), BF), ((576, 512), BF)],
        [latent.reshape(576, 512), cotangent.reshape(576, 512), gain, p_own, own_other, r_lon, r_lat, r_cor, *to_owner],
        smem=0,
    )
    return (
        output.reshape(latent.shape),
        grad_latent.reshape(latent.shape),
        grad_gain,
        grad_wqkv,
        grad_wout,
        grad_bias,
    )


def solution(mesh):
    specs = (
        P("lon", "lat", None, None),
        P("lon", "lat", None, None),
        P(),
        P(None, None, "tp"),
        P("tp", None),
        P("lat", None, "tp", None),
    )
    return jax.shard_map(on_device, mesh=mesh, in_specs=specs, out_specs=specs, check_vma=False)
```

```python
import jax
import jax.numpy as jnp
import numpy as np
from jax import lax
from jax.experimental import pallas as pl
from jax.experimental.pallas import tpu as pltpu
from jax.sharding import PartitionSpec as P

BF = jnp.bfloat16
F32 = jnp.float32
WTOK = 144
OFFS = 23
NT = (((1,), (1,)), ((), ()))
TN = (((0,), (0,)), ((), ()))
SECTIONS = (0, 216, 432, 504, 576)


def section_row(lon, lat, lev):
    lat_cells = 9 if lat < 9 else 3
    return (lon >= 6) + 2 * (lat >= 9), (lon % 6 * lat_cells + lat % 9) * 4 + lev


def placement():
    place = np.zeros((576, 576), np.float32)
    for a in range(2):
        for b in range(2):
            for p in range(12):
                for s in range(2):
                    for r in range(6):
                        row = (a * 2 + b) * WTOK + p * 12 + s * 6 + r
                        section, at = section_row(p, a * 6 + r, (b * 2 + s + 1) % 4)
                        place[row, SECTIONS[section] + at] = 1
    return place


def offset_order():
    order = np.zeros((276, 276), np.float32)
    for rs in range(12):
        for k in range(OFFS):
            order[rs * OFFS + k, k * 12 + rs] = 1
    return order


TO_WINDOW = placement()
ORDER = offset_order()


def dot(a, b, dims=(((1,), (0,)), ((), ()))):
    return lax.dot_general(a, b, dims, preferred_element_type=F32)


def call(body, outs, args, scratch=(), smem=1, after=(), us=1, mib=16, hbm=(), hbm_outs=()):
    vmem, far = pl.BlockSpec(memory_space=pltpu.VMEM), pl.BlockSpec(memory_space=pltpu.HBM)
    n = len(args)
    m = n + len(hbm)

    def kernel(*refs):
        body(*refs[:m], *refs[m + len(after) :])

    return pl.pallas_call(
        kernel,
        out_shape=[jax.ShapeDtypeStruct(s, t) for s, t in [*outs, *hbm_outs]],
        in_specs=[pl.BlockSpec(memory_space=pltpu.SMEM)] * smem
        + [vmem] * (n - smem)
        + [far] * len(hbm)
        + [pl.BlockSpec(memory_space=pl.ANY)] * len(after),
        out_specs=[vmem] * len(outs) + [far] * len(hbm_outs),
        scratch_shapes=list(scratch),
        compiler_params=pltpu.CompilerParams(vmem_limit_bytes=mib * 1024 * 1024),
        cost_estimate=pl.CostEstimate(flops=int(us * 1e9), bytes_accessed=0, transcendentals=0),
    )(*args, *hbm, *after)


TOKEN = ((8, 128), F32)


LOW_LON, LOW_LAT, HIGH_LON, HIGH_LAT = slice(0, 6), slice(0, 3), slice(6, 12), slice(3, 12)
PLACES = ((HIGH_LON, HIGH_LAT), (LOW_LON, HIGH_LAT), (HIGH_LON, LOW_LAT), (LOW_LON, LOW_LAT))


def halo_kernel(latent, cot, o_lon, o_lat, o_cor, tiles, sems):
    copies = []
    for j, grid in enumerate((latent, cot)):
        for k in range(4):
            rows = pl.ds(3 * k, 3)
            copies.append(pltpu.make_async_copy(grid.at[rows], tiles.at[j, rows], sems.at[4 * j + k]))
            copies[-1].start()
    for copy in copies:
        copy.wait()
    for (lon, lat), ref in zip(PLACES[1:], (o_lon, o_lat, o_cor)):
        for j in range(2):
            ref[j] = tiles[j, lon, lat].reshape(ref.shape[1:])


def bias_kernel(info, table, order, w_out, bias, w_copy, raw, entries, low_u, high_u):
    w_copy[...] = w_out[...]
    flat = table[...].reshape(16, 3312)
    for s_t in range(2):
        for s_u in range(2):
            for r_t in range(6):
                at = ((s_t * 2 + s_u) * 6 + r_t) * 138
                row = (s_t * 6 + r_t) * 16
                raw[row : row + 16, s_u * 138 : s_u * 138 + 138] = flat[:, at : at + 138]
    full = raw[...]
    high = full.astype(BF)
    rest = full - high.astype(F32)
    mid = rest.astype(BF)
    low = (rest - mid.astype(F32)).astype(BF)
    entries[...] = dot(low, order[...]) + dot(mid, order[...]) + dot(high, order[...])
    row = lax.broadcasted_iota(jnp.int32, (192, WTOK), 0)
    col = lax.broadcasted_iota(jnp.int32, (192, WTOK), 1)
    rs_t, rs_u, which = row // 16, col % 12, row % 16
    s_t, s_u = (rs_t >= 6).astype(jnp.int32), (rs_u >= 6).astype(jnp.int32)
    edge_t = (rs_t - s_t * 6 >= 3).astype(jnp.int32)
    edge_u = (rs_u - s_u * 6 >= 3).astype(jnp.int32)
    last_lat = (which >= 8).astype(jnp.int32) * info[0]
    last_lev = ((which % 8) >= 4).astype(jnp.int32)
    barred = (last_lat * (edge_t - edge_u) != 0) | (last_lev * (s_t - s_u) != 0)
    for p in range(12):
        at = entries[:, (11 - p) * 12 : (11 - p) * 12 + WTOK]
        at = jnp.where(barred, -jnp.inf, at)
        low_u[...] = at[:, 0:128]
        high_u[:, 0:16] = at[:, 128:144]
        for i in range(16):
            rows = slice(i * WTOK + p * 12, i * WTOK + p * 12 + 12)
            bias[rows, 0:128] = low_u[pl.ds(i, 12, stride=16), :]
            bias[rows, 128:WTOK] = high_u[pl.ds(i, 12, stride=16), :][:, 0:16]


def main_kernel(info, latent, cotangent, lon, lat, cor, place, gain, w_qkv, w_out, bias,
                keep, send, o_ds, att_s, gq_s, gk_s, gv_s, joined):
    def gathered(which):
        own = (latent, cotangent)[which][HIGH_LON, HIGH_LAT].reshape(216, 512)
        for j, rows in enumerate((own, lon[which], lat[which], cor[which])):
            joined[SECTIONS[j] : SECTIONS[j + 1], :] = rows.astype(F32)
        return dot(place[...], joined[...].astype(BF))

    values = gathered(0)
    cot = gathered(1).astype(BF)
    shifted = values - jnp.mean(values, -1, keepdims=True)
    normed = shifted * lax.rsqrt(jnp.mean(shifted * shifted, -1, keepdims=True) + 1e-05)
    hidden = (normed * gain[...]).astype(BF)
    q, k, v = [dot(hidden, w_qkv[j]).astype(BF) for j in range(3)]
    down = dot(cot, w_out[...], NT).astype(BF)
    head = lax.broadcasted_iota(jnp.int32, (WTOK, 256), 1) // 64

    def stacked(rows):
        return jnp.concatenate([jnp.where(head == h, rows, jnp.zeros_like(rows)) for h in range(4)], 0)

    def unstacked(rows):
        total = jnp.zeros((WTOK, 256), F32)
        for h in range(4):
            total = jnp.where(head == h, rows[h * WTOK : (h + 1) * WTOK], total)
        return total

    for w in range(4):
        rows = slice(w * WTOK, (w + 1) * WTOK)
        four = slice(w * 576, (w + 1) * 576)
        qs, ds_ = stacked(q[rows]), stacked(down[rows])
        scores = dot(qs, k[rows], NT) * 0.125 + bias[four, :]
        exps = jnp.exp(scores - jnp.max(scores, -1, keepdims=True))
        probs = exps / jnp.sum(exps, -1, keepdims=True)
        probs_low = probs.astype(BF)
        att_s[rows, :] = unstacked(dot(probs_low, v[rows])).astype(BF)
        dp = dot(ds_, v[rows], NT)
        gv_s[rows, :] = dot(probs_low, ds_, TN).astype(BF)
        grad = probs * (dp - jnp.sum(dp * probs, -1, keepdims=True))
        o_ds[four, :] = grad
        grad_low = grad.astype(BF)
        gq_s[rows, :] = unstacked(dot(grad_low, k[rows]) * 0.125).astype(BF)
        gk_s[rows, :] = (dot(grad_low, qs, TN) * 0.125).astype(BF)

    att, gq, gk, gv = att_s[...], gq_s[...], gk_s[...], gv_s[...]
    wo = dot(att, cot, TN)
    first = [dot(hidden, gq, TN), dot(hidden, gk, TN)]
    second = [dot(hidden, gv, TN), jnp.concatenate([wo[:, :256], wo[:, 256:]], 0)]
    core = info[1]
    for j in range(2):
        rows = slice(j * 512, (j + 1) * 512)
        keep[rows, :] = jnp.where(core == 0, first[j], second[j])
        send[rows, :] = jnp.where(core == 0, second[j], first[j]).astype(BF)

def terms_kernel(att, gq, gk, gv, w_qkv, back, terms):
    hid_part = dot(gq[...], w_qkv[0], NT) + dot(gk[...], w_qkv[1], NT) + dot(gv[...], w_qkv[2], NT)
    terms[:, 0:256] = dot(back[...], att[...]).astype(BF)
    terms[:, 256:768] = dot(back[...], hid_part.astype(BF)).astype(BF)


def core_sum_kernel(keep, recv, total):
    total[...] = (keep[...] + recv[...].astype(F32)).astype(BF)


def y_sum_kernel(parts, b_keep, b_recv, message):
    total = parts[0].astype(F32)
    for j in range(1, 4):
        total = total + parts[j].astype(F32)
    total = total.astype(BF)
    tail = jnp.zeros((16, 118), BF)
    for z in range(8):
        for x in range(2):
            j = z * 2 + x
            message[j, 0:16, :] = total[j * 16 : (j + 1) * 16]
            both = (b_keep[z, x].astype(F32) + b_recv[z, x].astype(F32)).astype(BF)
            message[j, 16:32, :] = jnp.concatenate([both, tail], 1)


def zx_sum_kernel(parts, copies):
    total = jnp.zeros((16, 256), F32)
    biases = []
    for x in range(2):
        bias = jnp.zeros((16, 256), F32)
        for z in range(8):
            total = total + parts[z * 2 + x, 0:16, :].astype(F32)
            bias = bias + parts[z * 2 + x, 16:32, :].astype(F32)
        biases.append(bias.astype(BF))
    total = total.astype(BF)
    for z in range(8):
        for x in range(2):
            copies[z * 2 + x, 0:16, :] = total
            copies[z * 2 + x, 16:32, :] = biases[x]


def pair_kernel(terms, others, w_out, w_other, o_own, o_lon, o_lat, o_cor, held, sems):
    copies = []
    for j, w in enumerate((w_out, w_other)):
        for k in range(2):
            rows = pl.ds(128 * k, 128)
            copies.append(pltpu.make_async_copy(w.at[rows], held.at[j, rows], sems.at[2 * j + k]))
            copies[-1].start()
    for copy in copies:
        copy.wait()
    out = dot(terms[:, 0:256], held[0]).astype(BF).astype(F32)
    out = out + dot(others[:, 0:256], held[1]).astype(BF).astype(F32)
    hid = terms[:, 256:768].astype(F32) + others[:, 256:768].astype(F32)
    for k, ref in enumerate((o_own, o_lon, o_lat, o_cor)):
        rows = slice(SECTIONS[k], SECTIONS[k + 1])
        ref[0] = out[rows].astype(BF)
        ref[1] = hid[rows].astype(BF)


def spread_kernel(parts, copies, b_half):
    for j in range(16):
        for k in range(4):
            copies[k, j * 16 : (j + 1) * 16, :] = parts[j, 0:16, :]
        b_half[j] = parts[j, 16:32, :]


def gain_kernel(info, mine, w_qkv, out):
    rows = mine[...].astype(F32)
    w0, w1, w2 = [w_qkv[j].astype(F32) for j in range(3)]
    total = jnp.where(info[1] == 0, rows[:512] * w0 + rows[512:] * w1, rows[:512] * w2)
    ones = jnp.ones((8, 256), F32)
    out[...] = lax.dot_general(ones, total, NT, precision=lax.Precision.HIGHEST, preferred_element_type=F32)


def gain_sum_kernel(mine, other, gain, out):
    out[...] = (mine[0:1, :] + other[0:1, :]) / gain[...]


def bias_out_kernel(info, mine, other, grad_bias, token, low, high, flat):
    token[...] = jnp.zeros_like(token)
    first = jnp.where(info[1] == 0, mine[...], other[...]).astype(F32)
    second = jnp.where(info[1] == 0, other[...], mine[...]).astype(F32)
    for j, half in enumerate((first, second)):
        half = half.reshape(256, 256)
        low[256 * j : 256 * j + 256, :] = half[:, 0:128]
        high[256 * j : 256 * j + 256, :] = half[:, 128:256]
    for s_t in range(2):
        for j in range(12):
            at = (s_t * 12 + j) * 138
            rows = pl.ds(s_t * 16 + j, 16, stride=32)
            flat[:, at : at + 128] = low[rows, :]
            flat[:, at + 128 : at + 138] = high[rows, :][:, 0:10]
    grad_bias[...] = flat[...].reshape(grad_bias.shape)


def weights_kernel(info, mine, other, token, wqkv, wout, held, held_out, sems):
    token[...] = jnp.zeros_like(token)
    first = jnp.where(info[1] == 0, mine[...], other[...]).astype(F32)
    second = jnp.where(info[1] == 0, other[...], mine[...]).astype(F32)
    copies = []
    for k in range(6):
        rows = pl.ds(k % 2 * 256, 256)
        half = first if k < 4 else second
        held[k] = half[k % 4 * 256 : (k % 4 + 1) * 256]
        copies.append(pltpu.make_async_copy(held.at[k], wqkv.at[k // 2, rows], sems.at[k]))
        copies[-1].start()
    held_out[:, 0:256] = second[512:768]
    held_out[:, 256:512] = second[768:]
    for k in range(2):
        rows = pl.ds(k * 128, 128)
        copies.append(pltpu.make_async_copy(held_out.at[rows], wout.at[rows], sems.at[6 + k]))
        copies[-1].start()
    for copy in copies:
        copy.wait()


def bias_grad_kernel(info, ds, order, keep, send, part, entries, tables):
    entries[...] = jnp.zeros_like(entries)
    for p in range(12):
        for i in range(16):
            part[i * 12 : i * 12 + 12, :] = ds[i * WTOK + p * 12 : i * WTOK + p * 12 + 12, :]
        at = slice((11 - p) * 12, (11 - p) * 12 + WTOK)
        entries[:, at] = entries[:, at] + part[...]
    total = entries[...].astype(BF)
    tables[...] = jnp.zeros_like(tables)
    for s_u in range(2):
        rows = dot(total, order[s_u], NT)
        for i in range(16):
            for s_t in range(2):
                tables[i, s_t, s_u * 6 : s_u * 6 + 6, :] = rows[i * 12 + s_t * 6 : i * 12 + s_t * 6 + 6]
    mine, other = tables[0:8], tables[8:16]
    keep[...] = jnp.where(info[1] == 0, mine, other).astype(BF)
    send[...] = jnp.where(info[1] == 0, other, mine).astype(BF)


def final_kernel(latent, cot, gain, own, lon, lat, cor, output, grad, token):
    token[...] = jnp.zeros_like(token)
    for (by_lon, by_lat), ref in zip(PLACES, (own, lon, lat, cor)):
        out_term, hid_term = ref[0].astype(F32), ref[1].astype(F32)
        tile = latent[by_lon, by_lat]
        values = tile.reshape(out_term.shape).astype(F32)
        output[by_lon, by_lat] = (values + out_term).astype(BF).reshape(tile.shape)
        shifted = values - jnp.mean(values, -1, keepdims=True)
        inv_std = lax.rsqrt(jnp.mean(shifted * shifted, -1, keepdims=True) + 1e-05)
        normed = shifted * inv_std
        scaled = hid_term * gain[...]
        inner = scaled - jnp.mean(scaled, -1, keepdims=True) - normed * jnp.mean(scaled * normed, -1, keepdims=True)
        above = cot[by_lon, by_lat].reshape(out_term.shape).astype(F32)
        grad[by_lon, by_lat] = (above + inv_std * inner).astype(BF).reshape(tile.shape)


def moved(value, by_lon, by_lat):
    n_lon, n_lat = lax.axis_size("lon"), lax.axis_size("lat")
    pairs = [
        (i * n_lat + j, (i + by_lon) % n_lon * n_lat + (j + by_lat) % n_lat)
        for i in range(n_lon)
        for j in range(n_lat)
    ]
    return lax.ppermute(value, ("lon", "lat"), pairs)


def swapped(value, lon_bits, lat_bits):
    n_lon, n_lat = lax.axis_size("lon"), lax.axis_size("lat")
    pairs = [(i * n_lat + j, (i ^ lon_bits) * n_lat + (j ^ lat_bits)) for i in range(n_lon) for j in range(n_lat)]
    return lax.ppermute(value, ("lon", "lat"), pairs)


def across_y(value):
    n_lat = lax.axis_size("lat")
    groups = [list(range(x, n_lat, 2)) for x in range(2)]
    return lax.all_to_all(value, "lat", 0, 0, axis_index_groups=groups)


def across_zx(value):
    n_lon, n_lat = lax.axis_size("lon"), lax.axis_size("lat")
    groups = [
        [i * n_lat + j + x for i in range(core, n_lon, 2) for x in range(2)]
        for core in range(2)
        for j in range(0, n_lat, 2)
    ]
    return lax.all_to_all(value, ("lon", "lat"), 0, 0, axis_index_groups=groups)


def other_group(value):
    return lax.ppermute(value, "tp", [(0, 1), (1, 0)])


def on_device(latent, cotangent, ln_gain, w_qkv, w_out, bias_table):
    place, back = jnp.asarray(TO_WINDOW, BF), jnp.asarray(TO_WINDOW.T, BF)
    order = jnp.asarray(ORDER, BF)
    order_halves = jnp.asarray(ORDER.reshape(2, 138, 276), BF)
    i_lon, i_lat = lax.axis_index("lon"), lax.axis_index("lat")
    last = (i_lat == lax.axis_size("lat") - 1).astype(jnp.int32)
    core = i_lon % 2
    info = jnp.stack([last, core]).astype(jnp.int32)
    gain = ln_gain.reshape(1, 512)

    part = lambda n: ((2, n, 512), BF)
    halos = [part(216), part(72), part(72)]
    s_lon, s_lat, s_cor = call(
        halo_kernel,
        halos,
        [],
        [pltpu.VMEM((2,) + latent.shape, BF), pltpu.SemaphoreType.DMA((8,))],
        smem=0,
        hbm=[latent, cotangent],
    )
    in_lon, in_lat, in_cor = moved(s_lon, -1, 0), moved(s_lat, 0, -1), moved(s_cor, -1, -1)

    bias, w_copy = call(
        bias_kernel,
        [((16 * WTOK, WTOK), F32), (w_out.shape, BF)],
        [info, bias_table, order, w_out],
        [pltpu.VMEM((192, 276), F32)] * 2 + [pltpu.VMEM((192, 128), F32)] * 2,
        us=2,
    )
    w_other = other_group(w_copy)

    keep, send, ds, att, gq, gk, gv = call(
        main_kernel,
        [((1024, 256), F32), ((1024, 256), BF), ((16 * WTOK, WTOK), F32)] + [((576, 256), BF)] * 4,
        [info, latent, cotangent, in_lon, in_lat, in_cor, place, gain, w_qkv, w_out, bias],
        [pltpu.VMEM((576, 512), F32)],
        us=9,
        mib=32,
    )
    recv = swapped(send, 1, 0)
    (terms,) = call(terms_kernel, [((576, 768), BF)], [att, gq, gk, gv, w_qkv, back], smem=0, after=[w_other], us=2)
    others = other_group(terms)
    own, s_lon, s_lat, s_cor = call(
        pair_kernel,
        [part(216)] + halos,
        [terms, others],
        [pltpu.VMEM((2, 256, 512), BF), pltpu.SemaphoreType.DMA((4,))],
        smem=0,
        us=2,
        hbm=[w_out, w_other],
    )

    (total,) = call(core_sum_kernel, [((1024, 256), BF)], [keep, recv], smem=0, after=[terms], us=0.5)
    parts = across_y(total.reshape(4, 256, 256))
    b_keep, b_send = call(
        bias_grad_kernel,
        [((8, 2, 16, 138), BF)] * 2,
        [info, ds, order_halves],
        [pltpu.VMEM((192, WTOK), F32), pltpu.VMEM((192, 276), F32), pltpu.VMEM((16, 2, 16, 138), F32)],
        us=2.5,
    )
    b_recv = swapped(b_send, 1, 0)
    (message,) = call(y_sum_kernel, [((16, 32, 256), BF)], [parts, b_keep, b_recv], smem=0, us=1)
    r_lon, r_lat, r_cor = moved(s_lon, 1, 0), moved(s_lat, 0, 1), moved(s_cor, 1, 1)
    (copies,) = call(zx_sum_kernel, [((16, 32, 256), BF)], [across_zx(message)], smem=0, us=1)

    output, grad_latent, done = call(
        final_kernel,
        [(latent.shape, BF), (latent.shape, BF), TOKEN],
        [latent, cotangent, gain, own, r_lon, r_lat, r_cor],
        smem=0,
        us=30,
    )

    copies, b_half = call(
        spread_kernel,
        [((4, 256, 256), BF), ((16, 16, 256), BF)],
        [across_zx(copies)],
        smem=0,
        after=[done],
        us=1,
    )
    mine = across_y(copies).reshape(1024, 256)
    b_other = swapped(b_half, 1, 0)
    grad_bias, done = call(
        bias_out_kernel,
        [(bias_table.shape, F32), TOKEN],
        [info, b_half, b_other],
        [pltpu.VMEM((512, 128), F32)] * 2 + [pltpu.VMEM((16, 3312), F32)],
        us=30,
    )

    (g_mine,) = call(
        gain_kernel, [((8, 512), F32)], [info, mine, w_qkv], after=[done], us=1
    )
    g_other = swapped(g_mine, 1, 0)
    g_pair = g_mine + g_other
    done, grad_wqkv, grad_wout = call(
        weights_kernel,
        [TOKEN],
        [info, mine, swapped(mine, 1, 0)],
        [pltpu.VMEM((6, 256, 256), F32), pltpu.VMEM((256, 512), F32), pltpu.SemaphoreType.DMA((8,))],
        hbm_outs=[((3, 512, 256), F32), ((256, 512), F32)],
        us=2,
    )
    (grad_gain,) = call(
        gain_sum_kernel, [((1, 512), F32)], [g_pair, other_group(g_pair), gain], smem=0, after=[done]
    )
    grad_gain = grad_gain.reshape(512)
    return output, grad_latent, grad_gain, grad_wqkv, grad_wout, grad_bias


def solution(mesh):
    specs = (
        P("lon", "lat", None, None),
        P("lon", "lat", None, None),
        P(),
        P(None, None, "tp"),
        P("tp", None),
        P("lat", None, "tp", None),
    )
    return jax.shard_map(on_device, mesh=mesh, in_specs=specs, out_specs=specs, check_vma=False)
```

```python
import jax
import jax.numpy as jnp
import numpy as np
from jax import lax
from jax.experimental import pallas as pl
from jax.experimental.pallas import tpu as pltpu
from jax.sharding import PartitionSpec as P

BF = jnp.bfloat16
F32 = jnp.float32
WTOK = 144
OFFS = 23
NT = (((1,), (1,)), ((), ()))
TN = (((0,), (0,)), ((), ()))
SECTIONS = (0, 216, 432, 504, 576)


def section_row(lon, lat, lev):
    lat_cells = 9 if lat < 9 else 3
    return (lon >= 6) + 2 * (lat >= 9), (lon % 6 * lat_cells + lat % 9) * 4 + lev


def placement():
    place = np.zeros((576, 576), np.float32)
    for a in range(2):
        for b in range(2):
            for p in range(12):
                for s in range(2):
                    for r in range(6):
                        row = (a * 2 + b) * WTOK + p * 12 + s * 6 + r
                        section, at = section_row(p, a * 6 + r, (b * 2 + s + 1) % 4)
                        place[row, SECTIONS[section] + at] = 1
    return place


def offset_order():
    order = np.zeros((276, 276), np.float32)
    for rs in range(12):
        for k in range(OFFS):
            order[rs * OFFS + k, k * 12 + rs] = 1
    return order


TO_WINDOW = placement()
ORDER = offset_order()


def dot(a, b, dims=(((1,), (0,)), ((), ()))):
    return lax.dot_general(a, b, dims, preferred_element_type=F32)


def call(body, outs, args, scratch=(), smem=1, after=(), us=1, mib=16, hbm=(), hbm_outs=()):
    vmem, far = pl.BlockSpec(memory_space=pltpu.VMEM), pl.BlockSpec(memory_space=pltpu.HBM)
    n = len(args)
    m = n + len(hbm)

    def kernel(*refs):
        body(*refs[:m], *refs[m + len(after) :])

    return pl.pallas_call(
        kernel,
        out_shape=[jax.ShapeDtypeStruct(s, t) for s, t in [*outs, *hbm_outs]],
        in_specs=[pl.BlockSpec(memory_space=pltpu.SMEM)] * smem
        + [vmem] * (n - smem)
        + [far] * len(hbm)
        + [pl.BlockSpec(memory_space=pl.ANY)] * len(after),
        out_specs=[vmem] * len(outs) + [far] * len(hbm_outs),
        scratch_shapes=list(scratch),
        compiler_params=pltpu.CompilerParams(vmem_limit_bytes=mib * 1024 * 1024),
        cost_estimate=pl.CostEstimate(flops=int(us * 1e9), bytes_accessed=0, transcendentals=0),
    )(*args, *hbm, *after)


TOKEN = ((8, 128), F32)


LOW_LON, LOW_LAT, HIGH_LON, HIGH_LAT = slice(0, 6), slice(0, 3), slice(6, 12), slice(3, 12)
PLACES = ((HIGH_LON, HIGH_LAT), (LOW_LON, HIGH_LAT), (HIGH_LON, LOW_LAT), (LOW_LON, LOW_LAT))


def halo_kernel(latent, cot, *outs):
    for (lon, lat), ref in zip(PLACES[1:], outs):
        for j, grid in enumerate((latent, cot)):
            ref[j] = grid[lon, lat].reshape(ref.shape[1:])


def bias_kernel(info, table, order, w_out, bias, w_copy, raw, entries, low_u, high_u):
    w_copy[...] = w_out[...]
    flat = table[...].reshape(16, 3312)
    for s_t in range(2):
        for s_u in range(2):
            for r_t in range(6):
                at = ((s_t * 2 + s_u) * 6 + r_t) * 138
                row = (s_t * 6 + r_t) * 16
                raw[row : row + 16, s_u * 138 : s_u * 138 + 138] = flat[:, at : at + 138]
    full = raw[...]
    high = full.astype(BF)
    rest = full - high.astype(F32)
    mid = rest.astype(BF)
    low = (rest - mid.astype(F32)).astype(BF)
    entries[...] = dot(low, order[...]) + dot(mid, order[...]) + dot(high, order[...])
    row = lax.broadcasted_iota(jnp.int32, (192, WTOK), 0)
    col = lax.broadcasted_iota(jnp.int32, (192, WTOK), 1)
    rs_t, rs_u, which = row // 16, col % 12, row % 16
    s_t, s_u = (rs_t >= 6).astype(jnp.int32), (rs_u >= 6).astype(jnp.int32)
    edge_t = (rs_t - s_t * 6 >= 3).astype(jnp.int32)
    edge_u = (rs_u - s_u * 6 >= 3).astype(jnp.int32)
    last_lat = (which >= 8).astype(jnp.int32) * info[0]
    last_lev = ((which % 8) >= 4).astype(jnp.int32)
    barred = (last_lat * (edge_t - edge_u) != 0) | (last_lev * (s_t - s_u) != 0)
    for p in range(12):
        at = entries[:, (11 - p) * 12 : (11 - p) * 12 + WTOK]
        at = jnp.where(barred, -jnp.inf, at)
        low_u[...] = at[:, 0:128]
        high_u[:, 0:16] = at[:, 128:144]
        for i in range(16):
            rows = slice(i * WTOK + p * 12, i * WTOK + p * 12 + 12)
            bias[rows, 0:128] = low_u[pl.ds(i, 12, stride=16), :]
            bias[rows, 128:WTOK] = high_u[pl.ds(i, 12, stride=16), :][:, 0:16]


def main_kernel(info, latent, cotangent, lon, lat, cor, place, gain, w_qkv, w_out, bias,
                keep, send, o_ds, att_s, gq_s, gk_s, gv_s, joined):
    def gathered(which):
        own = (latent, cotangent)[which][HIGH_LON, HIGH_LAT].reshape(216, 512)
        for j, rows in enumerate((own, lon[which], lat[which], cor[which])):
            joined[SECTIONS[j] : SECTIONS[j + 1], :] = rows.astype(F32)
        return dot(place[...], joined[...].astype(BF))

    values = gathered(0)
    cot = gathered(1).astype(BF)
    shifted = values - jnp.mean(values, -1, keepdims=True)
    normed = shifted * lax.rsqrt(jnp.mean(shifted * shifted, -1, keepdims=True) + 1e-05)
    hidden = (normed * gain[...]).astype(BF)
    q, k, v = [dot(hidden, w_qkv[j]).astype(BF) for j in range(3)]
    down = dot(cot, w_out[...], NT).astype(BF)
    head = lax.broadcasted_iota(jnp.int32, (WTOK, 256), 1) // 64

    def stacked(rows):
        return jnp.concatenate([jnp.where(head == h, rows, jnp.zeros_like(rows)) for h in range(4)], 0)

    def unstacked(rows):
        total = jnp.zeros((WTOK, 256), F32)
        for h in range(4):
            total = jnp.where(head == h, rows[h * WTOK : (h + 1) * WTOK], total)
        return total

    for w in range(4):
        rows = slice(w * WTOK, (w + 1) * WTOK)
        four = slice(w * 576, (w + 1) * 576)
        qs, ds_ = stacked(q[rows]), stacked(down[rows])
        scores = dot(qs, k[rows], NT) * 0.125 + bias[four, :]
        exps = jnp.exp(scores - jnp.max(scores, -1, keepdims=True))
        probs = exps / jnp.sum(exps, -1, keepdims=True)
        probs_low = probs.astype(BF)
        att_s[rows, :] = unstacked(dot(probs_low, v[rows])).astype(BF)
        dp = dot(ds_, v[rows], NT)
        gv_s[rows, :] = dot(probs_low, ds_, TN).astype(BF)
        grad = probs * (dp - jnp.sum(dp * probs, -1, keepdims=True))
        o_ds[four, :] = grad
        grad_low = grad.astype(BF)
        gq_s[rows, :] = unstacked(dot(grad_low, k[rows]) * 0.125).astype(BF)
        gk_s[rows, :] = (dot(grad_low, qs, TN) * 0.125).astype(BF)

    att, gq, gk, gv = att_s[...], gq_s[...], gk_s[...], gv_s[...]
    wo = dot(att, cot, TN)
    first = [dot(hidden, gq, TN), dot(hidden, gk, TN)]
    second = [dot(hidden, gv, TN), jnp.concatenate([wo[:, :256], wo[:, 256:]], 0)]
    core = info[1]
    for j in range(2):
        rows = slice(j * 512, (j + 1) * 512)
        keep[rows, :] = jnp.where(core == 0, first[j], second[j])
        send[rows, :] = jnp.where(core == 0, second[j], first[j]).astype(BF)

def terms_kernel(att, gq, gk, gv, w_qkv, back, terms):
    hid_part = dot(gq[...], w_qkv[0], NT) + dot(gk[...], w_qkv[1], NT) + dot(gv[...], w_qkv[2], NT)
    terms[:, 0:256] = dot(back[...], att[...]).astype(BF)
    terms[:, 256:768] = dot(back[...], hid_part.astype(BF)).astype(BF)


def core_sum_kernel(keep, recv, total):
    total[...] = (keep[...] + recv[...].astype(F32)).astype(BF)


def y_sum_kernel(parts, b_keep, b_recv, message):
    total = parts[0].astype(F32)
    for j in range(1, 4):
        total = total + parts[j].astype(F32)
    total = total.astype(BF)
    tail = jnp.zeros((16, 118), BF)
    for z in range(8):
        for x in range(2):
            j = z * 2 + x
            message[j, 0:16, :] = total[j * 16 : (j + 1) * 16]
            both = (b_keep[z, x].astype(F32) + b_recv[z, x].astype(F32)).astype(BF)
            message[j, 16:32, :] = jnp.concatenate([both, tail], 1)


def zx_sum_kernel(parts, copies):
    total = jnp.zeros((16, 256), F32)
    biases = []
    for x in range(2):
        bias = jnp.zeros((16, 256), F32)
        for z in range(8):
            total = total + parts[z * 2 + x, 0:16, :].astype(F32)
            bias = bias + parts[z * 2 + x, 16:32, :].astype(F32)
        biases.append(bias.astype(BF))
    total = total.astype(BF)
    for z in range(8):
        for x in range(2):
            copies[z * 2 + x, 0:16, :] = total
            copies[z * 2 + x, 16:32, :] = biases[x]


def pair_kernel(terms, others, w_out, w_other, o_own, o_lon, o_lat, o_cor, token):
    token[...] = jnp.zeros_like(token)
    out = dot(terms[:, 0:256], w_out[...]).astype(BF).astype(F32)
    out = out + dot(others[:, 0:256], w_other[...]).astype(BF).astype(F32)
    hid = terms[:, 256:768].astype(F32) + others[:, 256:768].astype(F32)
    for k, ref in enumerate((o_own, o_lon, o_lat, o_cor)):
        rows = slice(SECTIONS[k], SECTIONS[k + 1])
        ref[0] = out[rows].astype(BF)
        ref[1] = hid[rows].astype(BF)


def spread_kernel(parts, copies, b_half):
    for j in range(16):
        for k in range(4):
            copies[k, j * 16 : (j + 1) * 16, :] = parts[j, 0:16, :]
        b_half[j] = parts[j, 16:32, :]


def gain_kernel(info, mine, w_qkv, out):
    rows = mine[...].astype(F32)
    w0, w1, w2 = [w_qkv[j].astype(F32) for j in range(3)]
    total = jnp.where(info[1] == 0, rows[:512] * w0 + rows[512:] * w1, rows[:512] * w2)
    ones = jnp.ones((8, 256), F32)
    out[...] = lax.dot_general(ones, total, NT, precision=lax.Precision.HIGHEST, preferred_element_type=F32)


def gain_sum_kernel(mine, other, gain, out):
    out[...] = (mine[0:1, :] + other[0:1, :]) / gain[...]


def bias_out_kernel(info, mine, other, grad_bias, token, low, high, flat):
    token[...] = jnp.zeros_like(token)
    first = jnp.where(info[1] == 0, mine[...], other[...]).astype(F32)
    second = jnp.where(info[1] == 0, other[...], mine[...]).astype(F32)
    for j, half in enumerate((first, second)):
        half = half.reshape(256, 256)
        low[256 * j : 256 * j + 256, :] = half[:, 0:128]
        high[256 * j : 256 * j + 256, :] = half[:, 128:256]
    for s_t in range(2):
        for j in range(12):
            at = (s_t * 12 + j) * 138
            rows = pl.ds(s_t * 16 + j, 16, stride=32)
            flat[:, at : at + 128] = low[rows, :]
            flat[:, at + 128 : at + 138] = high[rows, :][:, 0:10]
    grad_bias[...] = flat[...].reshape(grad_bias.shape)


def weights_kernel(info, mine, other, token, wqkv, wout, held, held_out, sems):
    token[...] = jnp.zeros_like(token)
    first = jnp.where(info[1] == 0, mine[...], other[...]).astype(F32)
    second = jnp.where(info[1] == 0, other[...], mine[...]).astype(F32)
    copies = []
    for k in range(6):
        rows = pl.ds(k % 2 * 256, 256)
        half = first if k < 4 else second
        held[k] = half[k % 4 * 256 : (k % 4 + 1) * 256]
        copies.append(pltpu.make_async_copy(held.at[k], wqkv.at[k // 2, rows], sems.at[k]))
        copies[-1].start()
    held_out[:, 0:256] = second[512:768]
    held_out[:, 256:512] = second[768:]
    for k in range(2):
        rows = pl.ds(k * 128, 128)
        copies.append(pltpu.make_async_copy(held_out.at[rows], wout.at[rows], sems.at[6 + k]))
        copies[-1].start()
    for copy in copies:
        copy.wait()


def bias_grad_kernel(info, ds, order, keep, send, part, entries, tables):
    entries[...] = jnp.zeros_like(entries)
    for p in range(12):
        for i in range(16):
            part[i * 12 : i * 12 + 12, :] = ds[i * WTOK + p * 12 : i * WTOK + p * 12 + 12, :]
        at = slice((11 - p) * 12, (11 - p) * 12 + WTOK)
        entries[:, at] = entries[:, at] + part[...]
    total = entries[...].astype(BF)
    tables[...] = jnp.zeros_like(tables)
    for s_u in range(2):
        rows = dot(total, order[s_u], NT)
        for i in range(16):
            for s_t in range(2):
                tables[i, s_t, s_u * 6 : s_u * 6 + 6, :] = rows[i * 12 + s_t * 6 : i * 12 + s_t * 6 + 6]
    mine, other = tables[0:8], tables[8:16]
    keep[...] = jnp.where(info[1] == 0, mine, other).astype(BF)
    send[...] = jnp.where(info[1] == 0, other, mine).astype(BF)


def final_kernel(latent, cot, gain, own, lon, lat, cor, output, grad, token):
    token[...] = jnp.zeros_like(token)
    for (by_lon, by_lat), ref in zip(PLACES, (own, lon, lat, cor)):
        out_term, hid_term = ref[0].astype(F32), ref[1].astype(F32)
        tile = latent[by_lon, by_lat]
        values = tile.reshape(out_term.shape).astype(F32)
        output[by_lon, by_lat] = (values + out_term).astype(BF).reshape(tile.shape)
        shifted = values - jnp.mean(values, -1, keepdims=True)
        inv_std = lax.rsqrt(jnp.mean(shifted * shifted, -1, keepdims=True) + 1e-05)
        normed = shifted * inv_std
        scaled = hid_term * gain[...]
        inner = scaled - jnp.mean(scaled, -1, keepdims=True) - normed * jnp.mean(scaled * normed, -1, keepdims=True)
        above = cot[by_lon, by_lat].reshape(out_term.shape).astype(F32)
        grad[by_lon, by_lat] = (above + inv_std * inner).astype(BF).reshape(tile.shape)


def moved(value, by_lon, by_lat):
    n_lon, n_lat = lax.axis_size("lon"), lax.axis_size("lat")
    pairs = [
        (i * n_lat + j, (i + by_lon) % n_lon * n_lat + (j + by_lat) % n_lat)
        for i in range(n_lon)
        for j in range(n_lat)
    ]
    return lax.ppermute(value, ("lon", "lat"), pairs)


def swapped(value, lon_bits, lat_bits):
    n_lon, n_lat = lax.axis_size("lon"), lax.axis_size("lat")
    pairs = [(i * n_lat + j, (i ^ lon_bits) * n_lat + (j ^ lat_bits)) for i in range(n_lon) for j in range(n_lat)]
    return lax.ppermute(value, ("lon", "lat"), pairs)


def across_y(value):
    n_lat = lax.axis_size("lat")
    groups = [list(range(x, n_lat, 2)) for x in range(2)]
    return lax.all_to_all(value, "lat", 0, 0, axis_index_groups=groups)


def across_zx(value):
    n_lon, n_lat = lax.axis_size("lon"), lax.axis_size("lat")
    groups = [
        [i * n_lat + j + x for i in range(core, n_lon, 2) for x in range(2)]
        for core in range(2)
        for j in range(0, n_lat, 2)
    ]
    return lax.all_to_all(value, ("lon", "lat"), 0, 0, axis_index_groups=groups)


def other_group(value):
    return lax.ppermute(value, "tp", [(0, 1), (1, 0)])


def on_device(latent, cotangent, ln_gain, w_qkv, w_out, bias_table):
    place, back = jnp.asarray(TO_WINDOW, BF), jnp.asarray(TO_WINDOW.T, BF)
    order = jnp.asarray(ORDER, BF)
    order_halves = jnp.asarray(ORDER.reshape(2, 138, 276), BF)
    i_lon, i_lat = lax.axis_index("lon"), lax.axis_index("lat")
    last = (i_lat == lax.axis_size("lat") - 1).astype(jnp.int32)
    core = i_lon % 2
    info = jnp.stack([last, core]).astype(jnp.int32)
    gain = ln_gain.reshape(1, 512)

    part = lambda n: ((2, n, 512), BF)
    halos = [part(216), part(72), part(72)]
    s_lon, s_lat, s_cor = call(halo_kernel, halos, [latent, cotangent], smem=0)
    in_lon, in_lat, in_cor = moved(s_lon, -1, 0), moved(s_lat, 0, -1), moved(s_cor, -1, -1)

    bias, w_copy = call(
        bias_kernel,
        [((16 * WTOK, WTOK), F32), (w_out.shape, BF)],
        [info, bias_table, order, w_out],
        [pltpu.VMEM((192, 276), F32)] * 2 + [pltpu.VMEM((192, 128), F32)] * 2,
        us=2,
    )
    w_other = other_group(w_copy)

    keep, send, ds, att, gq, gk, gv = call(
        main_kernel,
        [((1024, 256), F32), ((1024, 256), BF), ((16 * WTOK, WTOK), F32)] + [((576, 256), BF)] * 4,
        [info, latent, cotangent, in_lon, in_lat, in_cor, place, gain, w_qkv, w_out, bias],
        [pltpu.VMEM((576, 512), F32)],
        us=9,
        mib=32,
    )
    recv = swapped(send, 1, 0)
    (terms,) = call(terms_kernel, [((576, 768), BF)], [att, gq, gk, gv, w_qkv, back], smem=0, after=[w_other], us=2)
    others = other_group(terms)
    own, s_lon, s_lat, s_cor, paired = call(
        pair_kernel, [part(216)] + halos + [TOKEN], [terms, others, w_out, w_other], smem=0, us=30
    )

    (total,) = call(core_sum_kernel, [((1024, 256), BF)], [keep, recv], smem=0, after=[terms], us=0.5)
    parts = across_y(total.reshape(4, 256, 256))
    b_keep, b_send = call(
        bias_grad_kernel,
        [((8, 2, 16, 138), BF)] * 2,
        [info, ds, order_halves],
        [pltpu.VMEM((192, WTOK), F32), pltpu.VMEM((192, 276), F32), pltpu.VMEM((16, 2, 16, 138), F32)],
        us=2.5,
    )
    b_recv = swapped(b_send, 1, 0)
    (message,) = call(y_sum_kernel, [((16, 32, 256), BF)], [parts, b_keep, b_recv], smem=0, us=1)
    r_lon, r_lat, r_cor = moved(s_lon, 1, 0), moved(s_lat, 0, 1), moved(s_cor, 1, 1)
    (copies,) = call(zx_sum_kernel, [((16, 32, 256), BF)], [across_zx(message)], smem=0, after=[paired], us=1)

    output, grad_latent, placed = call(
        final_kernel,
        [(latent.shape, BF), (latent.shape, BF), TOKEN],
        [latent, cotangent, gain, own, r_lon, r_lat, r_cor],
        smem=0,
        us=30,
    )

    copies, b_half = call(
        spread_kernel,
        [((4, 256, 256), BF), ((16, 16, 256), BF)],
        [across_zx(copies)],
        smem=0,
        us=1,
    )
    mine = across_y(copies).reshape(1024, 256)
    b_other = swapped(b_half, 1, 0)
    grad_bias, done = call(
        bias_out_kernel,
        [(bias_table.shape, F32), TOKEN],
        [info, b_half, b_other],
        [pltpu.VMEM((512, 128), F32)] * 2 + [pltpu.VMEM((16, 3312), F32)],
        after=[placed],
    )

    (g_mine,) = call(
        gain_kernel, [((8, 512), F32)], [info, mine, w_qkv], after=[done], us=30
    )
    g_other = swapped(g_mine, 1, 0)
    g_pair = g_mine + g_other
    done, grad_wqkv, grad_wout = call(
        weights_kernel,
        [TOKEN],
        [info, mine, swapped(mine, 1, 0)],
        [pltpu.VMEM((6, 256, 256), F32), pltpu.VMEM((256, 512), F32), pltpu.SemaphoreType.DMA((8,))],
        hbm_outs=[((3, 512, 256), F32), ((256, 512), F32)],
        us=2,
    )
    (grad_gain,) = call(
        gain_sum_kernel, [((1, 512), F32)], [g_pair, other_group(g_pair), gain], smem=0, after=[done]
    )
    grad_gain = grad_gain.reshape(512)
    return output, grad_latent, grad_gain, grad_wqkv, grad_wout, grad_bias


def solution(mesh):
    specs = (
        P("lon", "lat", None, None),
        P("lon", "lat", None, None),
        P(),
        P(None, None, "tp"),
        P("tp", None),
        P("lat", None, "tp", None),
    )
    return jax.shard_map(on_device, mesh=mesh, in_specs=specs, out_specs=specs, check_vma=False)
```

```python
import jax
import jax.numpy as jnp
import numpy as np
from jax import lax
from jax.experimental import pallas as pl
from jax.experimental.pallas import tpu as pltpu
from jax.sharding import PartitionSpec as P

BF = jnp.bfloat16
F32 = jnp.float32
WTOK = 144
OFFS = 23
NT = (((1,), (1,)), ((), ()))
TN = (((0,), (0,)), ((), ()))
SECTIONS = (0, 216, 432, 504, 576)


def section_row(lon, lat, lev):
    lat_cells = 9 if lat < 9 else 3
    return (lon >= 6) + 2 * (lat >= 9), (lon % 6 * lat_cells + lat % 9) * 4 + lev


def placement():
    place = np.zeros((576, 576), np.float32)
    for a in range(2):
        for b in range(2):
            for p in range(12):
                for s in range(2):
                    for r in range(6):
                        row = (a * 2 + b) * WTOK + p * 12 + s * 6 + r
                        section, at = section_row(p, a * 6 + r, (b * 2 + s + 1) % 4)
                        place[row, SECTIONS[section] + at] = 1
    return place


def offset_order():
    order = np.zeros((276, 276), np.float32)
    for rs in range(12):
        for k in range(OFFS):
            order[rs * OFFS + k, k * 12 + rs] = 1
    return order


TO_WINDOW = placement()
ORDER = offset_order()


def dot(a, b, dims=(((1,), (0,)), ((), ()))):
    return lax.dot_general(a, b, dims, preferred_element_type=F32)


def call(body, outs, args, scratch=(), smem=1, after=(), us=1, mib=16, hbm=(), hbm_outs=()):
    vmem, far = pl.BlockSpec(memory_space=pltpu.VMEM), pl.BlockSpec(memory_space=pltpu.HBM)
    n = len(args)
    m = n + len(hbm)

    def kernel(*refs):
        body(*refs[:m], *refs[m + len(after) :])

    return pl.pallas_call(
        kernel,
        out_shape=[jax.ShapeDtypeStruct(s, t) for s, t in [*outs, *hbm_outs]],
        in_specs=[pl.BlockSpec(memory_space=pltpu.SMEM)] * smem
        + [vmem] * (n - smem)
        + [far] * len(hbm)
        + [pl.BlockSpec(memory_space=pl.ANY)] * len(after),
        out_specs=[vmem] * len(outs) + [far] * len(hbm_outs),
        scratch_shapes=list(scratch),
        compiler_params=pltpu.CompilerParams(vmem_limit_bytes=mib * 1024 * 1024),
        cost_estimate=pl.CostEstimate(flops=int(us * 1e9), bytes_accessed=0, transcendentals=0),
    )(*args, *hbm, *after)


TOKEN = ((8, 128), F32)


LOW_LON, LOW_LAT, HIGH_LON, HIGH_LAT = slice(0, 6), slice(0, 3), slice(6, 12), slice(3, 12)
PLACES = ((HIGH_LON, HIGH_LAT), (LOW_LON, HIGH_LAT), (HIGH_LON, LOW_LAT), (LOW_LON, LOW_LAT))


def halo_kernel(latent, cot, *outs):
    for (lon, lat), ref in zip(PLACES[1:], outs):
        for j, grid in enumerate((latent, cot)):
            ref[j] = grid[lon, lat].reshape(ref.shape[1:])


def bias_kernel(info, table, order, w_out, bias, w_copy, raw, entries, low_u, high_u):
    w_copy[...] = w_out[...]
    flat = table[...].reshape(16, 3312)
    for s_t in range(2):
        for s_u in range(2):
            for r_t in range(6):
                at = ((s_t * 2 + s_u) * 6 + r_t) * 138
                row = (s_t * 6 + r_t) * 16
                raw[row : row + 16, s_u * 138 : s_u * 138 + 138] = flat[:, at : at + 138]
    full = raw[...]
    high = full.astype(BF)
    rest = full - high.astype(F32)
    mid = rest.astype(BF)
    low = (rest - mid.astype(F32)).astype(BF)
    entries[...] = dot(low, order[...]) + dot(mid, order[...]) + dot(high, order[...])
    row = lax.broadcasted_iota(jnp.int32, (192, WTOK), 0)
    col = lax.broadcasted_iota(jnp.int32, (192, WTOK), 1)
    rs_t, rs_u, which = row // 16, col % 12, row % 16
    s_t, s_u = (rs_t >= 6).astype(jnp.int32), (rs_u >= 6).astype(jnp.int32)
    edge_t = (rs_t - s_t * 6 >= 3).astype(jnp.int32)
    edge_u = (rs_u - s_u * 6 >= 3).astype(jnp.int32)
    last_lat = (which >= 8).astype(jnp.int32) * info[0]
    last_lev = ((which % 8) >= 4).astype(jnp.int32)
    barred = (last_lat * (edge_t - edge_u) != 0) | (last_lev * (s_t - s_u) != 0)
    for p in range(12):
        at = entries[:, (11 - p) * 12 : (11 - p) * 12 + WTOK]
        at = jnp.where(barred, -jnp.inf, at)
        low_u[...] = at[:, 0:128]
        high_u[:, 0:16] = at[:, 128:144]
        for i in range(16):
            rows = slice(i * WTOK + p * 12, i * WTOK + p * 12 + 12)
            bias[rows, 0:128] = low_u[pl.ds(i, 12, stride=16), :]
            bias[rows, 128:WTOK] = high_u[pl.ds(i, 12, stride=16), :][:, 0:16]


def main_kernel(info, latent, cotangent, lon, lat, cor, place, gain, w_qkv, w_out, bias,
                keep, send, o_ds, att_s, gq_s, gk_s, gv_s, joined):
    def gathered(which):
        own = (latent, cotangent)[which][HIGH_LON, HIGH_LAT].reshape(216, 512)
        for j, rows in enumerate((own, lon[which], lat[which], cor[which])):
            joined[SECTIONS[j] : SECTIONS[j + 1], :] = rows.astype(F32)
        return dot(place[...], joined[...].astype(BF))

    values = gathered(0)
    cot = gathered(1).astype(BF)
    shifted = values - jnp.mean(values, -1, keepdims=True)
    normed = shifted * lax.rsqrt(jnp.mean(shifted * shifted, -1, keepdims=True) + 1e-05)
    hidden = (normed * gain[...]).astype(BF)
    q, k, v = [dot(hidden, w_qkv[j]).astype(BF) for j in range(3)]
    down = dot(cot, w_out[...], NT).astype(BF)
    head = lax.broadcasted_iota(jnp.int32, (WTOK, 256), 1) // 64

    def stacked(rows):
        return jnp.concatenate([jnp.where(head == h, rows, jnp.zeros_like(rows)) for h in range(4)], 0)

    def unstacked(rows):
        total = jnp.zeros((WTOK, 256), F32)
        for h in range(4):
            total = jnp.where(head == h, rows[h * WTOK : (h + 1) * WTOK], total)
        return total

    for w in range(4):
        rows = slice(w * WTOK, (w + 1) * WTOK)
        four = slice(w * 576, (w + 1) * 576)
        qs, ds_ = stacked(q[rows]), stacked(down[rows])
        scores = dot(qs, k[rows], NT) * 0.125 + bias[four, :]
        exps = jnp.exp(scores - jnp.max(scores, -1, keepdims=True))
        probs = exps / jnp.sum(exps, -1, keepdims=True)
        probs_low = probs.astype(BF)
        att_s[rows, :] = unstacked(dot(probs_low, v[rows])).astype(BF)
        dp = dot(ds_, v[rows], NT)
        gv_s[rows, :] = dot(probs_low, ds_, TN).astype(BF)
        grad = probs * (dp - jnp.sum(dp * probs, -1, keepdims=True))
        o_ds[four, :] = grad
        grad_low = grad.astype(BF)
        gq_s[rows, :] = unstacked(dot(grad_low, k[rows]) * 0.125).astype(BF)
        gk_s[rows, :] = (dot(grad_low, qs, TN) * 0.125).astype(BF)

    att, gq, gk, gv = att_s[...], gq_s[...], gk_s[...], gv_s[...]
    wo = dot(att, cot, TN)
    first = [dot(hidden, gq, TN), dot(hidden, gk, TN)]
    second = [dot(hidden, gv, TN), jnp.concatenate([wo[:, :256], wo[:, 256:]], 0)]
    core = info[1]
    for j in range(2):
        rows = slice(j * 512, (j + 1) * 512)
        keep[rows, :] = jnp.where(core == 0, first[j], second[j])
        send[rows, :] = jnp.where(core == 0, second[j], first[j]).astype(BF)

def terms_kernel(att, gq, gk, gv, w_qkv, back, terms):
    hid_part = dot(gq[...], w_qkv[0], NT) + dot(gk[...], w_qkv[1], NT) + dot(gv[...], w_qkv[2], NT)
    terms[:, 0:256] = dot(back[...], att[...]).astype(BF)
    terms[:, 256:768] = dot(back[...], hid_part.astype(BF)).astype(BF)


def core_sum_kernel(keep, recv, total):
    total[...] = (keep[...] + recv[...].astype(F32)).astype(BF)


def y_sum_kernel(parts, b_keep, b_recv, message):
    total = parts[0].astype(F32)
    for j in range(1, 4):
        total = total + parts[j].astype(F32)
    total = total.astype(BF)
    both = (b_keep[...].astype(F32) + b_recv[...].astype(F32)).astype(BF)
    for j in range(16):
        rows = slice(j * 16, (j + 1) * 16)
        message[j, :, 0:256] = total[rows]
        message[j, :, 256:384] = both[rows]


def zx_sum_kernel(parts, copies):
    total = jnp.zeros((16, 256), F32)
    biases = []
    for x in range(2):
        bias = jnp.zeros((16, 128), F32)
        for z in range(8):
            total = total + parts[z * 2 + x, :, 0:256].astype(F32)
            bias = bias + parts[z * 2 + x, :, 256:384].astype(F32)
        biases.append(bias.astype(BF))
    total = total.astype(BF)
    for z in range(8):
        for x in range(2):
            copies[z * 2 + x, :, 0:256] = total
            copies[z * 2 + x, :, 256:384] = biases[x]


def pair_kernel(terms, others, w_out, w_other, o_own, o_lon, o_lat, o_cor, token):
    token[...] = jnp.zeros_like(token)
    out = dot(terms[:, 0:256], w_out[...]).astype(BF).astype(F32)
    out = out + dot(others[:, 0:256], w_other[...]).astype(BF).astype(F32)
    hid = terms[:, 256:768].astype(F32) + others[:, 256:768].astype(F32)
    for k, ref in enumerate((o_own, o_lon, o_lat, o_cor)):
        rows = slice(SECTIONS[k], SECTIONS[k + 1])
        ref[0] = out[rows].astype(BF)
        ref[1] = hid[rows].astype(BF)


def spread_kernel(parts, copies, b_half):
    for j in range(16):
        rows = slice(j * 16, (j + 1) * 16)
        for k in range(4):
            copies[k, rows, :] = parts[j, :, 0:256]
        b_half[rows, :] = parts[j, :, 256:384]


def gain_kernel(info, mine, w_qkv, out):
    rows = mine[...].astype(F32)
    w0, w1, w2 = [w_qkv[j].astype(F32) for j in range(3)]
    total = jnp.where(info[1] == 0, rows[:512] * w0 + rows[512:] * w1, rows[:512] * w2)
    ones = jnp.ones((8, 256), F32)
    out[...] = lax.dot_general(ones, total, NT, precision=lax.Precision.HIGHEST, preferred_element_type=F32)


def gain_sum_kernel(mine, other, gain, out):
    out[...] = (mine[0:1, :] + other[0:1, :]) / gain[...]


def bias_out_kernel(info, mine, other, grad_bias, token, rows, flat):
    token[...] = jnp.zeros_like(token)
    rows[0:256, :] = jnp.where(info[1] == 0, mine[...], other[...]).astype(F32)
    rows[256:512, :] = jnp.where(info[1] == 0, other[...], mine[...]).astype(F32)
    for s_t in range(2):
        for j in range(12):
            at = (s_t * 12 + j) * 138
            flat[:, at : at + 115] = rows[pl.ds(s_t * 16 + j, 16, stride=32), :][:, 0:115]
            last = rows[pl.ds(s_t * 16 + 12 + j // 3, 16, stride=32), :]
            flat[:, at + 115 : at + 138] = last[:, j % 3 * 23 : j % 3 * 23 + 23]
    grad_bias[...] = flat[...].reshape(grad_bias.shape)


def weights_kernel(info, mine, other, token, wqkv, wout, held, held_out, sems):
    token[...] = jnp.zeros_like(token)
    first = jnp.where(info[1] == 0, mine[...], other[...]).astype(F32)
    second = jnp.where(info[1] == 0, other[...], mine[...]).astype(F32)
    copies = []
    for k in range(6):
        rows = pl.ds(k % 2 * 256, 256)
        half = first if k < 4 else second
        held[k] = half[k % 4 * 256 : (k % 4 + 1) * 256]
        copies.append(pltpu.make_async_copy(held.at[k], wqkv.at[k // 2, rows], sems.at[k]))
        copies[-1].start()
    held_out[:, 0:256] = second[512:768]
    held_out[:, 256:512] = second[768:]
    for k in range(2):
        rows = pl.ds(k * 128, 128)
        copies.append(pltpu.make_async_copy(held_out.at[rows], wout.at[rows], sems.at[6 + k]))
        copies[-1].start()
    for copy in copies:
        copy.wait()


def bias_grad_kernel(info, ds, order, keep, send, part, entries, packed, *ends):
    entries[...] = jnp.zeros_like(entries)
    for p in range(12):
        for i in range(16):
            part[i * 12 : i * 12 + 12, :] = ds[i * WTOK + p * 12 : i * WTOK + p * 12 + 12, :]
        at = slice((11 - p) * 12, (11 - p) * 12 + WTOK)
        entries[:, at] = entries[:, at] + part[...]
    total = entries[...].astype(BF)
    packed[...] = jnp.zeros_like(packed)
    for s_u in range(2):
        rows = dot(total, order[s_u], NT)
        for half in range(32):
            at = half * 16 + s_u * 6
            packed[at : at + 6, 0:115] = rows[half * 6 : half * 6 + 6, 0:115]
        for q in range(3):
            last = ends[s_u * 3 + q]
            last[...] = jnp.zeros_like(last)
            last[:, q * 23 : q * 23 + 23] = rows[:, 115:138]
    for k in range(4):
        row = jnp.zeros((32, 128), F32)
        for q in range(3):
            s_u, r_t = (k * 3 + q) // 6, (k * 3 + q) % 6
            row = row + ends[s_u * 3 + q][pl.ds(r_t, 32, stride=6), :]
        packed[pl.ds(12 + k, 32, stride=16), :] = row
    mine, other = packed[0:256, :], packed[256:512, :]
    keep[...] = jnp.where(info[1] == 0, mine, other).astype(BF)
    send[...] = jnp.where(info[1] == 0, other, mine).astype(BF)


def final_kernel(latent, cot, gain, own, lon, lat, cor, output, grad, token):
    token[...] = jnp.zeros_like(token)
    for (by_lon, by_lat), ref in zip(PLACES, (own, lon, lat, cor)):
        out_term, hid_term = ref[0].astype(F32), ref[1].astype(F32)
        tile = latent[by_lon, by_lat]
        values = tile.reshape(out_term.shape).astype(F32)
        output[by_lon, by_lat] = (values + out_term).astype(BF).reshape(tile.shape)
        shifted = values - jnp.mean(values, -1, keepdims=True)
        inv_std = lax.rsqrt(jnp.mean(shifted * shifted, -1, keepdims=True) + 1e-05)
        normed = shifted * inv_std
        scaled = hid_term * gain[...]
        inner = scaled - jnp.mean(scaled, -1, keepdims=True) - normed * jnp.mean(scaled * normed, -1, keepdims=True)
        above = cot[by_lon, by_lat].reshape(out_term.shape).astype(F32)
        grad[by_lon, by_lat] = (above + inv_std * inner).astype(BF).reshape(tile.shape)


def moved(value, by_lon, by_lat):
    n_lon, n_lat = lax.axis_size("lon"), lax.axis_size("lat")
    pairs = [
        (i * n_lat + j, (i + by_lon) % n_lon * n_lat + (j + by_lat) % n_lat)
        for i in range(n_lon)
        for j in range(n_lat)
    ]
    return lax.ppermute(value, ("lon", "lat"), pairs)


def swapped(value, lon_bits, lat_bits):
    n_lon, n_lat = lax.axis_size("lon"), lax.axis_size("lat")
    pairs = [(i * n_lat + j, (i ^ lon_bits) * n_lat + (j ^ lat_bits)) for i in range(n_lon) for j in range(n_lat)]
    return lax.ppermute(value, ("lon", "lat"), pairs)


def across_y(value):
    n_lat = lax.axis_size("lat")
    groups = [list(range(x, n_lat, 2)) for x in range(2)]
    return lax.all_to_all(value, "lat", 0, 0, axis_index_groups=groups)


def across_zx(value):
    n_lon, n_lat = lax.axis_size("lon"), lax.axis_size("lat")
    groups = [
        [i * n_lat + j + x for i in range(core, n_lon, 2) for x in range(2)]
        for core in range(2)
        for j in range(0, n_lat, 2)
    ]
    return lax.all_to_all(value, ("lon", "lat"), 0, 0, axis_index_groups=groups)


def other_group(value):
    return lax.ppermute(value, "tp", [(0, 1), (1, 0)])


def on_device(latent, cotangent, ln_gain, w_qkv, w_out, bias_table):
    place, back = jnp.asarray(TO_WINDOW, BF), jnp.asarray(TO_WINDOW.T, BF)
    order = jnp.asarray(ORDER, BF)
    order_halves = jnp.asarray(ORDER.reshape(2, 138, 276), BF)
    i_lon, i_lat = lax.axis_index("lon"), lax.axis_index("lat")
    last = (i_lat == lax.axis_size("lat") - 1).astype(jnp.int32)
    core = i_lon % 2
    info = jnp.stack([last, core]).astype(jnp.int32)
    gain = ln_gain.reshape(1, 512)

    part = lambda n: ((2, n, 512), BF)
    halos = [part(216), part(72), part(72)]
    s_lon, s_lat, s_cor = call(halo_kernel, halos, [latent, cotangent], smem=0)
    in_lon, in_lat, in_cor = moved(s_lon, -1, 0), moved(s_lat, 0, -1), moved(s_cor, -1, -1)

    bias, w_copy = call(
        bias_kernel,
        [((16 * WTOK, WTOK), F32), (w_out.shape, BF)],
        [info, bias_table, order, w_out],
        [pltpu.VMEM((192, 276), F32)] * 2 + [pltpu.VMEM((192, 128), F32)] * 2,
        us=2,
    )
    w_other = other_group(w_copy)

    keep, send, ds, att, gq, gk, gv = call(
        main_kernel,
        [((1024, 256), F32), ((1024, 256), BF), ((16 * WTOK, WTOK), F32)] + [((576, 256), BF)] * 4,
        [info, latent, cotangent, in_lon, in_lat, in_cor, place, gain, w_qkv, w_out, bias],
        [pltpu.VMEM((576, 512), F32)],
        us=9,
        mib=32,
    )
    recv = swapped(send, 1, 0)
    (terms,) = call(terms_kernel, [((576, 768), BF)], [att, gq, gk, gv, w_qkv, back], smem=0, after=[w_other], us=2)
    others = other_group(terms)
    own, s_lon, s_lat, s_cor, paired = call(
        pair_kernel, [part(216)] + halos + [TOKEN], [terms, others, w_out, w_other], smem=0, us=30
    )

    (total,) = call(core_sum_kernel, [((1024, 256), BF)], [keep, recv], smem=0, after=[terms], us=0.5)
    parts = across_y(total.reshape(4, 256, 256))
    b_keep, b_send = call(
        bias_grad_kernel,
        [((256, 128), BF)] * 2,
        [info, ds, order_halves],
        [pltpu.VMEM((192, WTOK), F32), pltpu.VMEM((192, 276), F32), pltpu.VMEM((512, 128), F32)]
        + [pltpu.VMEM((192, 128), F32)] * 6,
        us=2.5,
    )
    b_recv = swapped(b_send, 1, 0)
    (message,) = call(y_sum_kernel, [((16, 16, 384), BF)], [parts, b_keep, b_recv], smem=0, us=1)
    r_lon, r_lat, r_cor = moved(s_lon, 1, 0), moved(s_lat, 0, 1), moved(s_cor, 1, 1)
    (copies,) = call(zx_sum_kernel, [((16, 16, 384), BF)], [across_zx(message)], smem=0, after=[paired], us=1)

    output, grad_latent, placed = call(
        final_kernel,
        [(latent.shape, BF), (latent.shape, BF), TOKEN],
        [latent, cotangent, gain, own, r_lon, r_lat, r_cor],
        smem=0,
        us=30,
    )

    copies, b_half = call(
        spread_kernel,
        [((4, 256, 256), BF), ((256, 128), BF)],
        [across_zx(copies)],
        smem=0,
        us=1,
    )
    mine = across_y(copies).reshape(1024, 256)
    b_other = swapped(b_half, 1, 0)
    grad_bias, done = call(
        bias_out_kernel,
        [(bias_table.shape, F32), TOKEN],
        [info, b_half, b_other],
        [pltpu.VMEM((512, 128), F32), pltpu.VMEM((16, 3312), F32)],
        after=[placed],
    )

    (g_mine,) = call(
        gain_kernel, [((8, 512), F32)], [info, mine, w_qkv], after=[done], us=30
    )
    g_other = swapped(g_mine, 1, 0)
    g_pair = g_mine + g_other
    done, grad_wqkv, grad_wout = call(
        weights_kernel,
        [TOKEN],
        [info, mine, swapped(mine, 1, 0)],
        [pltpu.VMEM((6, 256, 256), F32), pltpu.VMEM((256, 512), F32), pltpu.SemaphoreType.DMA((8,))],
        hbm_outs=[((3, 512, 256), F32), ((256, 512), F32)],
        us=2,
    )
    (grad_gain,) = call(
        gain_sum_kernel, [((1, 512), F32)], [g_pair, other_group(g_pair), gain], smem=0, after=[done]
    )
    grad_gain = grad_gain.reshape(512)
    return output, grad_latent, grad_gain, grad_wqkv, grad_wout, grad_bias


def solution(mesh):
    specs = (
        P("lon", "lat", None, None),
        P("lon", "lat", None, None),
        P(),
        P(None, None, "tp"),
        P("tp", None),
        P("lat", None, "tp", None),
    )
    return jax.shard_map(on_device, mesh=mesh, in_specs=specs, out_specs=specs, check_vma=False)
```

```python
import jax
import jax.numpy as jnp
import numpy as np
from jax import lax
from jax.experimental import pallas as pl
from jax.experimental.pallas import tpu as pltpu
from jax.sharding import PartitionSpec as P

BF = jnp.bfloat16
F32 = jnp.float32
WTOK = 144
OFFS = 23
NT = (((1,), (1,)), ((), ()))
TN = (((0,), (0,)), ((), ()))
SECTIONS = (0, 216, 432, 504, 576)


def section_row(lon, lat, lev):
    lat_cells = 9 if lat < 9 else 3
    return (lon >= 6) + 2 * (lat >= 9), (lon % 6 * lat_cells + lat % 9) * 4 + lev


def placement():
    place = np.zeros((576, 576), np.float32)
    for a in range(2):
        for b in range(2):
            for p in range(12):
                for s in range(2):
                    for r in range(6):
                        row = (a * 2 + b) * WTOK + p * 12 + s * 6 + r
                        section, at = section_row(p, a * 6 + r, (b * 2 + s + 1) % 4)
                        place[row, SECTIONS[section] + at] = 1
    return place


def offset_order():
    order = np.zeros((276, 276), np.float32)
    for rs in range(12):
        for k in range(OFFS):
            order[rs * OFFS + k, k * 12 + rs] = 1
    return order


TO_WINDOW = placement()
ORDER = offset_order()


def dot(a, b, dims=(((1,), (0,)), ((), ()))):
    return lax.dot_general(a, b, dims, preferred_element_type=F32)


def call(body, outs, args, scratch=(), smem=1, after=(), us=1, mib=16, hbm=(), hbm_outs=()):
    vmem, far = pl.BlockSpec(memory_space=pltpu.VMEM), pl.BlockSpec(memory_space=pltpu.HBM)
    n = len(args)
    m = n + len(hbm)

    def kernel(*refs):
        body(*refs[:m], *refs[m + len(after) :])

    return pl.pallas_call(
        kernel,
        out_shape=[jax.ShapeDtypeStruct(s, t) for s, t in [*outs, *hbm_outs]],
        in_specs=[pl.BlockSpec(memory_space=pltpu.SMEM)] * smem
        + [vmem] * (n - smem)
        + [far] * len(hbm)
        + [pl.BlockSpec(memory_space=pl.ANY)] * len(after),
        out_specs=[vmem] * len(outs) + [far] * len(hbm_outs),
        scratch_shapes=list(scratch),
        compiler_params=pltpu.CompilerParams(vmem_limit_bytes=mib * 1024 * 1024),
        cost_estimate=pl.CostEstimate(flops=int(us * 1e9), bytes_accessed=0, transcendentals=0),
    )(*args, *hbm, *after)


TOKEN = ((8, 128), F32)


LOW_LON, LOW_LAT, HIGH_LON, HIGH_LAT = slice(0, 6), slice(0, 3), slice(6, 12), slice(3, 12)
PLACES = ((HIGH_LON, HIGH_LAT), (LOW_LON, HIGH_LAT), (HIGH_LON, LOW_LAT), (LOW_LON, LOW_LAT))


def halo_kernel(latent, cot, *outs):
    for (lon, lat), ref in zip(PLACES[1:], outs):
        for j, grid in enumerate((latent, cot)):
            ref[j] = grid[lon, lat].reshape(ref.shape[1:])


def bias_kernel(info, table, order, bias, raw, entries, low_u, high_u):
    flat = table[...].reshape(16, 3312)
    for s_t in range(2):
        for s_u in range(2):
            for r_t in range(6):
                at = ((s_t * 2 + s_u) * 6 + r_t) * 138
                row = (s_t * 6 + r_t) * 16
                raw[row : row + 16, s_u * 138 : s_u * 138 + 138] = flat[:, at : at + 138]
    full = raw[...]
    high = full.astype(BF)
    rest = full - high.astype(F32)
    mid = rest.astype(BF)
    low = (rest - mid.astype(F32)).astype(BF)
    entries[...] = dot(low, order[...]) + dot(mid, order[...]) + dot(high, order[...])
    row = lax.broadcasted_iota(jnp.int32, (192, WTOK), 0)
    col = lax.broadcasted_iota(jnp.int32, (192, WTOK), 1)
    rs_t, rs_u, which = row // 16, col % 12, row % 16
    s_t, s_u = (rs_t >= 6).astype(jnp.int32), (rs_u >= 6).astype(jnp.int32)
    edge_t = (rs_t - s_t * 6 >= 3).astype(jnp.int32)
    edge_u = (rs_u - s_u * 6 >= 3).astype(jnp.int32)
    last_lat = (which >= 8).astype(jnp.int32) * info[0]
    last_lev = ((which % 8) >= 4).astype(jnp.int32)
    barred = (last_lat * (edge_t - edge_u) != 0) | (last_lev * (s_t - s_u) != 0)
    for p in range(12):
        at = entries[:, (11 - p) * 12 : (11 - p) * 12 + WTOK]
        at = jnp.where(barred, -jnp.inf, at)
        low_u[...] = at[:, 0:128]
        high_u[:, 0:16] = at[:, 128:144]
        for i in range(16):
            rows = slice(i * WTOK + p * 12, i * WTOK + p * 12 + 12)
            bias[rows, 0:128] = low_u[pl.ds(i, 12, stride=16), :]
            bias[rows, 128:WTOK] = high_u[pl.ds(i, 12, stride=16), :][:, 0:16]


def main_kernel(info, latent, cotangent, lon, lat, cor, place, gain, w_qkv, w_out, bias,
                keep, send, o_ds, att_s, gq_s, gk_s, gv_s, joined):
    def gathered(which):
        own = (latent, cotangent)[which][HIGH_LON, HIGH_LAT].reshape(216, 512)
        for j, rows in enumerate((own, lon[which], lat[which], cor[which])):
            joined[SECTIONS[j] : SECTIONS[j + 1], :] = rows.astype(F32)
        return dot(place[...], joined[...].astype(BF))

    values = gathered(0)
    cot = gathered(1).astype(BF)
    shifted = values - jnp.mean(values, -1, keepdims=True)
    normed = shifted * lax.rsqrt(jnp.mean(shifted * shifted, -1, keepdims=True) + 1e-05)
    hidden = (normed * gain[...]).astype(BF)
    q, k, v = [dot(hidden, w_qkv[j]).astype(BF) for j in range(3)]
    down = dot(cot, w_out[...], NT).astype(BF)
    head = lax.broadcasted_iota(jnp.int32, (WTOK, 256), 1) // 64

    def stacked(rows):
        return jnp.concatenate([jnp.where(head == h, rows, jnp.zeros_like(rows)) for h in range(4)], 0)

    def unstacked(rows):
        total = jnp.zeros((WTOK, 256), F32)
        for h in range(4):
            total = jnp.where(head == h, rows[h * WTOK : (h + 1) * WTOK], total)
        return total

    for w in range(4):
        rows = slice(w * WTOK, (w + 1) * WTOK)
        four = slice(w * 576, (w + 1) * 576)
        qs, ds_ = stacked(q[rows]), stacked(down[rows])
        scores = dot(qs, k[rows], NT) * 0.125 + bias[four, :]
        exps = jnp.exp(scores - jnp.max(scores, -1, keepdims=True))
        probs = exps / jnp.sum(exps, -1, keepdims=True)
        probs_low = probs.astype(BF)
        att_s[rows, :] = unstacked(dot(probs_low, v[rows])).astype(BF)
        dp = dot(ds_, v[rows], NT)
        gv_s[rows, :] = dot(probs_low, ds_, TN).astype(BF)
        grad = probs * (dp - jnp.sum(dp * probs, -1, keepdims=True))
        o_ds[four, :] = grad
        grad_low = grad.astype(BF)
        gq_s[rows, :] = unstacked(dot(grad_low, k[rows]) * 0.125).astype(BF)
        gk_s[rows, :] = (dot(grad_low, qs, TN) * 0.125).astype(BF)

    att, gq, gk, gv = att_s[...], gq_s[...], gk_s[...], gv_s[...]
    wo = dot(att, cot, TN)
    first = [dot(hidden, gq, TN), dot(hidden, gk, TN)]
    second = [dot(hidden, gv, TN), jnp.concatenate([wo[:, :256], wo[:, 256:]], 0)]
    core = info[1]
    for j in range(2):
        rows = slice(j * 512, (j + 1) * 512)
        keep[rows, :] = jnp.where(core == 0, first[j], second[j])
        send[rows, :] = jnp.where(core == 0, second[j], first[j]).astype(BF)

def terms_kernel(att, gq, gk, gv, w_qkv, back, terms):
    hid_part = dot(gq[...], w_qkv[0], NT) + dot(gk[...], w_qkv[1], NT) + dot(gv[...], w_qkv[2], NT)
    terms[:, 0:256] = dot(back[...], att[...]).astype(BF)
    terms[:, 256:768] = dot(back[...], hid_part.astype(BF)).astype(BF)


def core_sum_kernel(keep, recv, total):
    total[...] = (keep[...] + recv[...].astype(F32)).astype(BF)


def y_sum_kernel(parts, b_keep, b_recv, message):
    total = parts[0].astype(F32)
    for j in range(1, 4):
        total = total + parts[j].astype(F32)
    total = total.astype(BF)
    both = (b_keep[...].astype(F32) + b_recv[...].astype(F32)).astype(BF)
    for j in range(8):
        rows = slice(j * 32, (j + 1) * 32)
        message[j, :, 0:256] = total[rows]
        message[j, :, 256:384] = both[rows]


def z_sum_kernel(parts, mine, bias):
    total = parts[0].astype(F32)
    for j in range(1, 8):
        total = total + parts[j].astype(F32)
    mine[...] = total[:, 0:256].astype(BF)
    bias[...] = total[:, 256:384].astype(BF)


def x_sum_kernel(mine, recv, bias, copies):
    total = (mine[...].astype(F32) + recv[...].astype(F32)).astype(BF)
    for j in range(8):
        copies[j, :, 0:256] = total
        copies[j, :, 256:384] = bias[...]


def pair_kernel(terms, others, w_out, w_other, o_own, o_lon, o_lat, o_cor, token):
    token[...] = jnp.zeros_like(token)
    out = dot(terms[:, 0:256], w_out[...]).astype(BF).astype(F32)
    out = out + dot(others[:, 0:256], w_other[...]).astype(BF).astype(F32)
    hid = terms[:, 256:768].astype(F32) + others[:, 256:768].astype(F32)
    for k, ref in enumerate((o_own, o_lon, o_lat, o_cor)):
        rows = slice(SECTIONS[k], SECTIONS[k + 1])
        ref[0] = out[rows].astype(BF)
        ref[1] = hid[rows].astype(BF)


def spread_kernel(parts, copies, b_half):
    for j in range(8):
        rows = slice(j * 32, (j + 1) * 32)
        for k in range(4):
            copies[k, rows, :] = parts[j, :, 0:256]
        b_half[rows, :] = parts[j, :, 256:384]


def gain_kernel(info, mine, w_qkv, out):
    rows = mine[...].astype(F32)
    w0, w1, w2 = [w_qkv[j].astype(F32) for j in range(3)]
    total = jnp.where(info[1] == 0, rows[:512] * w0 + rows[512:] * w1, rows[:512] * w2)
    ones = jnp.ones((8, 256), F32)
    out[...] = lax.dot_general(ones, total, NT, precision=lax.Precision.HIGHEST, preferred_element_type=F32)


def gain_sum_kernel(mine, other, mine_tp, other_tp, gain, out):
    total = (mine[0:1, :] + other[0:1, :]) + (mine_tp[0:1, :] + other_tp[0:1, :])
    out[...] = total / gain[...]


def bias_out_kernel(info, mine, other, grad_bias, token, rows, flat):
    token[...] = jnp.zeros_like(token)
    rows[0:256, :] = jnp.where(info[1] == 0, mine[...], other[...]).astype(F32)
    rows[256:512, :] = jnp.where(info[1] == 0, other[...], mine[...]).astype(F32)
    for s_t in range(2):
        for j in range(12):
            at = (s_t * 12 + j) * 138
            flat[:, at : at + 115] = rows[pl.ds(s_t * 16 + j, 16, stride=32), :][:, 0:115]
            last = rows[pl.ds(s_t * 16 + 12 + j // 3, 16, stride=32), :]
            flat[:, at + 115 : at + 138] = last[:, j % 3 * 23 : j % 3 * 23 + 23]
    grad_bias[...] = flat[...].reshape(grad_bias.shape)


def weights_kernel(info, mine, other, token, wqkv, wout, held, held_out, sems):
    token[...] = jnp.zeros_like(token)
    first = jnp.where(info[1] == 0, mine[...], other[...]).astype(F32)
    second = jnp.where(info[1] == 0, other[...], mine[...]).astype(F32)
    copies = []
    for k in range(6):
        rows = pl.ds(k % 2 * 256, 256)
        half = first if k < 4 else second
        held[k] = half[k % 4 * 256 : (k % 4 + 1) * 256]
        copies.append(pltpu.make_async_copy(held.at[k], wqkv.at[k // 2, rows], sems.at[k]))
        copies[-1].start()
    held_out[:, 0:256] = second[512:768]
    held_out[:, 256:512] = second[768:]
    for k in range(2):
        rows = pl.ds(k * 128, 128)
        copies.append(pltpu.make_async_copy(held_out.at[rows], wout.at[rows], sems.at[6 + k]))
        copies[-1].start()
    for copy in copies:
        copy.wait()


def bias_grad_kernel(info, ds, order, keep, send, part, entries, packed, *ends):
    entries[...] = jnp.zeros_like(entries)
    for p in range(12):
        for i in range(16):
            part[i * 12 : i * 12 + 12, :] = ds[i * WTOK + p * 12 : i * WTOK + p * 12 + 12, :]
        at = slice((11 - p) * 12, (11 - p) * 12 + WTOK)
        entries[:, at] = entries[:, at] + part[...]
    total = entries[...].astype(BF)
    packed[...] = jnp.zeros_like(packed)
    for s_u in range(2):
        rows = dot(total, order[s_u], NT)
        for half in range(32):
            at = half * 16 + s_u * 6
            packed[at : at + 6, 0:115] = rows[half * 6 : half * 6 + 6, 0:115]
        for q in range(3):
            last = ends[s_u * 3 + q]
            last[...] = jnp.zeros_like(last)
            last[:, q * 23 : q * 23 + 23] = rows[:, 115:138]
    for k in range(4):
        row = jnp.zeros((32, 128), F32)
        for q in range(3):
            s_u, r_t = (k * 3 + q) // 6, (k * 3 + q) % 6
            row = row + ends[s_u * 3 + q][pl.ds(r_t, 32, stride=6), :]
        packed[pl.ds(12 + k, 32, stride=16), :] = row
    mine, other = packed[0:256, :], packed[256:512, :]
    keep[...] = jnp.where(info[1] == 0, mine, other).astype(BF)
    send[...] = jnp.where(info[1] == 0, other, mine).astype(BF)


def final_kernel(latent, cot, gain, own, lon, lat, cor, output, grad, token):
    token[...] = jnp.zeros_like(token)
    for (by_lon, by_lat), ref in zip(PLACES, (own, lon, lat, cor)):
        out_term, hid_term = ref[0].astype(F32), ref[1].astype(F32)
        tile = latent[by_lon, by_lat]
        values = tile.reshape(out_term.shape).astype(F32)
        output[by_lon, by_lat] = (values + out_term).astype(BF).reshape(tile.shape)
        shifted = values - jnp.mean(values, -1, keepdims=True)
        inv_std = lax.rsqrt(jnp.mean(shifted * shifted, -1, keepdims=True) + 1e-05)
        normed = shifted * inv_std
        scaled = hid_term * gain[...]
        inner = scaled - jnp.mean(scaled, -1, keepdims=True) - normed * jnp.mean(scaled * normed, -1, keepdims=True)
        above = cot[by_lon, by_lat].reshape(out_term.shape).astype(F32)
        grad[by_lon, by_lat] = (above + inv_std * inner).astype(BF).reshape(tile.shape)


def moved(value, by_lon, by_lat):
    n_lon, n_lat = lax.axis_size("lon"), lax.axis_size("lat")
    pairs = [
        (i * n_lat + j, (i + by_lon) % n_lon * n_lat + (j + by_lat) % n_lat)
        for i in range(n_lon)
        for j in range(n_lat)
    ]
    return lax.ppermute(value, ("lon", "lat"), pairs)


def swapped(value, lon_bits, lat_bits):
    n_lon, n_lat = lax.axis_size("lon"), lax.axis_size("lat")
    pairs = [(i * n_lat + j, (i ^ lon_bits) * n_lat + (j ^ lat_bits)) for i in range(n_lon) for j in range(n_lat)]
    return lax.ppermute(value, ("lon", "lat"), pairs)


def across_y(value):
    n_lat = lax.axis_size("lat")
    groups = [list(range(x, n_lat, 2)) for x in range(2)]
    return lax.all_to_all(value, "lat", 0, 0, axis_index_groups=groups)


def across_z(value):
    n_lon = lax.axis_size("lon")
    groups = [list(range(core, n_lon, 2)) for core in range(2)]
    return lax.all_to_all(value, "lon", 0, 0, axis_index_groups=groups)


def other_group(value):
    return lax.ppermute(value, "tp", [(0, 1), (1, 0)])


def other_group_and_core(value):
    n_lon = lax.axis_size("lon")
    return lax.ppermute(value, ("lon", "tp"), [(i * 2 + j, (i ^ 1) * 2 + (j ^ 1)) for i in range(n_lon) for j in range(2)])


def on_device(latent, cotangent, ln_gain, w_qkv, w_out, bias_table):
    place, back = jnp.asarray(TO_WINDOW, BF), jnp.asarray(TO_WINDOW.T, BF)
    order = jnp.asarray(ORDER, BF)
    order_halves = jnp.asarray(ORDER.reshape(2, 138, 276), BF)
    i_lon, i_lat = lax.axis_index("lon"), lax.axis_index("lat")
    last = (i_lat == lax.axis_size("lat") - 1).astype(jnp.int32)
    core = i_lon % 2
    info = jnp.stack([last, core]).astype(jnp.int32)
    gain = ln_gain.reshape(1, 512)

    part = lambda n: ((2, n, 512), BF)
    halos = [part(216), part(72), part(72)]
    s_lon, s_lat, s_cor = call(halo_kernel, halos, [latent, cotangent], smem=0)
    in_lon, in_lat, in_cor = moved(s_lon, -1, 0), moved(s_lat, 0, -1), moved(s_cor, -1, -1)

    (bias,) = call(
        bias_kernel,
        [((16 * WTOK, WTOK), F32)],
        [info, bias_table, order],
        [pltpu.VMEM((192, 276), F32)] * 2 + [pltpu.VMEM((192, 128), F32)] * 2,
        us=2,
    )
    w_other = other_group(w_out)

    keep, send, ds, att, gq, gk, gv = call(
        main_kernel,
        [((1024, 256), F32), ((1024, 256), BF), ((16 * WTOK, WTOK), F32)] + [((576, 256), BF)] * 4,
        [info, latent, cotangent, in_lon, in_lat, in_cor, place, gain, w_qkv, w_out, bias],
        [pltpu.VMEM((576, 512), F32)],
        us=9,
        mib=32,
    )
    recv = swapped(send, 1, 0)
    (terms,) = call(terms_kernel, [((576, 768), BF)], [att, gq, gk, gv, w_qkv, back], smem=0, us=2)
    others = other_group(terms)
    own, s_lon, s_lat, s_cor, paired = call(
        pair_kernel, [part(216)] + halos + [TOKEN], [terms, others, w_out, w_other], smem=0, us=30
    )

    (total,) = call(core_sum_kernel, [((1024, 256), BF)], [keep, recv], smem=0, after=[terms], us=0.5)
    parts = across_y(total.reshape(4, 256, 256))
    b_keep, b_send = call(
        bias_grad_kernel,
        [((256, 128), BF)] * 2,
        [info, ds, order_halves],
        [pltpu.VMEM((192, WTOK), F32), pltpu.VMEM((192, 276), F32), pltpu.VMEM((512, 128), F32)]
        + [pltpu.VMEM((192, 128), F32)] * 6,
        us=2.5,
    )
    b_recv = swapped(b_send, 1, 0)
    (message,) = call(y_sum_kernel, [((8, 32, 384), BF)], [parts, b_keep, b_recv], smem=0, us=1)
    x_mine, b_sum = call(
        z_sum_kernel, [((32, 256), BF), ((32, 128), BF)], [across_z(message)], smem=0, after=[paired], us=1
    )
    (copies,) = call(x_sum_kernel, [((8, 32, 384), BF)], [x_mine, swapped(x_mine, 0, 1), b_sum], smem=0, us=1)
    r_lon, r_lat, r_cor = moved(s_lon, 1, 0), moved(s_lat, 0, 1), moved(s_cor, 1, 1)

    output, grad_latent, placed = call(
        final_kernel,
        [(latent.shape, BF), (latent.shape, BF), TOKEN],
        [latent, cotangent, gain, own, r_lon, r_lat, r_cor],
        smem=0,
        us=30,
    )

    copies, b_half = call(
        spread_kernel,
        [((4, 256, 256), BF), ((256, 128), BF)],
        [across_z(copies)],
        smem=0,
        us=1,
    )
    mine = across_y(copies).reshape(1024, 256)
    b_other = swapped(b_half, 1, 0)
    grad_bias, done = call(
        bias_out_kernel,
        [(bias_table.shape, F32), TOKEN],
        [info, b_half, b_other],
        [pltpu.VMEM((512, 128), F32), pltpu.VMEM((16, 3312), F32)],
        after=[placed],
    )

    (g_mine,) = call(
        gain_kernel, [((8, 512), F32)], [info, mine, w_qkv], after=[done], us=30
    )
    g_parts = [g_mine, swapped(g_mine, 1, 0), other_group(g_mine), other_group_and_core(g_mine)]
    done, grad_wqkv, grad_wout = call(
        weights_kernel,
        [TOKEN],
        [info, mine, swapped(mine, 1, 0)],
        [pltpu.VMEM((6, 256, 256), F32), pltpu.VMEM((256, 512), F32), pltpu.SemaphoreType.DMA((8,))],
        hbm_outs=[((3, 512, 256), F32), ((256, 512), F32)],
        us=2,
    )
    (grad_gain,) = call(
        gain_sum_kernel, [((1, 512), F32)], [*g_parts, gain], smem=0, after=[done]
    )
    grad_gain = grad_gain.reshape(512)
    return output, grad_latent, grad_gain, grad_wqkv, grad_wout, grad_bias


def solution(mesh):
    specs = (
        P("lon", "lat", None, None),
        P("lon", "lat", None, None),
        P(),
        P(None, None, "tp"),
        P("tp", None),
        P("lat", None, "tp", None),
    )
    return jax.shard_map(on_device, mesh=mesh, in_specs=specs, out_specs=specs, check_vma=False)
```

```python
import jax
import jax.numpy as jnp
import numpy as np
from jax import lax
from jax.experimental import pallas as pl
from jax.experimental.pallas import tpu as pltpu
from jax.sharding import PartitionSpec as P

BF = jnp.bfloat16
F32 = jnp.float32
WTOK = 144
OFFS = 23
NT = (((1,), (1,)), ((), ()))
TN = (((0,), (0,)), ((), ()))
SECTIONS = (0, 216, 432, 504, 576)


def section_row(lon, lat, lev):
    lat_cells = 9 if lat < 9 else 3
    return (lon >= 6) + 2 * (lat >= 9), (lon % 6 * lat_cells + lat % 9) * 4 + lev


def placement():
    place = np.zeros((576, 576), np.float32)
    for a in range(2):
        for b in range(2):
            for p in range(12):
                for s in range(2):
                    for r in range(6):
                        row = (a * 2 + b) * WTOK + p * 12 + s * 6 + r
                        section, at = section_row(p, a * 6 + r, (b * 2 + s + 1) % 4)
                        place[row, SECTIONS[section] + at] = 1
    return place


def offset_order():
    order = np.zeros((276, 276), np.float32)
    for rs in range(12):
        for k in range(OFFS):
            order[rs * OFFS + k, k * 12 + rs] = 1
    return order


TO_WINDOW = placement()
ORDER = offset_order()


def dot(a, b, dims=(((1,), (0,)), ((), ()))):
    return lax.dot_general(a, b, dims, preferred_element_type=F32)


def call(body, outs, args, scratch=(), smem=1, after=(), us=1, mib=16, hbm=(), hbm_outs=()):
    vmem, far = pl.BlockSpec(memory_space=pltpu.VMEM), pl.BlockSpec(memory_space=pltpu.HBM)
    n = len(args)
    m = n + len(hbm)

    def kernel(*refs):
        body(*refs[:m], *refs[m + len(after) :])

    return pl.pallas_call(
        kernel,
        out_shape=[jax.ShapeDtypeStruct(s, t) for s, t in [*outs, *hbm_outs]],
        in_specs=[pl.BlockSpec(memory_space=pltpu.SMEM)] * smem
        + [vmem] * (n - smem)
        + [far] * len(hbm)
        + [pl.BlockSpec(memory_space=pl.ANY)] * len(after),
        out_specs=[vmem] * len(outs) + [far] * len(hbm_outs),
        scratch_shapes=list(scratch),
        compiler_params=pltpu.CompilerParams(vmem_limit_bytes=mib * 1024 * 1024),
        cost_estimate=pl.CostEstimate(flops=int(us * 1e9), bytes_accessed=0, transcendentals=0),
    )(*args, *hbm, *after)


TOKEN = ((8, 128), F32)


LOW_LON, LOW_LAT, HIGH_LON, HIGH_LAT = slice(0, 6), slice(0, 3), slice(6, 12), slice(3, 12)
PLACES = ((HIGH_LON, HIGH_LAT), (LOW_LON, HIGH_LAT), (HIGH_LON, LOW_LAT), (LOW_LON, LOW_LAT))


def halo_kernel(latent, cot, *outs):
    for (lon, lat), ref in zip(PLACES[1:], outs):
        for j, grid in enumerate((latent, cot)):
            ref[j] = grid[lon, lat].reshape(ref.shape[1:])


def bias_kernel(info, table, order, w_out, bias, w_copy, raw, entries, low_u, high_u):
    w_copy[...] = w_out[...]
    flat = table[...].reshape(16, 3312)
    for s_t in range(2):
        for s_u in range(2):
            for r_t in range(6):
                at = ((s_t * 2 + s_u) * 6 + r_t) * 138
                row = (s_t * 6 + r_t) * 16
                raw[row : row + 16, s_u * 138 : s_u * 138 + 138] = flat[:, at : at + 138]
    full = raw[...]
    high = full.astype(BF)
    rest = full - high.astype(F32)
    mid = rest.astype(BF)
    low = (rest - mid.astype(F32)).astype(BF)
    entries[...] = dot(low, order[...]) + dot(mid, order[...]) + dot(high, order[...])
    row = lax.broadcasted_iota(jnp.int32, (192, WTOK), 0)
    col = lax.broadcasted_iota(jnp.int32, (192, WTOK), 1)
    rs_t, rs_u, which = row // 16, col % 12, row % 16
    s_t, s_u = (rs_t >= 6).astype(jnp.int32), (rs_u >= 6).astype(jnp.int32)
    edge_t = (rs_t - s_t * 6 >= 3).astype(jnp.int32)
    edge_u = (rs_u - s_u * 6 >= 3).astype(jnp.int32)
    last_lat = (which >= 8).astype(jnp.int32) * info[0]
    last_lev = ((which % 8) >= 4).astype(jnp.int32)
    barred = (last_lat * (edge_t - edge_u) != 0) | (last_lev * (s_t - s_u) != 0)
    for p in range(12):
        at = entries[:, (11 - p) * 12 : (11 - p) * 12 + WTOK]
        at = jnp.where(barred, -jnp.inf, at)
        low_u[...] = at[:, 0:128]
        high_u[:, 0:16] = at[:, 128:144]
        for i in range(16):
            rows = slice(i * WTOK + p * 12, i * WTOK + p * 12 + 12)
            bias[rows, 0:128] = low_u[pl.ds(i, 12, stride=16), :]
            bias[rows, 128:WTOK] = high_u[pl.ds(i, 12, stride=16), :][:, 0:16]


def main_kernel(info, latent, cotangent, lon, lat, cor, place, gain, w_qkv, w_out, bias,
                keep, send, o_ds, att_s, gq_s, gk_s, gv_s, joined):
    def gathered(which):
        own = (latent, cotangent)[which][HIGH_LON, HIGH_LAT].reshape(216, 512)
        for j, rows in enumerate((own, lon[which], lat[which], cor[which])):
            joined[SECTIONS[j] : SECTIONS[j + 1], :] = rows.astype(F32)
        return dot(place[...], joined[...].astype(BF))

    values = gathered(0)
    cot = gathered(1).astype(BF)
    shifted = values - jnp.mean(values, -1, keepdims=True)
    normed = shifted * lax.rsqrt(jnp.mean(shifted * shifted, -1, keepdims=True) + 1e-05)
    hidden = (normed * gain[...]).astype(BF)
    q, k, v = [dot(hidden, w_qkv[j]).astype(BF) for j in range(3)]
    down = dot(cot, w_out[...], NT).astype(BF)
    head = lax.broadcasted_iota(jnp.int32, (WTOK, 256), 1) // 64

    def stacked(rows):
        return jnp.concatenate([jnp.where(head == h, rows, jnp.zeros_like(rows)) for h in range(4)], 0)

    def unstacked(rows):
        total = jnp.zeros((WTOK, 256), F32)
        for h in range(4):
            total = jnp.where(head == h, rows[h * WTOK : (h + 1) * WTOK], total)
        return total

    for w in range(4):
        rows = slice(w * WTOK, (w + 1) * WTOK)
        four = slice(w * 576, (w + 1) * 576)
        qs, ds_ = stacked(q[rows]), stacked(down[rows])
        scores = dot(qs, k[rows], NT) * 0.125 + bias[four, :]
        exps = jnp.exp(scores - jnp.max(scores, -1, keepdims=True))
        probs = exps / jnp.sum(exps, -1, keepdims=True)
        probs_low = probs.astype(BF)
        att_s[rows, :] = unstacked(dot(probs_low, v[rows])).astype(BF)
        dp = dot(ds_, v[rows], NT)
        gv_s[rows, :] = dot(probs_low, ds_, TN).astype(BF)
        grad = probs * (dp - jnp.sum(dp * probs, -1, keepdims=True))
        o_ds[four, :] = grad
        grad_low = grad.astype(BF)
        gq_s[rows, :] = unstacked(dot(grad_low, k[rows]) * 0.125).astype(BF)
        gk_s[rows, :] = (dot(grad_low, qs, TN) * 0.125).astype(BF)

    att, gq, gk, gv = att_s[...], gq_s[...], gk_s[...], gv_s[...]
    wo = dot(att, cot, TN)
    first = [dot(hidden, gq, TN), dot(hidden, gk, TN)]
    second = [dot(hidden, gv, TN), jnp.concatenate([wo[:, :256], wo[:, 256:]], 0)]
    core = info[1]
    for j in range(2):
        rows = slice(j * 512, (j + 1) * 512)
        keep[rows, :] = jnp.where(core == 0, first[j], second[j])
        send[rows, :] = jnp.where(core == 0, second[j], first[j]).astype(BF)

def terms_kernel(att, gq, gk, gv, w_qkv, back, terms):
    hid_part = dot(gq[...], w_qkv[0], NT) + dot(gk[...], w_qkv[1], NT) + dot(gv[...], w_qkv[2], NT)
    terms[:, 0:256] = dot(back[...], att[...]).astype(BF)
    terms[:, 256:768] = dot(back[...], hid_part.astype(BF)).astype(BF)


def core_sum_kernel(keep, recv, total):
    total[...] = (keep[...] + recv[...].astype(F32)).astype(BF)


def y_sum_kernel(parts, b_keep, b_recv, message):
    total = parts[0].astype(F32)
    for j in range(1, 4):
        total = total + parts[j].astype(F32)
    total = total.astype(BF)
    both = (b_keep[...].astype(F32) + b_recv[...].astype(F32)).astype(BF)
    for j in range(8):
        rows = slice(j * 32, (j + 1) * 32)
        message[j, :, 0:256] = total[rows]
        message[j, :, 256:384] = both[rows]


def z_sum_kernel(parts, mine, bias):
    total = parts[0].astype(F32)
    for j in range(1, 8):
        total = total + parts[j].astype(F32)
    mine[...] = total[:, 0:256].astype(BF)
    bias[...] = total[:, 256:384].astype(BF)


def x_sum_kernel(mine, recv, bias, copies):
    total = (mine[...].astype(F32) + recv[...].astype(F32)).astype(BF)
    for j in range(8):
        copies[j, :, 0:256] = total
        copies[j, :, 256:384] = bias[...]


def pair_kernel(terms, others, w_out, w_other, o_own, o_lon, o_lat, o_cor, token):
    token[...] = jnp.zeros_like(token)
    out = dot(terms[:, 0:256], w_out[...]).astype(BF).astype(F32)
    out = out + dot(others[:, 0:256], w_other[...]).astype(BF).astype(F32)
    hid = terms[:, 256:768].astype(F32) + others[:, 256:768].astype(F32)
    for k, ref in enumerate((o_own, o_lon, o_lat, o_cor)):
        rows = slice(SECTIONS[k], SECTIONS[k + 1])
        ref[0] = out[rows].astype(BF)
        ref[1] = hid[rows].astype(BF)


def spread_kernel(parts, copies, b_half):
    for j in range(8):
        rows = slice(j * 32, (j + 1) * 32)
        for k in range(4):
            copies[k, rows, :] = parts[j, :, 0:256]
        b_half[rows, :] = parts[j, :, 256:384]


def gain_kernel(info, mine, w_qkv, out):
    rows = mine[...].astype(F32)
    w0, w1, w2 = [w_qkv[j].astype(F32) for j in range(3)]
    total = jnp.where(info[1] == 0, rows[:512] * w0 + rows[512:] * w1, rows[:512] * w2)
    ones = jnp.ones((8, 256), F32)
    out[...] = lax.dot_general(ones, total, NT, precision=lax.Precision.HIGHEST, preferred_element_type=F32)


def gain_sum_kernel(mine, other, mine_tp, other_tp, gain, out):
    total = (mine[0:1, :] + other[0:1, :]) + (mine_tp[0:1, :] + other_tp[0:1, :])
    out[...] = total / gain[...]


def bias_out_kernel(info, mine, other, grad_bias, token, rows, flat):
    token[...] = jnp.zeros_like(token)
    rows[0:256, :] = jnp.where(info[1] == 0, mine[...], other[...]).astype(F32)
    rows[256:512, :] = jnp.where(info[1] == 0, other[...], mine[...]).astype(F32)
    for s_t in range(2):
        for j in range(12):
            at = (s_t * 12 + j) * 138
            flat[:, at : at + 115] = rows[pl.ds(s_t * 16 + j, 16, stride=32), :][:, 0:115]
            last = rows[pl.ds(s_t * 16 + 12 + j // 3, 16, stride=32), :]
            flat[:, at + 115 : at + 138] = last[:, j % 3 * 23 : j % 3 * 23 + 23]
    grad_bias[...] = flat[...].reshape(grad_bias.shape)


def weights_kernel(info, mine, other, token, wqkv, wout, held, held_out, sems):
    token[...] = jnp.zeros_like(token)
    first = jnp.where(info[1] == 0, mine[...], other[...]).astype(F32)
    second = jnp.where(info[1] == 0, other[...], mine[...]).astype(F32)
    copies = []
    for k in range(6):
        rows = pl.ds(k % 2 * 256, 256)
        half = first if k < 4 else second
        held[k] = half[k % 4 * 256 : (k % 4 + 1) * 256]
        copies.append(pltpu.make_async_copy(held.at[k], wqkv.at[k // 2, rows], sems.at[k]))
        copies[-1].start()
    held_out[:, 0:256] = second[512:768]
    held_out[:, 256:512] = second[768:]
    for k in range(2):
        rows = pl.ds(k * 128, 128)
        copies.append(pltpu.make_async_copy(held_out.at[rows], wout.at[rows], sems.at[6 + k]))
        copies[-1].start()
    for copy in copies:
        copy.wait()


def bias_grad_kernel(info, ds, order, keep, send, part, entries, packed, *ends):
    entries[...] = jnp.zeros_like(entries)
    for p in range(12):
        for i in range(16):
            part[i * 12 : i * 12 + 12, :] = ds[i * WTOK + p * 12 : i * WTOK + p * 12 + 12, :]
        at = slice((11 - p) * 12, (11 - p) * 12 + WTOK)
        entries[:, at] = entries[:, at] + part[...]
    total = entries[...].astype(BF)
    packed[...] = jnp.zeros_like(packed)
    for s_u in range(2):
        rows = dot(total, order[s_u], NT)
        for half in range(32):
            at = half * 16 + s_u * 6
            packed[at : at + 6, 0:115] = rows[half * 6 : half * 6 + 6, 0:115]
        for q in range(3):
            last = ends[s_u * 3 + q]
            last[...] = jnp.zeros_like(last)
            last[:, q * 23 : q * 23 + 23] = rows[:, 115:138]
    for k in range(4):
        row = jnp.zeros((32, 128), F32)
        for q in range(3):
            s_u, r_t = (k * 3 + q) // 6, (k * 3 + q) % 6
            row = row + ends[s_u * 3 + q][pl.ds(r_t, 32, stride=6), :]
        packed[pl.ds(12 + k, 32, stride=16), :] = row
    mine, other = packed[0:256, :], packed[256:512, :]
    keep[...] = jnp.where(info[1] == 0, mine, other).astype(BF)
    send[...] = jnp.where(info[1] == 0, other, mine).astype(BF)


def final_kernel(latent, cot, gain, own, lon, lat, cor, output, grad, token):
    token[...] = jnp.zeros_like(token)
    for (by_lon, by_lat), ref in zip(PLACES, (own, lon, lat, cor)):
        out_term, hid_term = ref[0].astype(F32), ref[1].astype(F32)
        tile = latent[by_lon, by_lat]
        values = tile.reshape(out_term.shape).astype(F32)
        output[by_lon, by_lat] = (values + out_term).astype(BF).reshape(tile.shape)
        shifted = values - jnp.mean(values, -1, keepdims=True)
        inv_std = lax.rsqrt(jnp.mean(shifted * shifted, -1, keepdims=True) + 1e-05)
        normed = shifted * inv_std
        scaled = hid_term * gain[...]
        inner = scaled - jnp.mean(scaled, -1, keepdims=True) - normed * jnp.mean(scaled * normed, -1, keepdims=True)
        above = cot[by_lon, by_lat].reshape(out_term.shape).astype(F32)
        grad[by_lon, by_lat] = (above + inv_std * inner).astype(BF).reshape(tile.shape)


def moved(value, by_lon, by_lat):
    n_lon, n_lat = lax.axis_size("lon"), lax.axis_size("lat")
    flip = 1 if by_lat else 0
    pairs = [
        ((i * n_lat + j) * 2 + k, ((i + by_lon) % n_lon * n_lat + (j + by_lat) % n_lat) * 2 + (k ^ flip))
        for i in range(n_lon)
        for j in range(n_lat)
        for k in range(2)
    ]
    return lax.ppermute(value, ("lon", "lat", "tp"), pairs)


def swapped(value, lon_bits, lat_bits):
    n_lon, n_lat = lax.axis_size("lon"), lax.axis_size("lat")
    pairs = [(i * n_lat + j, (i ^ lon_bits) * n_lat + (j ^ lat_bits)) for i in range(n_lon) for j in range(n_lat)]
    return lax.ppermute(value, ("lon", "lat"), pairs)


def across_y(value):
    n_lat = lax.axis_size("lat")
    groups = [list(range(x, n_lat, 2)) for x in range(2)]
    return lax.all_to_all(value, "lat", 0, 0, axis_index_groups=groups)


def across_z(value):
    n_lon = lax.axis_size("lon")
    groups = [list(range(core, n_lon, 2)) for core in range(2)]
    return lax.all_to_all(value, "lon", 0, 0, axis_index_groups=groups)


def other_group(value):
    return lax.ppermute(value, "tp", [(0, 1), (1, 0)])


def other_group_and_core(value):
    n_lon = lax.axis_size("lon")
    return lax.ppermute(value, ("lon", "tp"), [(i * 2 + j, (i ^ 1) * 2 + (j ^ 1)) for i in range(n_lon) for j in range(2)])


def on_device(latent, cotangent, ln_gain, w_qkv, w_out, bias_table):
    place, back = jnp.asarray(TO_WINDOW, BF), jnp.asarray(TO_WINDOW.T, BF)
    order = jnp.asarray(ORDER, BF)
    order_halves = jnp.asarray(ORDER.reshape(2, 138, 276), BF)
    i_lon, i_lat = lax.axis_index("lon"), lax.axis_index("lat")
    last = (i_lat == lax.axis_size("lat") - 1).astype(jnp.int32)
    core = i_lon % 2
    info = jnp.stack([last, core]).astype(jnp.int32)
    gain = ln_gain.reshape(1, 512)

    part = lambda n: ((2, n, 512), BF)
    halos = [part(216), part(72), part(72)]
    s_lon, s_lat, s_cor = call(halo_kernel, halos, [latent, cotangent], smem=0)
    in_lon, in_lat, in_cor = moved(s_lon, -1, 0), moved(s_lat, 0, -1), moved(s_cor, -1, -1)

    bias, w_copy = call(
        bias_kernel,
        [((16 * WTOK, WTOK), F32), (w_out.shape, BF)],
        [info, bias_table, order, w_out],
        [pltpu.VMEM((192, 276), F32)] * 2 + [pltpu.VMEM((192, 128), F32)] * 2,
        us=2,
    )
    w_other = other_group(w_copy)

    keep, send, ds, att, gq, gk, gv = call(
        main_kernel,
        [((1024, 256), F32), ((1024, 256), BF), ((16 * WTOK, WTOK), F32)] + [((576, 256), BF)] * 4,
        [info, latent, cotangent, in_lon, in_lat, in_cor, place, gain, w_qkv, w_out, bias],
        [pltpu.VMEM((576, 512), F32)],
        us=9,
        mib=32,
    )
    recv = swapped(send, 1, 0)
    (terms,) = call(terms_kernel, [((576, 768), BF)], [att, gq, gk, gv, w_qkv, back], smem=0, after=[w_other], us=2)
    others = other_group(terms)
    own, s_lon, s_lat, s_cor, paired = call(
        pair_kernel, [part(216)] + halos + [TOKEN], [terms, others, w_out, w_other], smem=0, us=30
    )

    (total,) = call(core_sum_kernel, [((1024, 256), BF)], [keep, recv], smem=0, after=[terms], us=0.5)
    parts = across_y(total.reshape(4, 256, 256))
    b_keep, b_send = call(
        bias_grad_kernel,
        [((256, 128), BF)] * 2,
        [info, ds, order_halves],
        [pltpu.VMEM((192, WTOK), F32), pltpu.VMEM((192, 276), F32), pltpu.VMEM((512, 128), F32)]
        + [pltpu.VMEM((192, 128), F32)] * 6,
        us=2.5,
    )
    b_recv = swapped(b_send, 1, 0)
    (message,) = call(y_sum_kernel, [((8, 32, 384), BF)], [parts, b_keep, b_recv], smem=0, us=1)
    x_mine, b_sum = call(
        z_sum_kernel, [((32, 256), BF), ((32, 128), BF)], [across_z(message)], smem=0, after=[paired], us=1
    )
    (copies,) = call(x_sum_kernel, [((8, 32, 384), BF)], [x_mine, swapped(x_mine, 0, 1), b_sum], smem=0, us=1)
    r_lon, r_lat, r_cor = moved(s_lon, 1, 0), moved(s_lat, 0, 1), moved(s_cor, 1, 1)

    output, grad_latent, placed = call(
        final_kernel,
        [(latent.shape, BF), (latent.shape, BF), TOKEN],
        [latent, cotangent, gain, own, r_lon, r_lat, r_cor],
        smem=0,
        us=30,
    )

    copies, b_half = call(
        spread_kernel,
        [((4, 256, 256), BF), ((256, 128), BF)],
        [across_z(copies)],
        smem=0,
        us=1,
    )
    mine = across_y(copies).reshape(1024, 256)
    b_other = swapped(b_half, 1, 0)
    grad_bias, done = call(
        bias_out_kernel,
        [(bias_table.shape, F32), TOKEN],
        [info, b_half, b_other],
        [pltpu.VMEM((512, 128), F32), pltpu.VMEM((16, 3312), F32)],
        after=[placed],
    )

    (g_mine,) = call(
        gain_kernel, [((8, 512), F32)], [info, mine, w_qkv], after=[done], us=30
    )
    g_parts = [g_mine, swapped(g_mine, 1, 0), other_group(g_mine), other_group_and_core(g_mine)]
    done, grad_wqkv, grad_wout = call(
        weights_kernel,
        [TOKEN],
        [info, mine, swapped(mine, 1, 0)],
        [pltpu.VMEM((6, 256, 256), F32), pltpu.VMEM((256, 512), F32), pltpu.SemaphoreType.DMA((8,))],
        hbm_outs=[((3, 512, 256), F32), ((256, 512), F32)],
        us=2,
    )
    (grad_gain,) = call(
        gain_sum_kernel, [((1, 512), F32)], [*g_parts, gain], smem=0, after=[done]
    )
    grad_gain = grad_gain.reshape(512)
    return output, grad_latent, grad_gain, grad_wqkv, grad_wout, grad_bias


def solution(mesh):
    specs = (
        P("lon", "lat", None, None),
        P("lon", "lat", None, None),
        P(),
        P(None, None, "tp"),
        P("tp", None),
        P("lat", None, "tp", None),
    )
    return jax.shard_map(on_device, mesh=mesh, in_specs=specs, out_specs=specs, check_vma=False)
```

```python
import jax
import jax.numpy as jnp
import numpy as np
from jax import lax
from jax.experimental import pallas as pl
from jax.experimental.pallas import tpu as pltpu
from jax.sharding import PartitionSpec as P

BF = jnp.bfloat16
F32 = jnp.float32
WTOK = 144
OFFS = 23
NT = (((1,), (1,)), ((), ()))
TN = (((0,), (0,)), ((), ()))


def section_row(lon, lat, lev):
    if lat < 6:
        return (lon >= 6) * 144 + (lon % 6 * 6 + lat) * 4 + lev
    return (lat >= 9) * 144 + (lon >= 6) * 72 + (lon % 6 * 3 + lat % 3) * 4 + lev


def placement():
    place = np.zeros((2, 288, 288), np.float32)
    for a in range(2):
        for b in range(2):
            for p in range(12):
                for s in range(2):
                    for r in range(6):
                        row = b * WTOK + p * 12 + s * 6 + r
                        place[a, row, section_row(p, a * 6 + r, (b * 2 + s + 1) % 4)] = 1
    return place


def offset_order():
    order = np.zeros((276, 276), np.float32)
    for rs in range(12):
        for k in range(OFFS):
            order[rs * OFFS + k, k * 12 + rs] = 1
    return order


TO_WINDOW = placement()
ORDER = offset_order()


def dot(a, b, dims=(((1,), (0,)), ((), ()))):
    return lax.dot_general(a, b, dims, preferred_element_type=F32)


def call(body, outs, args, scratch=(), smem=1, after=(), us=1, mib=16, hbm=(), hbm_outs=()):
    vmem, far = pl.BlockSpec(memory_space=pltpu.VMEM), pl.BlockSpec(memory_space=pltpu.HBM)
    n = len(args)
    m = n + len(hbm)

    def kernel(*refs):
        body(*refs[:m], *refs[m + len(after) :])

    return pl.pallas_call(
        kernel,
        out_shape=[jax.ShapeDtypeStruct(s, t) for s, t in [*outs, *hbm_outs]],
        in_specs=[pl.BlockSpec(memory_space=pltpu.SMEM)] * smem
        + [vmem] * (n - smem)
        + [far] * len(hbm)
        + [pl.BlockSpec(memory_space=pl.ANY)] * len(after),
        out_specs=[vmem] * len(outs) + [far] * len(hbm_outs),
        scratch_shapes=list(scratch),
        compiler_params=pltpu.CompilerParams(vmem_limit_bytes=mib * 1024 * 1024),
        cost_estimate=pl.CostEstimate(flops=int(us * 1e9), bytes_accessed=0, transcendentals=0),
    )(*args, *hbm, *after)


TOKEN = ((8, 128), F32)


LOW_LON, LOW_LAT, HIGH_LON, MID_LAT, HIGH_LAT = slice(0, 6), slice(0, 3), slice(6, 12), slice(3, 9), slice(9, 12)
PLACES = (
    ((HIGH_LON, MID_LAT), (HIGH_LON, HIGH_LAT)),
    ((LOW_LON, MID_LAT), (LOW_LON, HIGH_LAT)),
    ((HIGH_LON, LOW_LAT),),
    ((LOW_LON, LOW_LAT),),
)


def flat(tile):
    return tile.reshape(-1, tile.shape[-1])


def halo_kernel(latent, cot, *outs):
    for places, ref in zip(PLACES[1:], outs):
        for j, grid in enumerate((latent, cot)):
            ref[j] = jnp.concatenate([flat(grid[lon, lat]) for lon, lat in places], 0)


def bias_kernel(info, table, order, w_out, bias, w_copy, raw, entries, low_u, high_u):
    w_copy[...] = w_out[...]
    flat = table[...].reshape(16, 3312)
    for s_t in range(2):
        for s_u in range(2):
            for r_t in range(6):
                at = ((s_t * 2 + s_u) * 6 + r_t) * 138
                row = (s_t * 6 + r_t) * 16
                raw[row : row + 16, s_u * 138 : s_u * 138 + 138] = flat[:, at : at + 138]
    full = raw[...]
    high = full.astype(BF)
    rest = full - high.astype(F32)
    mid = rest.astype(BF)
    low = (rest - mid.astype(F32)).astype(BF)
    entries[...] = dot(low, order[...]) + dot(mid, order[...]) + dot(high, order[...])
    row = lax.broadcasted_iota(jnp.int32, (192, WTOK), 0)
    col = lax.broadcasted_iota(jnp.int32, (192, WTOK), 1)
    rs_t, rs_u, which = row // 16, col % 12, row % 16
    s_t, s_u = (rs_t >= 6).astype(jnp.int32), (rs_u >= 6).astype(jnp.int32)
    edge_t = (rs_t - s_t * 6 >= 3).astype(jnp.int32)
    edge_u = (rs_u - s_u * 6 >= 3).astype(jnp.int32)
    last_lat = (which >= 8).astype(jnp.int32) * info[0]
    last_lev = ((which % 8) >= 4).astype(jnp.int32)
    barred = (last_lat * (edge_t - edge_u) != 0) | (last_lev * (s_t - s_u) != 0)
    for p in range(12):
        at = entries[:, (11 - p) * 12 : (11 - p) * 12 + WTOK]
        at = jnp.where(barred, -jnp.inf, at)
        low_u[...] = at[:, 0:128]
        high_u[:, 0:16] = at[:, 128:144]
        for i in range(16):
            rows = slice(i * WTOK + p * 12, i * WTOK + p * 12 + 12)
            bias[rows, 0:128] = low_u[pl.ds(i, 12, stride=16), :]
            bias[rows, 128:WTOK] = high_u[pl.ds(i, 12, stride=16), :][:, 0:16]


def main_kernel(info, latent, cotangent, lon, lat, cor, place, gain, w_qkv, w_out, bias,
                keep, send, o_ds, att_s, gq_s, gk_s, gv_s, joined):
    def gathered(which):
        grid = (latent, cotangent)[which]
        beside = lon[which].astype(F32)
        parts = (flat(grid[HIGH_LON, MID_LAT]), beside[0:144], flat(grid[HIGH_LON, HIGH_LAT]), beside[144:216])
        start = 0
        for rows in (*parts, lat[which], cor[which]):
            joined[start : start + rows.shape[0], :] = rows.astype(F32)
            start += rows.shape[0]
        rows = joined[...].astype(BF)
        return jnp.concatenate([dot(place[a], rows[a * 288 : (a + 1) * 288]) for a in range(2)], 0)

    values = gathered(0)
    cot = gathered(1).astype(BF)
    shifted = values - jnp.mean(values, -1, keepdims=True)
    normed = shifted * lax.rsqrt(jnp.mean(shifted * shifted, -1, keepdims=True) + 1e-05)
    hidden = (normed * gain[...]).astype(BF)
    q, k, v = [dot(hidden, w_qkv[j]).astype(BF) for j in range(3)]
    down = dot(cot, w_out[...], NT).astype(BF)
    head = lax.broadcasted_iota(jnp.int32, (WTOK, 256), 1) // 64

    def stacked(rows):
        return jnp.concatenate([jnp.where(head == h, rows, jnp.zeros_like(rows)) for h in range(4)], 0)

    def unstacked(rows):
        total = jnp.zeros((WTOK, 256), F32)
        for h in range(4):
            total = jnp.where(head == h, rows[h * WTOK : (h + 1) * WTOK], total)
        return total

    for w in range(4):
        rows = slice(w * WTOK, (w + 1) * WTOK)
        four = slice(w * 576, (w + 1) * 576)
        qs, ds_ = stacked(q[rows]), stacked(down[rows])
        scores = dot(qs, k[rows], NT) * 0.125 + bias[four, :]
        exps = jnp.exp(scores - jnp.max(scores, -1, keepdims=True))
        probs = exps / jnp.sum(exps, -1, keepdims=True)
        probs_low = probs.astype(BF)
        att_s[rows, :] = unstacked(dot(probs_low, v[rows])).astype(BF)
        dp = dot(ds_, v[rows], NT)
        gv_s[rows, :] = dot(probs_low, ds_, TN).astype(BF)
        grad = probs * (dp - jnp.sum(dp * probs, -1, keepdims=True))
        o_ds[four, :] = grad
        grad_low = grad.astype(BF)
        gq_s[rows, :] = unstacked(dot(grad_low, k[rows]) * 0.125).astype(BF)
        gk_s[rows, :] = (dot(grad_low, qs, TN) * 0.125).astype(BF)

    att, gq, gk, gv = att_s[...], gq_s[...], gk_s[...], gv_s[...]
    wo = dot(att, cot, TN)
    first = [dot(hidden, gq, TN), dot(hidden, gk, TN)]
    second = [dot(hidden, gv, TN), jnp.concatenate([wo[:, :256], wo[:, 256:]], 0)]
    core = info[1]
    for j in range(2):
        rows = slice(j * 512, (j + 1) * 512)
        keep[rows, :] = jnp.where(core == 0, first[j], second[j])
        send[rows, :] = jnp.where(core == 0, second[j], first[j]).astype(BF)

def terms_kernel(att, gq, gk, gv, w_qkv, back, terms):
    hid_part = dot(gq[...], w_qkv[0], NT) + dot(gk[...], w_qkv[1], NT) + dot(gv[...], w_qkv[2], NT)
    hid_part = hid_part.astype(BF)
    for a in range(2):
        rows = slice(a * 288, (a + 1) * 288)
        terms[rows, 0:256] = dot(back[a], att[rows, :]).astype(BF)
        terms[rows, 256:768] = dot(back[a], hid_part[rows]).astype(BF)


def sent(copies, source, target, sem):
    copies.append(pltpu.make_async_copy(source, target, sem))
    copies[-1].start()


def finish(copies):
    for copy in copies:
        copy.wait()


def core_sum_kernel(keep, recv, total, held, sems):
    copies = []
    for k in range(4):
        rows = slice(k * 256, (k + 1) * 256)
        held[k] = (keep[rows, :] + recv[rows, :].astype(F32)).astype(BF)
        sent(copies, held.at[k], total.at[k], sems.at[k])
    finish(copies)


def y_sum_kernel(parts, b_keep, b_recv, message, held, sems):
    copies = []
    for j in range(8):
        rows = slice(j * 32, (j + 1) * 32)
        total = parts[0, rows, :].astype(F32)
        for k in range(1, 4):
            total = total + parts[k, rows, :].astype(F32)
        held[j, :, 0:256] = total.astype(BF)
        held[j, :, 256:384] = (b_keep[rows, :].astype(F32) + b_recv[rows, :].astype(F32)).astype(BF)
        sent(copies, held.at[j], message.at[j], sems.at[j])
    finish(copies)


def z_sum_kernel(parts, mine, bias):
    total = parts[0].astype(F32)
    for j in range(1, 8):
        total = total + parts[j].astype(F32)
    mine[...] = total[:, 0:256].astype(BF)
    bias[...] = total[:, 256:384].astype(BF)


def x_sum_kernel(mine, recv, bias, out, held, sems):
    held[:, 0:256] = (mine[...].astype(F32) + recv[...].astype(F32)).astype(BF)
    held[:, 256:384] = bias[...]
    copies = []
    for j in range(8):
        sent(copies, held, out.at[j], sems.at[j])
    finish(copies)


def pair_kernel(terms, others, w_out, w_other, o_own, o_lon, o_lat, o_cor, token):
    token[...] = jnp.zeros_like(token)
    out = dot(terms[:, 0:256], w_out[...]).astype(BF).astype(F32)
    out = out + dot(others[:, 0:256], w_other[...]).astype(BF).astype(F32)
    hid = terms[:, 256:768].astype(F32) + others[:, 256:768].astype(F32)
    for j, rows in enumerate((out, hid)):
        o_own[j] = jnp.concatenate([rows[0:144], rows[288:360]], 0).astype(BF)
        o_lon[j] = jnp.concatenate([rows[144:288], rows[360:432]], 0).astype(BF)
        o_lat[j] = rows[432:504].astype(BF)
        o_cor[j] = rows[504:576].astype(BF)


def spread_kernel(parts, b_half, out, held, sems):
    for j in range(8):
        rows = slice(j * 32, (j + 1) * 32)
        held[rows, :] = parts[j, :, 0:256]
        b_half[rows, :] = parts[j, :, 256:384]
    copies = []
    for k in range(4):
        sent(copies, held, out.at[k], sems.at[k])
    finish(copies)


def gain_kernel(info, mine, w_qkv, out):
    rows = mine[...].astype(F32)
    w0, w1, w2 = [w_qkv[j].astype(F32) for j in range(3)]
    total = jnp.where(info[1] == 0, rows[:512] * w0 + rows[512:] * w1, rows[:512] * w2)
    total = total[:, 0:128] + total[:, 128:256]
    high = total.astype(BF)
    low = (total - high.astype(F32)).astype(BF)
    ones = jnp.ones((8, 128), BF)
    out[...] = dot(ones, high, NT) + dot(ones, low, NT)


def gain_sum_kernel(mine, other, mine_tp, other_tp, gain, out):
    total = (mine[0:1, :] + other[0:1, :]) + (mine_tp[0:1, :] + other_tp[0:1, :])
    out[...] = total / gain[...]


def bias_out_kernel(info, mine, other, grad_bias, token, rows, flat):
    token[...] = jnp.zeros_like(token)
    rows[0:256, :] = jnp.where(info[1] == 0, mine[...], other[...]).astype(F32)
    rows[256:512, :] = jnp.where(info[1] == 0, other[...], mine[...]).astype(F32)
    for s_t in range(2):
        for j in range(12):
            at = (s_t * 12 + j) * 138
            flat[:, at : at + 115] = rows[pl.ds(s_t * 16 + j, 16, stride=32), :][:, 0:115]
            last = rows[pl.ds(s_t * 16 + 12 + j // 3, 16, stride=32), :]
            flat[:, at + 115 : at + 138] = last[:, j % 3 * 23 : j % 3 * 23 + 23]
    grad_bias[...] = flat[...].reshape(grad_bias.shape)


def weights_kernel(info, mine, other, token, wqkv, wout, held, held_out, sems):
    token[...] = jnp.zeros_like(token)
    first = jnp.where(info[1] == 0, mine[...], other[...]).astype(F32)
    second = jnp.where(info[1] == 0, other[...], mine[...]).astype(F32)
    copies = []
    for k in range(6):
        rows = pl.ds(k % 2 * 256, 256)
        half = first if k < 4 else second
        held[k] = half[k % 4 * 256 : (k % 4 + 1) * 256]
        copies.append(pltpu.make_async_copy(held.at[k], wqkv.at[k // 2, rows], sems.at[k]))
        copies[-1].start()
    held_out[:, 0:256] = second[512:768]
    held_out[:, 256:512] = second[768:]
    for k in range(2):
        rows = pl.ds(k * 128, 128)
        copies.append(pltpu.make_async_copy(held_out.at[rows], wout.at[rows], sems.at[6 + k]))
        copies[-1].start()
    for copy in copies:
        copy.wait()


def bias_grad_kernel(info, ds, order, keep, send, part, entries, packed, *ends):
    entries[...] = jnp.zeros_like(entries)
    for p in range(12):
        for i in range(16):
            part[i * 12 : i * 12 + 12, :] = ds[i * WTOK + p * 12 : i * WTOK + p * 12 + 12, :]
        at = slice((11 - p) * 12, (11 - p) * 12 + WTOK)
        entries[:, at] = entries[:, at] + part[...]
    total = entries[...].astype(BF)
    packed[...] = jnp.zeros_like(packed)
    for s_u in range(2):
        rows = dot(total, order[s_u], NT)
        for half in range(32):
            at = half * 16 + s_u * 6
            packed[at : at + 6, 0:115] = rows[half * 6 : half * 6 + 6, 0:115]
        for q in range(3):
            last = ends[s_u * 3 + q]
            last[...] = jnp.zeros_like(last)
            last[:, q * 23 : q * 23 + 23] = rows[:, 115:138]
    for k in range(4):
        row = jnp.zeros((32, 128), F32)
        for q in range(3):
            s_u, r_t = (k * 3 + q) // 6, (k * 3 + q) % 6
            row = row + ends[s_u * 3 + q][pl.ds(r_t, 32, stride=6), :]
        packed[pl.ds(12 + k, 32, stride=16), :] = row
    mine, other = packed[0:256, :], packed[256:512, :]
    keep[...] = jnp.where(info[1] == 0, mine, other).astype(BF)
    send[...] = jnp.where(info[1] == 0, other, mine).astype(BF)


def final_kernel(latent, cot, gain, own, lon, lat, cor, token, output, grad, held, sems):
    token[...] = jnp.zeros_like(token)
    copies = []
    for k in (1, 3, 0, 2):
        ref = (own, lon, lat, cor)[k]
        out_terms, hid_terms = ref[0].astype(F32), ref[1].astype(F32)
        start = 0
        for by_lon, by_lat in PLACES[k]:
            tile = latent[by_lon, by_lat]
            values = flat(tile).astype(F32)
            rows = slice(start, start + values.shape[0])
            start += values.shape[0]
            held[0, by_lon, by_lat] = (values + out_terms[rows]).astype(BF).reshape(tile.shape)
            shifted = values - jnp.mean(values, -1, keepdims=True)
            inv_std = lax.rsqrt(jnp.mean(shifted * shifted, -1, keepdims=True) + 1e-05)
            normed = shifted * inv_std
            scaled = hid_terms[rows] * gain[...]
            inner = scaled - jnp.mean(scaled, -1, keepdims=True) - normed * jnp.mean(scaled * normed, -1, keepdims=True)
            above = flat(cot[by_lon, by_lat]).astype(F32)
            held[1, by_lon, by_lat] = (above + inv_std * inner).astype(BF).reshape(tile.shape)
        if k >= 2:
            for j, ref in enumerate((output, grad)):
                for first in (0, 3):
                    rows = pl.ds(first + (6 if k == 2 else 0), 3)
                    sent(copies, held.at[j, rows], ref.at[rows], sems.at[len(copies)])
    finish(copies)


def moved(value, by_lon, by_lat):
    n_lon, n_lat = lax.axis_size("lon"), lax.axis_size("lat")
    flip = 1 if by_lat else 0
    pairs = [
        ((i * n_lat + j) * 2 + k, ((i + by_lon) % n_lon * n_lat + (j + by_lat) % n_lat) * 2 + (k ^ flip))
        for i in range(n_lon)
        for j in range(n_lat)
        for k in range(2)
    ]
    return lax.ppermute(value, ("lon", "lat", "tp"), pairs)


def swapped(value, lon_bits, lat_bits):
    n_lon, n_lat = lax.axis_size("lon"), lax.axis_size("lat")
    pairs = [(i * n_lat + j, (i ^ lon_bits) * n_lat + (j ^ lat_bits)) for i in range(n_lon) for j in range(n_lat)]
    return lax.ppermute(value, ("lon", "lat"), pairs)


def across_y(value):
    n_lat = lax.axis_size("lat")
    groups = [list(range(x, n_lat, 2)) for x in range(2)]
    return lax.all_to_all(value, "lat", 0, 0, axis_index_groups=groups)


def across_z(value):
    n_lon = lax.axis_size("lon")
    groups = [list(range(core, n_lon, 2)) for core in range(2)]
    return lax.all_to_all(value, "lon", 0, 0, axis_index_groups=groups)


def other_group(value):
    return lax.ppermute(value, "tp", [(0, 1), (1, 0)])


def other_group_and_core(value):
    n_lon = lax.axis_size("lon")
    return lax.ppermute(value, ("lon", "tp"), [(i * 2 + j, (i ^ 1) * 2 + (j ^ 1)) for i in range(n_lon) for j in range(2)])


def on_device(latent, cotangent, ln_gain, w_qkv, w_out, bias_table):
    place, back = jnp.asarray(TO_WINDOW, BF), jnp.asarray(TO_WINDOW.transpose(0, 2, 1), BF)
    order = jnp.asarray(ORDER, BF)
    order_halves = jnp.asarray(ORDER.reshape(2, 138, 276), BF)
    i_lon, i_lat = lax.axis_index("lon"), lax.axis_index("lat")
    last = (i_lat == lax.axis_size("lat") - 1).astype(jnp.int32)
    core = i_lon % 2
    info = jnp.stack([last, core]).astype(jnp.int32)
    gain = ln_gain.reshape(1, 512)

    part = lambda n: ((2, n, 512), BF)
    halos = [part(216), part(72), part(72)]
    s_lon, s_lat, s_cor = call(halo_kernel, halos, [latent, cotangent], smem=0)
    in_lon, in_lat, in_cor = moved(s_lon, -1, 0), moved(s_lat, 0, -1), moved(s_cor, -1, -1)

    bias, w_copy = call(
        bias_kernel,
        [((16 * WTOK, WTOK), F32), (w_out.shape, BF)],
        [info, bias_table, order, w_out],
        [pltpu.VMEM((192, 276), F32)] * 2 + [pltpu.VMEM((192, 128), F32)] * 2,
        us=2,
    )
    w_other = other_group(w_copy)

    keep, send, ds, att, gq, gk, gv = call(
        main_kernel,
        [((1024, 256), F32), ((1024, 256), BF), ((16 * WTOK, WTOK), F32)] + [((576, 256), BF)] * 4,
        [info, latent, cotangent, in_lon, in_lat, in_cor, place, gain, w_qkv, w_out, bias],
        [pltpu.VMEM((576, 512), F32)],
        us=9,
        mib=32,
    )
    recv = swapped(send, 1, 0)
    (terms,) = call(terms_kernel, [((576, 768), BF)], [att, gq, gk, gv, w_qkv, back], smem=0, after=[w_other], us=2)
    others = other_group(terms)
    own, s_lon, s_lat, s_cor, paired = call(
        pair_kernel, [part(216)] + halos + [TOKEN], [terms, others, w_out, w_other], smem=0, us=30
    )

    (total,) = call(
        core_sum_kernel,
        [],
        [keep, recv],
        [pltpu.VMEM((4, 256, 256), BF), pltpu.SemaphoreType.DMA((4,))],
        smem=0,
        after=[terms],
        us=0.5,
        hbm_outs=[((4, 256, 256), BF)],
    )
    parts = across_y(total)
    b_keep, b_send = call(
        bias_grad_kernel,
        [((256, 128), BF)] * 2,
        [info, ds, order_halves],
        [pltpu.VMEM((192, WTOK), F32), pltpu.VMEM((192, 276), F32), pltpu.VMEM((512, 128), F32)]
        + [pltpu.VMEM((192, 128), F32)] * 6,
        us=2.5,
    )
    b_recv = swapped(b_send, 1, 0)
    (message,) = call(
        y_sum_kernel,
        [],
        [parts, b_keep, b_recv],
        [pltpu.VMEM((8, 32, 384), BF), pltpu.SemaphoreType.DMA((8,))],
        smem=0,
        hbm_outs=[((8, 32, 384), BF)],
    )
    x_mine, b_sum = call(
        z_sum_kernel, [((32, 256), BF), ((32, 128), BF)], [across_z(message)], smem=0, after=[paired], us=1
    )
    (copies,) = call(
        x_sum_kernel,
        [],
        [x_mine, swapped(x_mine, 0, 1), b_sum],
        [pltpu.VMEM((32, 384), BF), pltpu.SemaphoreType.DMA((8,))],
        smem=0,
        hbm_outs=[((8, 32, 384), BF)],
    )
    r_lon, r_lat, r_cor = moved(s_lon, 1, 0), moved(s_lat, 0, 1), moved(s_cor, 1, 1)

    placed, output, grad_latent = call(
        final_kernel,
        [TOKEN],
        [latent, cotangent, gain, own, r_lon, r_lat, r_cor],
        [pltpu.VMEM((2,) + latent.shape, BF), pltpu.SemaphoreType.DMA((8,))],
        hbm_outs=[(latent.shape, BF)] * 2,
        smem=0,
        us=30,
    )

    b_half, copies = call(
        spread_kernel,
        [((256, 128), BF)],
        [across_z(copies)],
        [pltpu.VMEM((256, 256), BF), pltpu.SemaphoreType.DMA((4,))],
        smem=0,
        hbm_outs=[((4, 256, 256), BF)],
    )
    mine = across_y(copies).reshape(1024, 256)
    b_other = swapped(b_half, 1, 0)
    grad_bias, done = call(
        bias_out_kernel,
        [(bias_table.shape, F32), TOKEN],
        [info, b_half, b_other],
        [pltpu.VMEM((512, 128), F32), pltpu.VMEM((16, 3312), F32)],
        after=[placed],
    )

    (g_mine,) = call(
        gain_kernel, [((8, 512), F32)], [info, mine, w_qkv], after=[done], us=30
    )
    g_parts = [g_mine, swapped(g_mine, 1, 0), other_group(g_mine), other_group_and_core(g_mine)]
    done, grad_wqkv, grad_wout = call(
        weights_kernel,
        [TOKEN],
        [info, mine, swapped(mine, 1, 0)],
        [pltpu.VMEM((6, 256, 256), F32), pltpu.VMEM((256, 512), F32), pltpu.SemaphoreType.DMA((8,))],
        hbm_outs=[((3, 512, 256), F32), ((256, 512), F32)],
        us=2,
    )
    (grad_gain,) = call(
        gain_sum_kernel, [((1, 512), F32)], [*g_parts, gain], smem=0, after=[done]
    )
    grad_gain = grad_gain.reshape(512)
    return output, grad_latent, grad_gain, grad_wqkv, grad_wout, grad_bias


def solution(mesh):
    specs = (
        P("lon", "lat", None, None),
        P("lon", "lat", None, None),
        P(),
        P(None, None, "tp"),
        P("tp", None),
        P("lat", None, "tp", None),
    )
    return jax.shard_map(on_device, mesh=mesh, in_specs=specs, out_specs=specs, check_vma=False)
```

```python
import jax
import jax.numpy as jnp
import numpy as np
from jax import lax
from jax.experimental import pallas as pl
from jax.experimental.pallas import tpu as pltpu
from jax.sharding import PartitionSpec as P

BF = jnp.bfloat16
F32 = jnp.float32
WTOK = 144
OFFS = 23
NT = (((1,), (1,)), ((), ()))
TN = (((0,), (0,)), ((), ()))


def section_row(lon, lat, lev):
    if lat < 6:
        return (lon >= 6) * 144 + (lon % 6 * 6 + lat) * 4 + lev
    return (lat >= 9) * 144 + (lon >= 6) * 72 + (lon % 6 * 3 + lat % 3) * 4 + lev


def placement():
    place = np.zeros((2, 288, 288), np.float32)
    for a in range(2):
        for b in range(2):
            for p in range(12):
                for s in range(2):
                    for r in range(6):
                        row = b * WTOK + p * 12 + s * 6 + r
                        place[a, row, section_row(p, a * 6 + r, (b * 2 + s + 1) % 4)] = 1
    return place


def offset_order():
    order = np.zeros((276, 276), np.float32)
    for rs in range(12):
        for k in range(OFFS):
            order[rs * OFFS + k, k * 12 + rs] = 1
    return order


TO_WINDOW = placement()
ORDER = offset_order()


def dot(a, b, dims=(((1,), (0,)), ((), ()))):
    return lax.dot_general(a, b, dims, preferred_element_type=F32)


def call(body, outs, args, scratch=(), smem=1, after=(), us=1, mib=16, hbm=(), hbm_outs=()):
    vmem, far = pl.BlockSpec(memory_space=pltpu.VMEM), pl.BlockSpec(memory_space=pltpu.HBM)
    n = len(args)
    m = n + len(hbm)

    def kernel(*refs):
        body(*refs[:m], *refs[m + len(after) :])

    return pl.pallas_call(
        kernel,
        out_shape=[jax.ShapeDtypeStruct(s, t) for s, t in [*outs, *hbm_outs]],
        in_specs=[pl.BlockSpec(memory_space=pltpu.SMEM)] * smem
        + [vmem] * (n - smem)
        + [far] * len(hbm)
        + [pl.BlockSpec(memory_space=pl.ANY)] * len(after),
        out_specs=[vmem] * len(outs) + [far] * len(hbm_outs),
        scratch_shapes=list(scratch),
        compiler_params=pltpu.CompilerParams(vmem_limit_bytes=mib * 1024 * 1024),
        cost_estimate=pl.CostEstimate(flops=int(us * 1e9), bytes_accessed=0, transcendentals=0),
    )(*args, *hbm, *after)


TOKEN = ((8, 128), F32)


LOW_LON, LOW_LAT, HIGH_LON, MID_LAT, HIGH_LAT = slice(0, 6), slice(0, 3), slice(6, 12), slice(3, 9), slice(9, 12)
PLACES = (
    ((HIGH_LON, MID_LAT), (HIGH_LON, HIGH_LAT)),
    ((LOW_LON, MID_LAT), (LOW_LON, HIGH_LAT)),
    ((HIGH_LON, LOW_LAT),),
    ((LOW_LON, LOW_LAT),),
)


def flat(tile):
    return tile.reshape(-1, tile.shape[-1])


def sent(copies, source, target, sem):
    copies.append(pltpu.make_async_copy(source, target, sem))
    copies[-1].start()


def finish(copies):
    for copy in copies:
        copy.wait()


def halo_kernel(latent, cot, o_lon, o_lat, o_cor, tiles, h_lon, h_lat, h_cor, in_sems, out_sems):
    arrived, copies = [], []
    for first in (0, 3, 6, 9):
        for j, grid in enumerate((latent, cot)):
            rows = pl.ds(first, 3)
            sent(arrived, grid.at[rows], tiles.at[j, rows], in_sems.at[len(arrived)])
    finish(arrived[:4])
    for places, held, ref in ((PLACES[1], h_lon, o_lon), (PLACES[3], h_cor, o_cor), (PLACES[2], h_lat, o_lat)):
        if held is h_lat:
            finish(arrived[4:])
        for j in range(2):
            held[j] = jnp.concatenate([flat(tiles[j, lon, lat]) for lon, lat in places], 0)
            sent(copies, held.at[j], ref.at[j], out_sems.at[len(copies)])
    finish(copies)


def bias_kernel(info, table, order, w_out, bias, w_copy, raw, entries, t0, t1, t2):
    w_copy[...] = w_out[...]
    flat = table[...].reshape(16, 3312)
    for s_t in range(2):
        for s_u in range(2):
            for r_t in range(6):
                at = ((s_t * 2 + s_u) * 6 + r_t) * 138
                row = (s_t * 6 + r_t) * 16
                raw[row : row + 16, s_u * 138 : s_u * 138 + 138] = flat[:, at : at + 138]
    full = raw[...]
    high = full.astype(BF)
    rest = full - high.astype(F32)
    mid = rest.astype(BF)
    low = (rest - mid.astype(F32)).astype(BF)
    wide = dot(low, order[...]) + dot(mid, order[...]) + dot(high, order[...])
    t0[...] = wide[:, 0:128]
    t1[...] = wide[:, 128:256]
    t2[:, 0:20] = wide[:, 256:276]
    for i in range(16):
        at, rows = pl.ds(i, 12, stride=16), slice(i * 12, i * 12 + 12)
        entries[rows, 0:128] = t0[at, :]
        entries[rows, 128:256] = t1[at, :]
        entries[rows, 256:276] = t2[at, :][:, 0:20]
    row = lax.broadcasted_iota(jnp.int32, (192, WTOK), 0)
    col = lax.broadcasted_iota(jnp.int32, (192, WTOK), 1)
    rs_t, rs_u, which = row % 12, col % 12, row // 12
    s_t, s_u = (rs_t >= 6).astype(jnp.int32), (rs_u >= 6).astype(jnp.int32)
    edge_t = (rs_t - s_t * 6 >= 3).astype(jnp.int32)
    edge_u = (rs_u - s_u * 6 >= 3).astype(jnp.int32)
    last_lat = (which >= 8).astype(jnp.int32) * info[0]
    last_lev = ((which % 8) >= 4).astype(jnp.int32)
    barred = (last_lat * (edge_t - edge_u) != 0) | (last_lev * (s_t - s_u) != 0)
    for p in range(12):
        at = jnp.where(barred, -jnp.inf, entries[:, (11 - p) * 12 : (11 - p) * 12 + WTOK])
        for i in range(16):
            bias[i * WTOK + p * 12 : i * WTOK + p * 12 + 12, :] = at[i * 12 : i * 12 + 12]


def main_kernel(info, latent, cotangent, lon, lat, cor, place, gain, w_qkv, w_out, bias,
                keep, send, o_ds, att_s, gq_s, gk_s, gv_s, joined):
    def gathered(which):
        grid = (latent, cotangent)[which]
        beside = lon[which].astype(F32)
        parts = (flat(grid[HIGH_LON, MID_LAT]), beside[0:144], flat(grid[HIGH_LON, HIGH_LAT]), beside[144:216])
        start = 0
        for rows in (*parts, lat[which], cor[which]):
            joined[start : start + rows.shape[0], :] = rows.astype(F32)
            start += rows.shape[0]
        rows = joined[...].astype(BF)
        return jnp.concatenate([dot(place[a], rows[a * 288 : (a + 1) * 288]) for a in range(2)], 0)

    values = gathered(0)
    cot = gathered(1).astype(BF)
    shifted = values - jnp.mean(values, -1, keepdims=True)
    normed = shifted * lax.rsqrt(jnp.mean(shifted * shifted, -1, keepdims=True) + 1e-05)
    hidden = (normed * gain[...]).astype(BF)
    q, k, v = [dot(hidden, w_qkv[j]).astype(BF) for j in range(3)]
    down = dot(cot, w_out[...], NT).astype(BF)
    head = lax.broadcasted_iota(jnp.int32, (WTOK, 256), 1) // 64

    def stacked(rows):
        return jnp.concatenate([jnp.where(head == h, rows, jnp.zeros_like(rows)) for h in range(4)], 0)

    def unstacked(rows):
        total = jnp.zeros((WTOK, 256), F32)
        for h in range(4):
            total = jnp.where(head == h, rows[h * WTOK : (h + 1) * WTOK], total)
        return total

    for w in range(4):
        rows = slice(w * WTOK, (w + 1) * WTOK)
        four = slice(w * 576, (w + 1) * 576)
        qs, ds_ = stacked(q[rows]), stacked(down[rows])
        scores = dot(qs, k[rows], NT) * 0.125 + bias[four, :]
        exps = jnp.exp(scores - jnp.max(scores, -1, keepdims=True))
        probs = exps / jnp.sum(exps, -1, keepdims=True)
        probs_low = probs.astype(BF)
        att_s[rows, :] = unstacked(dot(probs_low, v[rows])).astype(BF)
        dp = dot(ds_, v[rows], NT)
        gv_s[rows, :] = dot(probs_low, ds_, TN).astype(BF)
        grad = probs * (dp - jnp.sum(dp * probs, -1, keepdims=True))
        o_ds[four, :] = grad
        grad_low = grad.astype(BF)
        gq_s[rows, :] = unstacked(dot(grad_low, k[rows]) * 0.125).astype(BF)
        gk_s[rows, :] = (dot(grad_low, qs, TN) * 0.125).astype(BF)

    att, gq, gk, gv = att_s[...], gq_s[...], gk_s[...], gv_s[...]
    wo = dot(att, cot, TN)
    first = [dot(hidden, gq, TN), dot(hidden, gk, TN)]
    second = [dot(hidden, gv, TN), jnp.concatenate([wo[:, :256], wo[:, 256:]], 0)]
    core = info[1]
    for j in range(2):
        rows = slice(j * 512, (j + 1) * 512)
        keep[rows, :] = jnp.where(core == 0, first[j], second[j])
        send[rows, :] = jnp.where(core == 0, second[j], first[j]).astype(BF)

def terms_kernel(att, gq, gk, gv, w_qkv, back, terms):
    hid_part = dot(gq[...], w_qkv[0], NT) + dot(gk[...], w_qkv[1], NT) + dot(gv[...], w_qkv[2], NT)
    hid_part = hid_part.astype(BF)
    for a in range(2):
        rows = slice(a * 288, (a + 1) * 288)
        terms[rows, 0:256] = dot(back[a], att[rows, :]).astype(BF)
        terms[rows, 256:768] = dot(back[a], hid_part[rows]).astype(BF)


def core_sum_kernel(keep, recv, total, held, sems):
    copies = []
    for k in range(4):
        rows = slice(k * 256, (k + 1) * 256)
        held[k] = (keep[rows, :] + recv[rows, :].astype(F32)).astype(BF)
        sent(copies, held.at[k], total.at[k], sems.at[k])
    finish(copies)


def y_sum_kernel(parts, b_keep, b_recv, message, held, sems):
    copies = []
    for j in range(8):
        rows = slice(j * 32, (j + 1) * 32)
        total = parts[0, rows, :].astype(F32)
        for k in range(1, 4):
            total = total + parts[k, rows, :].astype(F32)
        held[j, :, 0:256] = total.astype(BF)
        held[j, :, 256:384] = (b_keep[rows, :].astype(F32) + b_recv[rows, :].astype(F32)).astype(BF)
        sent(copies, held.at[j], message.at[j], sems.at[j])
    finish(copies)


def z_sum_kernel(parts, mine, bias):
    total = parts[0].astype(F32)
    for j in range(1, 8):
        total = total + parts[j].astype(F32)
    mine[...] = total[:, 0:256].astype(BF)
    bias[...] = total[:, 256:384].astype(BF)


def x_sum_kernel(mine, recv, bias, out, held, sems):
    held[:, 0:256] = (mine[...].astype(F32) + recv[...].astype(F32)).astype(BF)
    held[:, 256:384] = bias[...]
    copies = []
    for j in range(8):
        sent(copies, held, out.at[j], sems.at[j])
    finish(copies)


def pair_kernel(terms, others, w_out, w_other, o_own, o_lon, o_lat, o_cor, token):
    token[...] = jnp.zeros_like(token)
    out = dot(terms[:, 0:256], w_out[...]).astype(BF).astype(F32)
    out = out + dot(others[:, 0:256], w_other[...]).astype(BF).astype(F32)
    hid = terms[:, 256:768].astype(F32) + others[:, 256:768].astype(F32)
    for j, rows in enumerate((out, hid)):
        o_own[j] = jnp.concatenate([rows[0:144], rows[288:360]], 0).astype(BF)
        o_lon[j] = jnp.concatenate([rows[144:288], rows[360:432]], 0).astype(BF)
        o_lat[j] = rows[432:504].astype(BF)
        o_cor[j] = rows[504:576].astype(BF)


def spread_kernel(parts, b_half, out, held, sems):
    for j in range(8):
        rows = slice(j * 32, (j + 1) * 32)
        held[rows, :] = parts[j, :, 0:256]
        b_half[rows, :] = parts[j, :, 256:384]
    copies = []
    for k in range(4):
        sent(copies, held, out.at[k], sems.at[k])
    finish(copies)


def gain_kernel(info, mine, w_qkv, out):
    rows = mine[...].astype(F32)
    w0, w1, w2 = [w_qkv[j].astype(F32) for j in range(3)]
    total = jnp.where(info[1] == 0, rows[:512] * w0 + rows[512:] * w1, rows[:512] * w2)
    total = total[:, 0:128] + total[:, 128:256]
    high = total.astype(BF)
    low = (total - high.astype(F32)).astype(BF)
    ones = jnp.ones((8, 128), BF)
    out[...] = dot(ones, high, NT) + dot(ones, low, NT)


def gain_sum_kernel(mine, other, mine_tp, other_tp, gain, out):
    total = (mine[0:1, :] + other[0:1, :]) + (mine_tp[0:1, :] + other_tp[0:1, :])
    out[...] = total / gain[...]


def bias_out_kernel(info, mine, other, grad_bias, token, rows, flat):
    token[...] = jnp.zeros_like(token)
    rows[0:256, :] = jnp.where(info[1] == 0, mine[...], other[...]).astype(F32)
    rows[256:512, :] = jnp.where(info[1] == 0, other[...], mine[...]).astype(F32)
    for s_t in range(2):
        for j in range(12):
            at = (s_t * 12 + j) * 138
            flat[:, at : at + 115] = rows[pl.ds(s_t * 16 + j, 16, stride=32), :][:, 0:115]
            last = rows[pl.ds(s_t * 16 + 12 + j // 3, 16, stride=32), :]
            flat[:, at + 115 : at + 138] = last[:, j % 3 * 23 : j % 3 * 23 + 23]
    grad_bias[...] = flat[...].reshape(grad_bias.shape)


def weights_kernel(info, mine, other, token, wqkv, wout, held, held_out, sems):
    token[...] = jnp.zeros_like(token)
    first = jnp.where(info[1] == 0, mine[...], other[...]).astype(F32)
    second = jnp.where(info[1] == 0, other[...], mine[...]).astype(F32)
    copies = []
    for k in range(6):
        rows = pl.ds(k % 2 * 256, 256)
        half = first if k < 4 else second
        held[k] = half[k % 4 * 256 : (k % 4 + 1) * 256]
        copies.append(pltpu.make_async_copy(held.at[k], wqkv.at[k // 2, rows], sems.at[k]))
        copies[-1].start()
    held_out[:, 0:256] = second[512:768]
    held_out[:, 256:512] = second[768:]
    for k in range(2):
        rows = pl.ds(k * 128, 128)
        copies.append(pltpu.make_async_copy(held_out.at[rows], wout.at[rows], sems.at[6 + k]))
        copies[-1].start()
    for copy in copies:
        copy.wait()


def bias_grad_kernel(info, ds, order, keep, send, part, entries, packed, *ends):
    entries[...] = jnp.zeros_like(entries)
    for p in range(12):
        for i in range(16):
            part[i * 12 : i * 12 + 12, :] = ds[i * WTOK + p * 12 : i * WTOK + p * 12 + 12, :]
        at = slice((11 - p) * 12, (11 - p) * 12 + WTOK)
        entries[:, at] = entries[:, at] + part[...]
    total = entries[...].astype(BF)
    packed[...] = jnp.zeros_like(packed)
    for s_u in range(2):
        rows = dot(total, order[s_u], NT)
        for half in range(32):
            at = half * 16 + s_u * 6
            packed[at : at + 6, 0:115] = rows[half * 6 : half * 6 + 6, 0:115]
        for q in range(3):
            last = ends[s_u * 3 + q]
            last[...] = jnp.zeros_like(last)
            last[:, q * 23 : q * 23 + 23] = rows[:, 115:138]
    for k in range(4):
        row = jnp.zeros((32, 128), F32)
        for q in range(3):
            s_u, r_t = (k * 3 + q) // 6, (k * 3 + q) % 6
            row = row + ends[s_u * 3 + q][pl.ds(r_t, 32, stride=6), :]
        packed[pl.ds(12 + k, 32, stride=16), :] = row
    mine, other = packed[0:256, :], packed[256:512, :]
    keep[...] = jnp.where(info[1] == 0, mine, other).astype(BF)
    send[...] = jnp.where(info[1] == 0, other, mine).astype(BF)


def final_kernel(latent, cot, gain, own, lon, lat, cor, token, output, grad, held, sems):
    token[...] = jnp.zeros_like(token)
    copies = []
    for k in (1, 3, 0, 2):
        ref = (own, lon, lat, cor)[k]
        out_terms, hid_terms = ref[0].astype(F32), ref[1].astype(F32)
        start = 0
        for by_lon, by_lat in PLACES[k]:
            tile = latent[by_lon, by_lat]
            values = flat(tile).astype(F32)
            rows = slice(start, start + values.shape[0])
            start += values.shape[0]
            held[0, by_lon, by_lat] = (values + out_terms[rows]).astype(BF).reshape(tile.shape)
            shifted = values - jnp.mean(values, -1, keepdims=True)
            inv_std = lax.rsqrt(jnp.mean(shifted * shifted, -1, keepdims=True) + 1e-05)
            normed = shifted * inv_std
            scaled = hid_terms[rows] * gain[...]
            inner = scaled - jnp.mean(scaled, -1, keepdims=True) - normed * jnp.mean(scaled * normed, -1, keepdims=True)
            above = flat(cot[by_lon, by_lat]).astype(F32)
            held[1, by_lon, by_lat] = (above + inv_std * inner).astype(BF).reshape(tile.shape)
        if k >= 2:
            for j, ref in enumerate((output, grad)):
                for first in (0, 3):
                    rows = pl.ds(first + (6 if k == 2 else 0), 3)
                    sent(copies, held.at[j, rows], ref.at[rows], sems.at[len(copies)])
    finish(copies)


def moved(value, by_lon, by_lat):
    n_lon, n_lat = lax.axis_size("lon"), lax.axis_size("lat")
    flip = 1 if by_lat else 0
    pairs = [
        ((i * n_lat + j) * 2 + k, ((i + by_lon) % n_lon * n_lat + (j + by_lat) % n_lat) * 2 + (k ^ flip))
        for i in range(n_lon)
        for j in range(n_lat)
        for k in range(2)
    ]
    return lax.ppermute(value, ("lon", "lat", "tp"), pairs)


def swapped(value, lon_bits, lat_bits):
    n_lon, n_lat = lax.axis_size("lon"), lax.axis_size("lat")
    pairs = [(i * n_lat + j, (i ^ lon_bits) * n_lat + (j ^ lat_bits)) for i in range(n_lon) for j in range(n_lat)]
    return lax.ppermute(value, ("lon", "lat"), pairs)


def across_y(value):
    n_lat = lax.axis_size("lat")
    groups = [list(range(x, n_lat, 2)) for x in range(2)]
    return lax.all_to_all(value, "lat", 0, 0, axis_index_groups=groups)


def across_z(value):
    n_lon = lax.axis_size("lon")
    groups = [list(range(core, n_lon, 2)) for core in range(2)]
    return lax.all_to_all(value, "lon", 0, 0, axis_index_groups=groups)


def other_group(value):
    return lax.ppermute(value, "tp", [(0, 1), (1, 0)])


def other_group_and_core(value):
    n_lon = lax.axis_size("lon")
    return lax.ppermute(value, ("lon", "tp"), [(i * 2 + j, (i ^ 1) * 2 + (j ^ 1)) for i in range(n_lon) for j in range(2)])


def on_device(latent, cotangent, ln_gain, w_qkv, w_out, bias_table):
    place, back = jnp.asarray(TO_WINDOW, BF), jnp.asarray(TO_WINDOW.transpose(0, 2, 1), BF)
    order = jnp.asarray(ORDER, BF)
    order_halves = jnp.asarray(ORDER.reshape(2, 138, 276), BF)
    i_lon, i_lat = lax.axis_index("lon"), lax.axis_index("lat")
    last = (i_lat == lax.axis_size("lat") - 1).astype(jnp.int32)
    core = i_lon % 2
    info = jnp.stack([last, core]).astype(jnp.int32)
    gain = ln_gain.reshape(1, 512)

    part = lambda n: ((2, n, 512), BF)
    halos = [part(216), part(72), part(72)]
    s_lon, s_lat, s_cor = call(
        halo_kernel,
        [],
        [],
        [pltpu.VMEM((2,) + latent.shape, BF)]
        + [pltpu.VMEM(shape, BF) for shape, _ in halos]
        + [pltpu.SemaphoreType.DMA((8,)), pltpu.SemaphoreType.DMA((6,))],
        smem=0,
        mib=60,
        hbm=[latent, cotangent],
        hbm_outs=halos,
    )
    in_lon, in_lat, in_cor = moved(s_lon, -1, 0), moved(s_lat, 0, -1), moved(s_cor, -1, -1)

    bias, w_copy = call(
        bias_kernel,
        [((16 * WTOK, WTOK), F32), (w_out.shape, BF)],
        [info, bias_table, order, w_out],
        [pltpu.VMEM((192, 276), F32)] * 2 + [pltpu.VMEM((192, 128), F32)] * 3,
        us=2,
    )
    w_other = other_group(w_copy)

    keep, send, ds, att, gq, gk, gv = call(
        main_kernel,
        [((1024, 256), F32), ((1024, 256), BF), ((16 * WTOK, WTOK), F32)] + [((576, 256), BF)] * 4,
        [info, latent, cotangent, in_lon, in_lat, in_cor, place, gain, w_qkv, w_out, bias],
        [pltpu.VMEM((576, 512), F32)],
        us=9,
        mib=32,
    )
    recv = swapped(send, 1, 0)
    (terms,) = call(terms_kernel, [((576, 768), BF)], [att, gq, gk, gv, w_qkv, back], smem=0, after=[w_other], us=2)
    others = other_group(terms)
    own, s_lon, s_lat, s_cor, paired = call(
        pair_kernel, [part(216)] + halos + [TOKEN], [terms, others, w_out, w_other], smem=0, us=30
    )

    (total,) = call(
        core_sum_kernel,
        [],
        [keep, recv],
        [pltpu.VMEM((4, 256, 256), BF), pltpu.SemaphoreType.DMA((4,))],
        smem=0,
        after=[terms],
        us=0.5,
        hbm_outs=[((4, 256, 256), BF)],
    )
    parts = across_y(total)
    b_keep, b_send = call(
        bias_grad_kernel,
        [((256, 128), BF)] * 2,
        [info, ds, order_halves],
        [pltpu.VMEM((192, WTOK), F32), pltpu.VMEM((192, 276), F32), pltpu.VMEM((512, 128), F32)]
        + [pltpu.VMEM((192, 128), F32)] * 6,
        us=2.5,
    )
    b_recv = swapped(b_send, 1, 0)
    (message,) = call(
        y_sum_kernel,
        [],
        [parts, b_keep, b_recv],
        [pltpu.VMEM((8, 32, 384), BF), pltpu.SemaphoreType.DMA((8,))],
        smem=0,
        hbm_outs=[((8, 32, 384), BF)],
    )
    x_mine, b_sum = call(
        z_sum_kernel, [((32, 256), BF), ((32, 128), BF)], [across_z(message)], smem=0, after=[paired], us=1
    )
    (copies,) = call(
        x_sum_kernel,
        [],
        [x_mine, swapped(x_mine, 0, 1), b_sum],
        [pltpu.VMEM((32, 384), BF), pltpu.SemaphoreType.DMA((8,))],
        smem=0,
        hbm_outs=[((8, 32, 384), BF)],
    )
    r_lon, r_lat, r_cor = moved(s_lon, 1, 0), moved(s_lat, 0, 1), moved(s_cor, 1, 1)

    placed, output, grad_latent = call(
        final_kernel,
        [TOKEN],
        [latent, cotangent, gain, own, r_lon, r_lat, r_cor],
        [pltpu.VMEM((2,) + latent.shape, BF), pltpu.SemaphoreType.DMA((8,))],
        hbm_outs=[(latent.shape, BF)] * 2,
        smem=0,
        us=30,
    )

    b_half, copies = call(
        spread_kernel,
        [((256, 128), BF)],
        [across_z(copies)],
        [pltpu.VMEM((256, 256), BF), pltpu.SemaphoreType.DMA((4,))],
        smem=0,
        hbm_outs=[((4, 256, 256), BF)],
    )
    mine = across_y(copies).reshape(1024, 256)
    b_other = swapped(b_half, 1, 0)
    grad_bias, done = call(
        bias_out_kernel,
        [(bias_table.shape, F32), TOKEN],
        [info, b_half, b_other],
        [pltpu.VMEM((512, 128), F32), pltpu.VMEM((16, 3312), F32)],
        after=[placed],
    )

    (g_mine,) = call(
        gain_kernel, [((8, 512), F32)], [info, mine, w_qkv], after=[done], us=30
    )
    g_parts = [g_mine, swapped(g_mine, 1, 0), other_group(g_mine), other_group_and_core(g_mine)]
    done, grad_wqkv, grad_wout = call(
        weights_kernel,
        [TOKEN],
        [info, mine, swapped(mine, 1, 0)],
        [pltpu.VMEM((6, 256, 256), F32), pltpu.VMEM((256, 512), F32), pltpu.SemaphoreType.DMA((8,))],
        hbm_outs=[((3, 512, 256), F32), ((256, 512), F32)],
        us=2,
    )
    (grad_gain,) = call(
        gain_sum_kernel, [((1, 512), F32)], [*g_parts, gain], smem=0, after=[done]
    )
    grad_gain = grad_gain.reshape(512)
    return output, grad_latent, grad_gain, grad_wqkv, grad_wout, grad_bias


def solution(mesh):
    specs = (
        P("lon", "lat", None, None),
        P("lon", "lat", None, None),
        P(),
        P(None, None, "tp"),
        P("tp", None),
        P("lat", None, "tp", None),
    )
    return jax.shard_map(on_device, mesh=mesh, in_specs=specs, out_specs=specs, check_vma=False)
```

```python
import functools

import jax
import jax.numpy as jnp
import numpy as np
from jax import lax
from jax.experimental import pallas as pl
from jax.experimental.pallas import tpu as pltpu
from jax.sharding import PartitionSpec as P

BF = jnp.bfloat16
F32 = jnp.float32
WTOK = 144
OFFS = 23
NT = (((1,), (1,)), ((), ()))
TN = (((0,), (0,)), ((), ()))


def section_row(lon, lat, lev):
    if lat < 6:
        return (lon >= 6) * 144 + (lon % 6 * 6 + lat) * 4 + lev
    return (lat >= 9) * 144 + (lon >= 6) * 72 + (lon % 6 * 3 + lat % 3) * 4 + lev


def placement():
    place = np.zeros((2, 288, 288), np.float32)
    for a in range(2):
        for b in range(2):
            for p in range(12):
                for s in range(2):
                    for r in range(6):
                        row = b * WTOK + p * 12 + s * 6 + r
                        place[a, row, section_row(p, a * 6 + r, (b * 2 + s + 1) % 4)] = 1
    return place


def offset_order():
    order = np.zeros((276, 276), np.float32)
    for rs in range(12):
        for k in range(OFFS):
            order[rs * OFFS + k, k * 12 + rs] = 1
    return order


TO_WINDOW = placement()
ORDER = offset_order()


def dot(a, b, dims=(((1,), (0,)), ((), ()))):
    return lax.dot_general(a, b, dims, preferred_element_type=F32)


def call(body, outs, args, scratch=(), smem=1, after=(), us=1, mib=16, hbm=(), hbm_outs=()):
    vmem, far = pl.BlockSpec(memory_space=pltpu.VMEM), pl.BlockSpec(memory_space=pltpu.HBM)
    n = len(args)
    m = n + len(hbm)

    def kernel(*refs):
        body(*refs[:m], *refs[m + len(after) :])

    return pl.pallas_call(
        kernel,
        out_shape=[jax.ShapeDtypeStruct(s, t) for s, t in [*outs, *hbm_outs]],
        in_specs=[pl.BlockSpec(memory_space=pltpu.SMEM)] * smem
        + [vmem] * (n - smem)
        + [far] * len(hbm)
        + [pl.BlockSpec(memory_space=pl.ANY)] * len(after),
        out_specs=[vmem] * len(outs) + [far] * len(hbm_outs),
        scratch_shapes=list(scratch),
        compiler_params=pltpu.CompilerParams(vmem_limit_bytes=mib * 1024 * 1024),
        cost_estimate=pl.CostEstimate(flops=int(us * 1e9), bytes_accessed=0, transcendentals=0),
    )(*args, *hbm, *after)


TOKEN = ((8, 128), F32)


LOW_LON, LOW_LAT, HIGH_LON, MID_LAT, HIGH_LAT = slice(0, 6), slice(0, 3), slice(6, 12), slice(3, 9), slice(9, 12)
PLACES = (
    ((HIGH_LON, MID_LAT), (HIGH_LON, HIGH_LAT)),
    ((LOW_LON, MID_LAT), (LOW_LON, HIGH_LAT)),
    ((HIGH_LON, LOW_LAT),),
    ((LOW_LON, LOW_LAT),),
)


def flat(tile):
    return tile.reshape(-1, tile.shape[-1])


def sent(copies, source, target, sem):
    copies.append(pltpu.make_async_copy(source, target, sem))
    copies[-1].start()


def finish(copies):
    for copy in copies:
        copy.wait()


def halo_kernel(which, latent, cot, *refs):
    n = len(which)
    outs, tiles, helds, in_sems, out_sems = refs[:n], refs[n], refs[n + 1 : 2 * n + 1], refs[-2], refs[-1]
    lons = (0, 3, 6, 9) if 2 in which else (0, 3)
    arrived, copies = [], []
    for first in lons:
        for j, grid in enumerate((latent, cot)):
            rows = pl.ds(first, 3)
            if 2 in which:
                part = (rows, pl.ds(0, 3))
                sent(arrived, grid.at[part], tiles.at[(j,) + part], in_sems.at[len(arrived)])
            else:
                sent(arrived, grid.at[rows], tiles.at[j, rows], in_sems.at[len(arrived)])
    finish(arrived)
    for k, held, ref in zip(which, helds, outs):
        for j in range(2):
            held[j] = jnp.concatenate([flat(tiles[j, lon, lat]) for lon, lat in PLACES[k]], 0)
            sent(copies, held.at[j], ref.at[j], out_sems.at[len(copies)])
    finish(copies)


def bias_kernel(info, table, order, w_out, bias, w_copy, raw, entries, t0, t1, t2):
    w_copy[...] = w_out[...]
    flat = table[...].reshape(16, 3312)
    for s_t in range(2):
        for s_u in range(2):
            for r_t in range(6):
                at = ((s_t * 2 + s_u) * 6 + r_t) * 138
                row = (s_t * 6 + r_t) * 16
                raw[row : row + 16, s_u * 138 : s_u * 138 + 138] = flat[:, at : at + 138]
    full = raw[...]
    high = full.astype(BF)
    rest = full - high.astype(F32)
    mid = rest.astype(BF)
    low = (rest - mid.astype(F32)).astype(BF)
    wide = dot(low, order[...]) + dot(mid, order[...]) + dot(high, order[...])
    t0[...] = wide[:, 0:128]
    t1[...] = wide[:, 128:256]
    t2[:, 0:20] = wide[:, 256:276]
    for i in range(16):
        at, rows = pl.ds(i, 12, stride=16), slice(i * 12, i * 12 + 12)
        entries[rows, 0:128] = t0[at, :]
        entries[rows, 128:256] = t1[at, :]
        entries[rows, 256:276] = t2[at, :][:, 0:20]
    row = lax.broadcasted_iota(jnp.int32, (192, WTOK), 0)
    col = lax.broadcasted_iota(jnp.int32, (192, WTOK), 1)
    rs_t, rs_u, which = row % 12, col % 12, row // 12
    s_t, s_u = (rs_t >= 6).astype(jnp.int32), (rs_u >= 6).astype(jnp.int32)
    edge_t = (rs_t - s_t * 6 >= 3).astype(jnp.int32)
    edge_u = (rs_u - s_u * 6 >= 3).astype(jnp.int32)
    last_lat = (which >= 8).astype(jnp.int32) * info[0]
    last_lev = ((which % 8) >= 4).astype(jnp.int32)
    barred = (last_lat * (edge_t - edge_u) != 0) | (last_lev * (s_t - s_u) != 0)
    for p in range(12):
        at = jnp.where(barred, -jnp.inf, entries[:, (11 - p) * 12 : (11 - p) * 12 + WTOK])
        for i in range(16):
            bias[i * WTOK + p * 12 : i * WTOK + p * 12 + 12, :] = at[i * 12 : i * 12 + 12]


def main_kernel(info, latent, cotangent, lon, lat, cor, place, gain, w_qkv, w_out, bias,
                keep, send, o_ds, att_s, gq_s, gk_s, gv_s, joined):
    def gathered(which):
        grid = (latent, cotangent)[which]
        beside = lon[which].astype(F32)
        parts = (flat(grid[HIGH_LON, MID_LAT]), beside[0:144], flat(grid[HIGH_LON, HIGH_LAT]), beside[144:216])
        start = 0
        for rows in (*parts, lat[which], cor[which]):
            joined[start : start + rows.shape[0], :] = rows.astype(F32)
            start += rows.shape[0]
        rows = joined[...].astype(BF)
        return jnp.concatenate([dot(place[a], rows[a * 288 : (a + 1) * 288]) for a in range(2)], 0)

    values = gathered(0)
    cot = gathered(1).astype(BF)
    shifted = values - jnp.mean(values, -1, keepdims=True)
    normed = shifted * lax.rsqrt(jnp.mean(shifted * shifted, -1, keepdims=True) + 1e-05)
    hidden = (normed * gain[...]).astype(BF)
    q, k, v = [dot(hidden, w_qkv[j]).astype(BF) for j in range(3)]
    down = dot(cot, w_out[...], NT).astype(BF)
    head = lax.broadcasted_iota(jnp.int32, (WTOK, 256), 1) // 64

    def stacked(rows):
        return jnp.concatenate([jnp.where(head == h, rows, jnp.zeros_like(rows)) for h in range(4)], 0)

    def unstacked(rows):
        total = jnp.zeros((WTOK, 256), F32)
        for h in range(4):
            total = jnp.where(head == h, rows[h * WTOK : (h + 1) * WTOK], total)
        return total

    for w in range(4):
        rows = slice(w * WTOK, (w + 1) * WTOK)
        four = slice(w * 576, (w + 1) * 576)
        qs, ds_ = stacked(q[rows]), stacked(down[rows])
        scores = dot(qs, k[rows], NT) * 0.125 + bias[four, :]
        exps = jnp.exp(scores - jnp.max(scores, -1, keepdims=True))
        probs = exps / jnp.sum(exps, -1, keepdims=True)
        probs_low = probs.astype(BF)
        att_s[rows, :] = unstacked(dot(probs_low, v[rows])).astype(BF)
        dp = dot(ds_, v[rows], NT)
        gv_s[rows, :] = dot(probs_low, ds_, TN).astype(BF)
        grad = probs * (dp - jnp.sum(dp * probs, -1, keepdims=True))
        o_ds[four, :] = grad
        grad_low = grad.astype(BF)
        gq_s[rows, :] = unstacked(dot(grad_low, k[rows]) * 0.125).astype(BF)
        gk_s[rows, :] = (dot(grad_low, qs, TN) * 0.125).astype(BF)

    att, gq, gk, gv = att_s[...], gq_s[...], gk_s[...], gv_s[...]
    wo = dot(att, cot, TN)
    first = [dot(hidden, gq, TN), dot(hidden, gk, TN)]
    second = [dot(hidden, gv, TN), jnp.concatenate([wo[:, :256], wo[:, 256:]], 0)]
    core = info[1]
    for j in range(2):
        rows = slice(j * 512, (j + 1) * 512)
        keep[rows, :] = jnp.where(core == 0, first[j], second[j])
        send[rows, :] = jnp.where(core == 0, second[j], first[j]).astype(BF)

def terms_kernel(att, gq, gk, gv, w_qkv, back, terms):
    hid_part = dot(gq[...], w_qkv[0], NT) + dot(gk[...], w_qkv[1], NT) + dot(gv[...], w_qkv[2], NT)
    hid_part = hid_part.astype(BF)
    for a in range(2):
        rows = slice(a * 288, (a + 1) * 288)
        terms[rows, 0:256] = dot(back[a], att[rows, :]).astype(BF)
        terms[rows, 256:768] = dot(back[a], hid_part[rows]).astype(BF)


def core_sum_kernel(keep, recv, total, held, sems):
    copies = []
    for k in range(4):
        rows = slice(k * 256, (k + 1) * 256)
        held[k] = (keep[rows, :] + recv[rows, :].astype(F32)).astype(BF)
        sent(copies, held.at[k], total.at[k], sems.at[k])
    finish(copies)


def y_sum_kernel(parts, b_keep, b_recv, message, held, sems):
    copies = []
    for j in range(8):
        rows = slice(j * 32, (j + 1) * 32)
        total = parts[0, rows, :].astype(F32)
        for k in range(1, 4):
            total = total + parts[k, rows, :].astype(F32)
        held[j, :, 0:256] = total.astype(BF)
        held[j, :, 256:384] = (b_keep[rows, :].astype(F32) + b_recv[rows, :].astype(F32)).astype(BF)
        sent(copies, held.at[j], message.at[j], sems.at[j])
    finish(copies)


def z_sum_kernel(parts, mine, bias):
    total = parts[0].astype(F32)
    for j in range(1, 8):
        total = total + parts[j].astype(F32)
    mine[...] = total[:, 0:256].astype(BF)
    bias[...] = total[:, 256:384].astype(BF)


def x_sum_kernel(mine, recv, bias, out, held, sems):
    held[:, 0:256] = (mine[...].astype(F32) + recv[...].astype(F32)).astype(BF)
    held[:, 256:384] = bias[...]
    copies = []
    for j in range(8):
        sent(copies, held, out.at[j], sems.at[j])
    finish(copies)


def pair_kernel(terms, others, w_out, w_other, o_own, o_lon, o_lat, o_cor, token):
    token[...] = jnp.zeros_like(token)
    out = dot(terms[:, 0:256], w_out[...]).astype(BF).astype(F32)
    out = out + dot(others[:, 0:256], w_other[...]).astype(BF).astype(F32)
    hid = terms[:, 256:768].astype(F32) + others[:, 256:768].astype(F32)
    for j, rows in enumerate((out, hid)):
        o_own[j] = jnp.concatenate([rows[0:144], rows[288:360]], 0).astype(BF)
        o_lon[j] = jnp.concatenate([rows[144:288], rows[360:432]], 0).astype(BF)
        o_lat[j] = rows[432:504].astype(BF)
        o_cor[j] = rows[504:576].astype(BF)


def spread_kernel(parts, b_half, out, held, sems):
    for j in range(8):
        rows = slice(j * 32, (j + 1) * 32)
        held[rows, :] = parts[j, :, 0:256]
        b_half[rows, :] = parts[j, :, 256:384]
    copies = []
    for k in range(4):
        sent(copies, held, out.at[k], sems.at[k])
    finish(copies)


def gain_kernel(info, mine, w_qkv, out):
    rows = mine[...].astype(F32)
    w0, w1, w2 = [w_qkv[j].astype(F32) for j in range(3)]
    total = jnp.where(info[1] == 0, rows[:512] * w0 + rows[512:] * w1, rows[:512] * w2)
    total = total[:, 0:128] + total[:, 128:256]
    high = total.astype(BF)
    low = (total - high.astype(F32)).astype(BF)
    ones = jnp.ones((8, 128), BF)
    out[...] = dot(ones, high, NT) + dot(ones, low, NT)


def gain_sum_kernel(mine, other, mine_tp, other_tp, gain, out):
    total = (mine[0:1, :] + other[0:1, :]) + (mine_tp[0:1, :] + other_tp[0:1, :])
    out[...] = total / gain[...]


def bias_out_kernel(info, mine, other, grad_bias, token, rows, flat):
    token[...] = jnp.zeros_like(token)
    rows[0:256, :] = jnp.where(info[1] == 0, mine[...], other[...]).astype(F32)
    rows[256:512, :] = jnp.where(info[1] == 0, other[...], mine[...]).astype(F32)
    for s_t in range(2):
        for j in range(12):
            at = (s_t * 12 + j) * 138
            flat[:, at : at + 115] = rows[pl.ds(s_t * 16 + j, 16, stride=32), :][:, 0:115]
            last = rows[pl.ds(s_t * 16 + 12 + j // 3, 16, stride=32), :]
            flat[:, at + 115 : at + 138] = last[:, j % 3 * 23 : j % 3 * 23 + 23]
    grad_bias[...] = flat[...].reshape(grad_bias.shape)


def weights_kernel(info, mine, other, token, wqkv, wout, held, held_out, sems):
    token[...] = jnp.zeros_like(token)
    first = jnp.where(info[1] == 0, mine[...], other[...]).astype(F32)
    second = jnp.where(info[1] == 0, other[...], mine[...]).astype(F32)
    copies = []
    for k in range(6):
        rows = pl.ds(k % 2 * 256, 256)
        half = first if k < 4 else second
        held[k] = half[k % 4 * 256 : (k % 4 + 1) * 256]
        copies.append(pltpu.make_async_copy(held.at[k], wqkv.at[k // 2, rows], sems.at[k]))
        copies[-1].start()
    held_out[:, 0:256] = second[512:768]
    held_out[:, 256:512] = second[768:]
    for k in range(2):
        rows = pl.ds(k * 128, 128)
        copies.append(pltpu.make_async_copy(held_out.at[rows], wout.at[rows], sems.at[6 + k]))
        copies[-1].start()
    for copy in copies:
        copy.wait()


def bias_grad_kernel(info, ds, order, keep, send, part, entries, packed, *ends):
    entries[...] = jnp.zeros_like(entries)
    for p in range(12):
        for i in range(16):
            part[i * 12 : i * 12 + 12, :] = ds[i * WTOK + p * 12 : i * WTOK + p * 12 + 12, :]
        at = slice((11 - p) * 12, (11 - p) * 12 + WTOK)
        entries[:, at] = entries[:, at] + part[...]
    total = entries[...].astype(BF)
    packed[...] = jnp.zeros_like(packed)
    for s_u in range(2):
        rows = dot(total, order[s_u], NT)
        for half in range(32):
            at = half * 16 + s_u * 6
            packed[at : at + 6, 0:115] = rows[half * 6 : half * 6 + 6, 0:115]
        for q in range(3):
            last = ends[s_u * 3 + q]
            last[...] = jnp.zeros_like(last)
            last[:, q * 23 : q * 23 + 23] = rows[:, 115:138]
    for k in range(4):
        row = jnp.zeros((32, 128), F32)
        for q in range(3):
            s_u, r_t = (k * 3 + q) // 6, (k * 3 + q) % 6
            row = row + ends[s_u * 3 + q][pl.ds(r_t, 32, stride=6), :]
        packed[pl.ds(12 + k, 32, stride=16), :] = row
    mine, other = packed[0:256, :], packed[256:512, :]
    keep[...] = jnp.where(info[1] == 0, mine, other).astype(BF)
    send[...] = jnp.where(info[1] == 0, other, mine).astype(BF)


def final_kernel(latent, cot, gain, own, lon, lat, cor, token, output, grad, held, sems):
    token[...] = jnp.zeros_like(token)
    copies = []
    for k in (1, 3, 0, 2):
        ref = (own, lon, lat, cor)[k]
        out_terms, hid_terms = ref[0].astype(F32), ref[1].astype(F32)
        start = 0
        for by_lon, by_lat in PLACES[k]:
            tile = latent[by_lon, by_lat]
            values = flat(tile).astype(F32)
            rows = slice(start, start + values.shape[0])
            start += values.shape[0]
            held[0, by_lon, by_lat] = (values + out_terms[rows]).astype(BF).reshape(tile.shape)
            shifted = values - jnp.mean(values, -1, keepdims=True)
            inv_std = lax.rsqrt(jnp.mean(shifted * shifted, -1, keepdims=True) + 1e-05)
            normed = shifted * inv_std
            scaled = hid_terms[rows] * gain[...]
            inner = scaled - jnp.mean(scaled, -1, keepdims=True) - normed * jnp.mean(scaled * normed, -1, keepdims=True)
            above = flat(cot[by_lon, by_lat]).astype(F32)
            held[1, by_lon, by_lat] = (above + inv_std * inner).astype(BF).reshape(tile.shape)
        if k >= 2:
            for j, ref in enumerate((output, grad)):
                for first in (0, 3):
                    rows = pl.ds(first + (6 if k == 2 else 0), 3)
                    sent(copies, held.at[j, rows], ref.at[rows], sems.at[len(copies)])
    finish(copies)


def moved(value, by_lon, by_lat):
    n_lon, n_lat = lax.axis_size("lon"), lax.axis_size("lat")
    flip = 1 if by_lat else 0
    pairs = [
        ((i * n_lat + j) * 2 + k, ((i + by_lon) % n_lon * n_lat + (j + by_lat) % n_lat) * 2 + (k ^ flip))
        for i in range(n_lon)
        for j in range(n_lat)
        for k in range(2)
    ]
    return lax.ppermute(value, ("lon", "lat", "tp"), pairs)


def swapped(value, lon_bits, lat_bits):
    n_lon, n_lat = lax.axis_size("lon"), lax.axis_size("lat")
    pairs = [(i * n_lat + j, (i ^ lon_bits) * n_lat + (j ^ lat_bits)) for i in range(n_lon) for j in range(n_lat)]
    return lax.ppermute(value, ("lon", "lat"), pairs)


def across_y(value):
    n_lat = lax.axis_size("lat")
    groups = [list(range(x, n_lat, 2)) for x in range(2)]
    return lax.all_to_all(value, "lat", 0, 0, axis_index_groups=groups)


def across_z(value):
    n_lon = lax.axis_size("lon")
    groups = [list(range(core, n_lon, 2)) for core in range(2)]
    return lax.all_to_all(value, "lon", 0, 0, axis_index_groups=groups)


def other_group(value):
    return lax.ppermute(value, "tp", [(0, 1), (1, 0)])


def other_group_and_core(value):
    n_lon = lax.axis_size("lon")
    return lax.ppermute(value, ("lon", "tp"), [(i * 2 + j, (i ^ 1) * 2 + (j ^ 1)) for i in range(n_lon) for j in range(2)])


def on_device(latent, cotangent, ln_gain, w_qkv, w_out, bias_table):
    place, back = jnp.asarray(TO_WINDOW, BF), jnp.asarray(TO_WINDOW.transpose(0, 2, 1), BF)
    order = jnp.asarray(ORDER, BF)
    order_halves = jnp.asarray(ORDER.reshape(2, 138, 276), BF)
    i_lon, i_lat = lax.axis_index("lon"), lax.axis_index("lat")
    last = (i_lat == lax.axis_size("lat") - 1).astype(jnp.int32)
    core = i_lon % 2
    info = jnp.stack([last, core]).astype(jnp.int32)
    gain = ln_gain.reshape(1, 512)

    part = lambda n: ((2, n, 512), BF)
    halos = [part(216), part(72), part(72)]
    def halo(which, after):
        shapes = [halos[k - 1] for k in which]
        return call(
            functools.partial(halo_kernel, which),
            [],
            [],
            [pltpu.VMEM((2,) + latent.shape, BF)]
            + [pltpu.VMEM(shape, BF) for shape, _ in shapes]
            + [pltpu.SemaphoreType.DMA((8,)), pltpu.SemaphoreType.DMA((4,))],
            smem=0,
            mib=60,
            hbm=[latent, cotangent],
            hbm_outs=shapes,
            after=after,
        )

    s_lat, s_cor = halo((2, 3), [])
    (s_lon,) = halo((1,), [s_lat])
    in_lon, in_lat, in_cor = moved(s_lon, -1, 0), moved(s_lat, 0, -1), moved(s_cor, -1, -1)

    bias, w_copy = call(
        bias_kernel,
        [((16 * WTOK, WTOK), F32), (w_out.shape, BF)],
        [info, bias_table, order, w_out],
        [pltpu.VMEM((192, 276), F32)] * 2 + [pltpu.VMEM((192, 128), F32)] * 3,
        us=30,
    )
    w_other = other_group(w_copy)

    keep, send, ds, att, gq, gk, gv = call(
        main_kernel,
        [((1024, 256), F32), ((1024, 256), BF), ((16 * WTOK, WTOK), F32)] + [((576, 256), BF)] * 4,
        [info, latent, cotangent, in_lon, in_lat, in_cor, place, gain, w_qkv, w_out, bias],
        [pltpu.VMEM((576, 512), F32)],
        us=9,
        mib=32,
    )
    recv = swapped(send, 1, 0)
    (terms,) = call(terms_kernel, [((576, 768), BF)], [att, gq, gk, gv, w_qkv, back], smem=0, after=[w_other], us=2)
    others = other_group(terms)
    own, s_lon, s_lat, s_cor, paired = call(
        pair_kernel, [part(216)] + halos + [TOKEN], [terms, others, w_out, w_other], smem=0, us=30
    )

    (total,) = call(
        core_sum_kernel,
        [],
        [keep, recv],
        [pltpu.VMEM((4, 256, 256), BF), pltpu.SemaphoreType.DMA((4,))],
        smem=0,
        after=[terms],
        us=0.5,
        hbm_outs=[((4, 256, 256), BF)],
    )
    parts = across_y(total)
    b_keep, b_send = call(
        bias_grad_kernel,
        [((256, 128), BF)] * 2,
        [info, ds, order_halves],
        [pltpu.VMEM((192, WTOK), F32), pltpu.VMEM((192, 276), F32), pltpu.VMEM((512, 128), F32)]
        + [pltpu.VMEM((192, 128), F32)] * 6,
        us=2.5,
    )
    b_recv = swapped(b_send, 1, 0)
    (message,) = call(
        y_sum_kernel,
        [],
        [parts, b_keep, b_recv],
        [pltpu.VMEM((8, 32, 384), BF), pltpu.SemaphoreType.DMA((8,))],
        smem=0,
        hbm_outs=[((8, 32, 384), BF)],
    )
    x_mine, b_sum = call(
        z_sum_kernel, [((32, 256), BF), ((32, 128), BF)], [across_z(message)], smem=0, after=[paired], us=1
    )
    (copies,) = call(
        x_sum_kernel,
        [],
        [x_mine, swapped(x_mine, 0, 1), b_sum],
        [pltpu.VMEM((32, 384), BF), pltpu.SemaphoreType.DMA((8,))],
        smem=0,
        hbm_outs=[((8, 32, 384), BF)],
    )
    r_lon, r_lat, r_cor = moved(s_lon, 1, 0), moved(s_lat, 0, 1), moved(s_cor, 1, 1)

    placed, output, grad_latent = call(
        final_kernel,
        [TOKEN],
        [latent, cotangent, gain, own, r_lon, r_lat, r_cor],
        [pltpu.VMEM((2,) + latent.shape, BF), pltpu.SemaphoreType.DMA((8,))],
        hbm_outs=[(latent.shape, BF)] * 2,
        smem=0,
        us=30,
    )

    b_half, copies = call(
        spread_kernel,
        [((256, 128), BF)],
        [across_z(copies)],
        [pltpu.VMEM((256, 256), BF), pltpu.SemaphoreType.DMA((4,))],
        smem=0,
        hbm_outs=[((4, 256, 256), BF)],
    )
    mine = across_y(copies).reshape(1024, 256)
    b_other = swapped(b_half, 1, 0)
    grad_bias, done = call(
        bias_out_kernel,
        [(bias_table.shape, F32), TOKEN],
        [info, b_half, b_other],
        [pltpu.VMEM((512, 128), F32), pltpu.VMEM((16, 3312), F32)],
        after=[placed],
    )

    (g_mine,) = call(
        gain_kernel, [((8, 512), F32)], [info, mine, w_qkv], after=[done], us=30
    )
    g_parts = [g_mine, swapped(g_mine, 1, 0), other_group(g_mine), other_group_and_core(g_mine)]
    done, grad_wqkv, grad_wout = call(
        weights_kernel,
        [TOKEN],
        [info, mine, swapped(mine, 1, 0)],
        [pltpu.VMEM((6, 256, 256), F32), pltpu.VMEM((256, 512), F32), pltpu.SemaphoreType.DMA((8,))],
        hbm_outs=[((3, 512, 256), F32), ((256, 512), F32)],
        us=2,
    )
    (grad_gain,) = call(
        gain_sum_kernel, [((1, 512), F32)], [*g_parts, gain], smem=0, after=[done]
    )
    grad_gain = grad_gain.reshape(512)
    return output, grad_latent, grad_gain, grad_wqkv, grad_wout, grad_bias


def solution(mesh):
    specs = (
        P("lon", "lat", None, None),
        P("lon", "lat", None, None),
        P(),
        P(None, None, "tp"),
        P("tp", None),
        P("lat", None, "tp", None),
    )
    return jax.shard_map(on_device, mesh=mesh, in_specs=specs, out_specs=specs, check_vma=False)
```

```python
import jax
import jax.numpy as jnp
import numpy as np
from jax import lax
from jax.experimental import pallas as pl
from jax.experimental.pallas import tpu as pltpu
from jax.sharding import PartitionSpec as P

BF = jnp.bfloat16
F32 = jnp.float32
WTOK = 144
OFFS = 23
NT = (((1,), (1,)), ((), ()))
TN = (((0,), (0,)), ((), ()))


def section_row(lon, lat, lev):
    if lat < 6:
        return (lon >= 6) * 144 + (lon % 6 * 6 + lat) * 4 + lev
    return (lat >= 9) * 144 + (lon >= 6) * 72 + (lon % 6 * 3 + lat % 3) * 4 + lev


def placement():
    place = np.zeros((2, 288, 288), np.float32)
    for a in range(2):
        for b in range(2):
            for p in range(12):
                for s in range(2):
                    for r in range(6):
                        row = b * WTOK + p * 12 + s * 6 + r
                        place[a, row, section_row(p, a * 6 + r, (b * 2 + s + 1) % 4)] = 1
    return place


def offset_order():
    order = np.zeros((276, 276), np.float32)
    for rs in range(12):
        for k in range(OFFS):
            order[rs * OFFS + k, k * 12 + rs] = 1
    return order


TO_WINDOW = placement()
ORDER = offset_order()


def dot(a, b, dims=(((1,), (0,)), ((), ()))):
    return lax.dot_general(a, b, dims, preferred_element_type=F32)


def call(body, outs, args, scratch=(), smem=1, after=(), us=1, mib=16, hbm=(), hbm_outs=()):
    vmem, far = pl.BlockSpec(memory_space=pltpu.VMEM), pl.BlockSpec(memory_space=pltpu.HBM)
    n = len(args)
    m = n + len(hbm)

    def kernel(*refs):
        body(*refs[:m], *refs[m + len(after) :])

    return pl.pallas_call(
        kernel,
        out_shape=[jax.ShapeDtypeStruct(s, t) for s, t in [*outs, *hbm_outs]],
        in_specs=[pl.BlockSpec(memory_space=pltpu.SMEM)] * smem
        + [vmem] * (n - smem)
        + [far] * len(hbm)
        + [pl.BlockSpec(memory_space=pl.ANY)] * len(after),
        out_specs=[vmem] * len(outs) + [far] * len(hbm_outs),
        scratch_shapes=list(scratch),
        compiler_params=pltpu.CompilerParams(vmem_limit_bytes=mib * 1024 * 1024),
        cost_estimate=pl.CostEstimate(flops=int(us * 1e9), bytes_accessed=0, transcendentals=0),
    )(*args, *hbm, *after)


TOKEN = ((8, 128), F32)


LOW_LON, LOW_LAT, HIGH_LON, MID_LAT, HIGH_LAT = slice(0, 6), slice(0, 3), slice(6, 12), slice(3, 9), slice(9, 12)
PLACES = (
    ((HIGH_LON, MID_LAT), (HIGH_LON, HIGH_LAT)),
    ((LOW_LON, MID_LAT), (LOW_LON, HIGH_LAT)),
    ((HIGH_LON, LOW_LAT),),
    ((LOW_LON, LOW_LAT),),
)


def flat(tile):
    return tile.reshape(-1, tile.shape[-1])


def sent(copies, source, target, sem):
    copies.append(pltpu.make_async_copy(source, target, sem))
    copies[-1].start()


def finish(copies):
    for copy in copies:
        copy.wait()


def halo_kernel(latent, cot, o_lon, o_lat, o_cor, tiles, h_lon, h_lat, h_cor, in_sems, out_sems):
    arrived, copies = [], []
    for first in (0, 3, 6, 9):
        for j, grid in enumerate((latent, cot)):
            rows = pl.ds(first, 3)
            sent(arrived, grid.at[rows], tiles.at[j, rows], in_sems.at[len(arrived)])
    finish(arrived[:4])
    for places, held, ref in ((PLACES[1], h_lon, o_lon), (PLACES[3], h_cor, o_cor), (PLACES[2], h_lat, o_lat)):
        if held is h_lat:
            finish(arrived[4:])
        for j in range(2):
            held[j] = jnp.concatenate([flat(tiles[j, lon, lat]) for lon, lat in places], 0)
            sent(copies, held.at[j], ref.at[j], out_sems.at[len(copies)])
    finish(copies)


def bias_kernel(info, table, order, w_out, bias, w_copy, raw, entries, t0, t1, t2):
    w_copy[...] = w_out[...]
    flat = table[...].reshape(16, 3312)
    for s_t in range(2):
        for s_u in range(2):
            for r_t in range(6):
                at = ((s_t * 2 + s_u) * 6 + r_t) * 138
                row = (s_t * 6 + r_t) * 16
                raw[row : row + 16, s_u * 138 : s_u * 138 + 138] = flat[:, at : at + 138]
    full = raw[...]
    high = full.astype(BF)
    rest = full - high.astype(F32)
    mid = rest.astype(BF)
    low = (rest - mid.astype(F32)).astype(BF)
    wide = dot(low, order[...]) + dot(mid, order[...]) + dot(high, order[...])
    t0[...] = wide[:, 0:128]
    t1[...] = wide[:, 128:256]
    t2[:, 0:20] = wide[:, 256:276]
    for i in range(16):
        at, rows = pl.ds(i, 12, stride=16), slice(i * 12, i * 12 + 12)
        entries[rows, 0:128] = t0[at, :]
        entries[rows, 128:256] = t1[at, :]
        entries[rows, 256:276] = t2[at, :][:, 0:20]
    row = lax.broadcasted_iota(jnp.int32, (192, WTOK), 0)
    col = lax.broadcasted_iota(jnp.int32, (192, WTOK), 1)
    rs_t, rs_u, which = row % 12, col % 12, row // 12
    s_t, s_u = (rs_t >= 6).astype(jnp.int32), (rs_u >= 6).astype(jnp.int32)
    edge_t = (rs_t - s_t * 6 >= 3).astype(jnp.int32)
    edge_u = (rs_u - s_u * 6 >= 3).astype(jnp.int32)
    last_lat = (which >= 8).astype(jnp.int32) * info[0]
    last_lev = ((which % 8) >= 4).astype(jnp.int32)
    barred = (last_lat * (edge_t - edge_u) != 0) | (last_lev * (s_t - s_u) != 0)
    for p in range(12):
        at = jnp.where(barred, -jnp.inf, entries[:, (11 - p) * 12 : (11 - p) * 12 + WTOK])
        for i in range(16):
            bias[i * WTOK + p * 12 : i * WTOK + p * 12 + 12, :] = at[i * 12 : i * 12 + 12]


def main_kernel(info, latent, cotangent, lon, lat, cor, place, gain, w_qkv, w_out, bias,
                keep, send, o_ds, att_s, gq_s, gk_s, gv_s, joined):
    def gathered(which):
        grid = (latent, cotangent)[which]
        beside = lon[which].astype(F32)
        parts = (flat(grid[HIGH_LON, MID_LAT]), beside[0:144], flat(grid[HIGH_LON, HIGH_LAT]), beside[144:216])
        start = 0
        for rows in (*parts, lat[which], cor[which]):
            joined[start : start + rows.shape[0], :] = rows.astype(F32)
            start += rows.shape[0]
        rows = joined[...].astype(BF)
        return jnp.concatenate([dot(place[a], rows[a * 288 : (a + 1) * 288]) for a in range(2)], 0)

    values = gathered(0)
    cot = gathered(1).astype(BF)
    shifted = values - jnp.mean(values, -1, keepdims=True)
    normed = shifted * lax.rsqrt(jnp.mean(shifted * shifted, -1, keepdims=True) + 1e-05)
    hidden = (normed * gain[...]).astype(BF)
    q, k, v = [dot(hidden, w_qkv[j]).astype(BF) for j in range(3)]
    down = dot(cot, w_out[...], NT).astype(BF)
    head = lax.broadcasted_iota(jnp.int32, (WTOK, 256), 1) // 64

    def stacked(rows):
        return jnp.concatenate([jnp.where(head == h, rows, jnp.zeros_like(rows)) for h in range(4)], 0)

    def unstacked(rows):
        total = jnp.zeros((WTOK, 256), F32)
        for h in range(4):
            total = jnp.where(head == h, rows[h * WTOK : (h + 1) * WTOK], total)
        return total

    for w in range(4):
        rows = slice(w * WTOK, (w + 1) * WTOK)
        four = slice(w * 576, (w + 1) * 576)
        qs, ds_ = stacked(q[rows] * BF(0.125)), stacked(down[rows])
        scores = dot(qs, k[rows], NT) + bias[four, :]
        exps = jnp.exp(scores - jnp.max(scores, -1, keepdims=True))
        probs = exps * (1.0 / jnp.sum(exps, -1, keepdims=True))
        probs_low = probs.astype(BF)
        att_s[rows, :] = unstacked(dot(probs_low, v[rows])).astype(BF)
        dp = dot(ds_, v[rows], NT)
        gv_s[rows, :] = dot(probs_low, ds_, TN).astype(BF)
        grad = probs * (dp - jnp.sum(dp * probs, -1, keepdims=True))
        o_ds[four, :] = grad
        grad_low = grad.astype(BF)
        gq_s[rows, :] = unstacked(dot(grad_low, k[rows]) * 0.125).astype(BF)
        gk_s[rows, :] = dot(grad_low, qs, TN).astype(BF)

    att, gq, gk, gv = att_s[...], gq_s[...], gk_s[...], gv_s[...]
    wo = dot(att, cot, TN)
    first = [dot(hidden, gq, TN), dot(hidden, gk, TN)]
    second = [dot(hidden, gv, TN), jnp.concatenate([wo[:, :256], wo[:, 256:]], 0)]
    core = info[1]
    for j in range(2):
        rows = slice(j * 512, (j + 1) * 512)
        keep[rows, :] = jnp.where(core == 0, first[j], second[j])
        send[rows, :] = jnp.where(core == 0, second[j], first[j]).astype(BF)

def terms_kernel(att, gq, gk, gv, w_qkv, back, terms):
    hid_part = dot(gq[...], w_qkv[0], NT) + dot(gk[...], w_qkv[1], NT) + dot(gv[...], w_qkv[2], NT)
    hid_part = hid_part.astype(BF)
    for a in range(2):
        rows = slice(a * 288, (a + 1) * 288)
        terms[rows, 0:256] = dot(back[a], att[rows, :]).astype(BF)
        terms[rows, 256:768] = dot(back[a], hid_part[rows]).astype(BF)


def core_sum_kernel(keep, recv, total, held, sems):
    copies = []
    for k in range(4):
        rows = slice(k * 256, (k + 1) * 256)
        held[k] = (keep[rows, :] + recv[rows, :].astype(F32)).astype(BF)
        sent(copies, held.at[k], total.at[k], sems.at[k])
    finish(copies)


def y_sum_kernel(parts, b_keep, b_recv, message, held, sems):
    copies = []
    for j in range(8):
        rows = slice(j * 32, (j + 1) * 32)
        total = parts[0, rows, :].astype(F32)
        for k in range(1, 4):
            total = total + parts[k, rows, :].astype(F32)
        held[j, :, 0:256] = total.astype(BF)
        held[j, :, 256:384] = (b_keep[rows, :].astype(F32) + b_recv[rows, :].astype(F32)).astype(BF)
        sent(copies, held.at[j], message.at[j], sems.at[j])
    finish(copies)


def z_sum_kernel(parts, mine, bias):
    total = parts[0].astype(F32)
    for j in range(1, 8):
        total = total + parts[j].astype(F32)
    mine[...] = total[:, 0:256].astype(BF)
    bias[...] = total[:, 256:384].astype(BF)


def x_sum_kernel(mine, recv, bias, out, held, sems):
    held[:, 0:256] = (mine[...].astype(F32) + recv[...].astype(F32)).astype(BF)
    held[:, 256:384] = bias[...]
    copies = []
    for j in range(8):
        sent(copies, held, out.at[j], sems.at[j])
    finish(copies)


def pair_kernel(terms, others, w_out, w_other, o_own, o_lon, o_lat, o_cor, token):
    token[...] = jnp.zeros_like(token)
    out = dot(terms[:, 0:256], w_out[...]).astype(BF).astype(F32)
    out = out + dot(others[:, 0:256], w_other[...]).astype(BF).astype(F32)
    hid = terms[:, 256:768].astype(F32) + others[:, 256:768].astype(F32)
    for j, rows in enumerate((out, hid)):
        o_own[j] = jnp.concatenate([rows[0:144], rows[288:360]], 0).astype(BF)
        o_lon[j] = jnp.concatenate([rows[144:288], rows[360:432]], 0).astype(BF)
        o_lat[j] = rows[432:504].astype(BF)
        o_cor[j] = rows[504:576].astype(BF)


def spread_kernel(parts, b_half, out, held, sems):
    for j in range(8):
        rows = slice(j * 32, (j + 1) * 32)
        held[rows, :] = parts[j, :, 0:256]
        b_half[rows, :] = parts[j, :, 256:384]
    copies = []
    for k in range(4):
        sent(copies, held, out.at[k], sems.at[k])
    finish(copies)


def gain_kernel(info, mine, w_qkv, out):
    rows = mine[...].astype(F32)
    w0, w1, w2 = [w_qkv[j].astype(F32) for j in range(3)]
    total = jnp.where(info[1] == 0, rows[:512] * w0 + rows[512:] * w1, rows[:512] * w2)
    total = total[:, 0:128] + total[:, 128:256]
    high = total.astype(BF)
    low = (total - high.astype(F32)).astype(BF)
    ones = jnp.ones((8, 128), BF)
    out[...] = dot(ones, high, NT) + dot(ones, low, NT)


def gain_sum_kernel(mine, other, mine_tp, other_tp, gain, out):
    total = (mine[0:1, :] + other[0:1, :]) + (mine_tp[0:1, :] + other_tp[0:1, :])
    out[...] = total / gain[...]


def bias_out_kernel(info, mine, other, grad_bias, token, rows, flat):
    token[...] = jnp.zeros_like(token)
    rows[0:256, :] = jnp.where(info[1] == 0, mine[...], other[...]).astype(F32)
    rows[256:512, :] = jnp.where(info[1] == 0, other[...], mine[...]).astype(F32)
    for s_t in range(2):
        for j in range(12):
            at = (s_t * 12 + j) * 138
            flat[:, at : at + 115] = rows[pl.ds(s_t * 16 + j, 16, stride=32), :][:, 0:115]
            last = rows[pl.ds(s_t * 16 + 12 + j // 3, 16, stride=32), :]
            flat[:, at + 115 : at + 138] = last[:, j % 3 * 23 : j % 3 * 23 + 23]
    grad_bias[...] = flat[...].reshape(grad_bias.shape)


def weights_kernel(info, mine, other, token, wqkv, wout, held, held_out, sems):
    token[...] = jnp.zeros_like(token)
    first = jnp.where(info[1] == 0, mine[...], other[...]).astype(F32)
    second = jnp.where(info[1] == 0, other[...], mine[...]).astype(F32)
    copies = []
    for k in range(6):
        rows = pl.ds(k % 2 * 256, 256)
        half = first if k < 4 else second
        held[k] = half[k % 4 * 256 : (k % 4 + 1) * 256]
        copies.append(pltpu.make_async_copy(held.at[k], wqkv.at[k // 2, rows], sems.at[k]))
        copies[-1].start()
    held_out[:, 0:256] = second[512:768]
    held_out[:, 256:512] = second[768:]
    for k in range(2):
        rows = pl.ds(k * 128, 128)
        copies.append(pltpu.make_async_copy(held_out.at[rows], wout.at[rows], sems.at[6 + k]))
        copies[-1].start()
    for copy in copies:
        copy.wait()


def bias_grad_kernel(info, ds, order, keep, send, part, entries, packed, *ends):
    entries[...] = jnp.zeros_like(entries)
    for p in range(12):
        for i in range(16):
            part[i * 12 : i * 12 + 12, :] = ds[i * WTOK + p * 12 : i * WTOK + p * 12 + 12, :]
        at = slice((11 - p) * 12, (11 - p) * 12 + WTOK)
        entries[:, at] = entries[:, at] + part[...]
    total = entries[...].astype(BF)
    packed[...] = jnp.zeros_like(packed)
    for s_u in range(2):
        rows = dot(total, order[s_u], NT)
        for half in range(32):
            at = half * 16 + s_u * 6
            packed[at : at + 6, 0:115] = rows[half * 6 : half * 6 + 6, 0:115]
        for q in range(3):
            last = ends[s_u * 3 + q]
            last[...] = jnp.zeros_like(last)
            last[:, q * 23 : q * 23 + 23] = rows[:, 115:138]
    for k in range(4):
        row = jnp.zeros((32, 128), F32)
        for q in range(3):
            s_u, r_t = (k * 3 + q) // 6, (k * 3 + q) % 6
            row = row + ends[s_u * 3 + q][pl.ds(r_t, 32, stride=6), :]
        packed[pl.ds(12 + k, 32, stride=16), :] = row
    mine, other = packed[0:256, :], packed[256:512, :]
    keep[...] = jnp.where(info[1] == 0, mine, other).astype(BF)
    send[...] = jnp.where(info[1] == 0, other, mine).astype(BF)


def final_kernel(latent, cot, gain, own, lon, lat, cor, token, output, grad, held, sems):
    token[...] = jnp.zeros_like(token)
    copies = []
    for k in (1, 3, 0, 2):
        ref = (own, lon, lat, cor)[k]
        out_terms, hid_terms = ref[0].astype(F32), ref[1].astype(F32)
        start = 0
        for by_lon, by_lat in PLACES[k]:
            tile = latent[by_lon, by_lat]
            values = flat(tile).astype(F32)
            rows = slice(start, start + values.shape[0])
            start += values.shape[0]
            held[0, by_lon, by_lat] = (values + out_terms[rows]).astype(BF).reshape(tile.shape)
            shifted = values - jnp.mean(values, -1, keepdims=True)
            inv_std = lax.rsqrt(jnp.mean(shifted * shifted, -1, keepdims=True) + 1e-05)
            normed = shifted * inv_std
            scaled = hid_terms[rows] * gain[...]
            inner = scaled - jnp.mean(scaled, -1, keepdims=True) - normed * jnp.mean(scaled * normed, -1, keepdims=True)
            above = flat(cot[by_lon, by_lat]).astype(F32)
            held[1, by_lon, by_lat] = (above + inv_std * inner).astype(BF).reshape(tile.shape)
        if k >= 2:
            for j, ref in enumerate((output, grad)):
                for first in (0, 3):
                    rows = pl.ds(first + (6 if k == 2 else 0), 3)
                    sent(copies, held.at[j, rows], ref.at[rows], sems.at[len(copies)])
    finish(copies)


def moved(value, by_lon, by_lat):
    n_lon, n_lat = lax.axis_size("lon"), lax.axis_size("lat")
    flip = 1 if by_lat else 0
    pairs = [
        ((i * n_lat + j) * 2 + k, ((i + by_lon) % n_lon * n_lat + (j + by_lat) % n_lat) * 2 + (k ^ flip))
        for i in range(n_lon)
        for j in range(n_lat)
        for k in range(2)
    ]
    return lax.ppermute(value, ("lon", "lat", "tp"), pairs)


def swapped(value, lon_bits, lat_bits):
    n_lon, n_lat = lax.axis_size("lon"), lax.axis_size("lat")
    pairs = [(i * n_lat + j, (i ^ lon_bits) * n_lat + (j ^ lat_bits)) for i in range(n_lon) for j in range(n_lat)]
    return lax.ppermute(value, ("lon", "lat"), pairs)


def across_y(value):
    n_lat = lax.axis_size("lat")
    groups = [list(range(x, n_lat, 2)) for x in range(2)]
    return lax.all_to_all(value, "lat", 0, 0, axis_index_groups=groups)


def across_z(value):
    n_lon = lax.axis_size("lon")
    groups = [list(range(core, n_lon, 2)) for core in range(2)]
    return lax.all_to_all(value, "lon", 0, 0, axis_index_groups=groups)


def other_group(value):
    return lax.ppermute(value, "tp", [(0, 1), (1, 0)])


def other_group_and_core(value):
    n_lon = lax.axis_size("lon")
    return lax.ppermute(value, ("lon", "tp"), [(i * 2 + j, (i ^ 1) * 2 + (j ^ 1)) for i in range(n_lon) for j in range(2)])


def on_device(latent, cotangent, ln_gain, w_qkv, w_out, bias_table):
    place, back = jnp.asarray(TO_WINDOW, BF), jnp.asarray(TO_WINDOW.transpose(0, 2, 1), BF)
    order = jnp.asarray(ORDER, BF)
    order_halves = jnp.asarray(ORDER.reshape(2, 138, 276), BF)
    i_lon, i_lat = lax.axis_index("lon"), lax.axis_index("lat")
    last = (i_lat == lax.axis_size("lat") - 1).astype(jnp.int32)
    core = i_lon % 2
    info = jnp.stack([last, core]).astype(jnp.int32)
    gain = ln_gain.reshape(1, 512)

    part = lambda n: ((2, n, 512), BF)
    halos = [part(216), part(72), part(72)]
    s_lon, s_lat, s_cor = call(
        halo_kernel,
        [],
        [],
        [pltpu.VMEM((2,) + latent.shape, BF)]
        + [pltpu.VMEM(shape, BF) for shape, _ in halos]
        + [pltpu.SemaphoreType.DMA((8,)), pltpu.SemaphoreType.DMA((6,))],
        smem=0,
        mib=60,
        hbm=[latent, cotangent],
        hbm_outs=halos,
    )
    in_lon, in_lat, in_cor = moved(s_lon, -1, 0), moved(s_lat, 0, -1), moved(s_cor, -1, -1)

    bias, w_copy = call(
        bias_kernel,
        [((16 * WTOK, WTOK), F32), (w_out.shape, BF)],
        [info, bias_table, order, w_out],
        [pltpu.VMEM((192, 276), F32)] * 2 + [pltpu.VMEM((192, 128), F32)] * 3,
        us=2,
    )
    w_other = other_group(w_copy)

    keep, send, ds, att, gq, gk, gv = call(
        main_kernel,
        [((1024, 256), F32), ((1024, 256), BF), ((16 * WTOK, WTOK), F32)] + [((576, 256), BF)] * 4,
        [info, latent, cotangent, in_lon, in_lat, in_cor, place, gain, w_qkv, w_out, bias],
        [pltpu.VMEM((576, 512), F32)],
        us=9,
        mib=32,
    )
    recv = swapped(send, 1, 0)
    (terms,) = call(terms_kernel, [((576, 768), BF)], [att, gq, gk, gv, w_qkv, back], smem=0, after=[w_other], us=2)
    others = other_group(terms)
    own, s_lon, s_lat, s_cor, paired = call(
        pair_kernel, [part(216)] + halos + [TOKEN], [terms, others, w_out, w_other], smem=0, us=30
    )

    (total,) = call(
        core_sum_kernel,
        [],
        [keep, recv],
        [pltpu.VMEM((4, 256, 256), BF), pltpu.SemaphoreType.DMA((4,))],
        smem=0,
        after=[terms],
        us=0.5,
        hbm_outs=[((4, 256, 256), BF)],
    )
    parts = across_y(total)
    b_keep, b_send = call(
        bias_grad_kernel,
        [((256, 128), BF)] * 2,
        [info, ds, order_halves],
        [pltpu.VMEM((192, WTOK), F32), pltpu.VMEM((192, 276), F32), pltpu.VMEM((512, 128), F32)]
        + [pltpu.VMEM((192, 128), F32)] * 6,
        us=2.5,
    )
    b_recv = swapped(b_send, 1, 0)
    (message,) = call(
        y_sum_kernel,
        [],
        [parts, b_keep, b_recv],
        [pltpu.VMEM((8, 32, 384), BF), pltpu.SemaphoreType.DMA((8,))],
        smem=0,
        hbm_outs=[((8, 32, 384), BF)],
    )
    x_mine, b_sum = call(
        z_sum_kernel, [((32, 256), BF), ((32, 128), BF)], [across_z(message)], smem=0, after=[paired], us=1
    )
    (copies,) = call(
        x_sum_kernel,
        [],
        [x_mine, swapped(x_mine, 0, 1), b_sum],
        [pltpu.VMEM((32, 384), BF), pltpu.SemaphoreType.DMA((8,))],
        smem=0,
        hbm_outs=[((8, 32, 384), BF)],
    )
    r_lon, r_lat, r_cor = moved(s_lon, 1, 0), moved(s_lat, 0, 1), moved(s_cor, 1, 1)

    placed, output, grad_latent = call(
        final_kernel,
        [TOKEN],
        [latent, cotangent, gain, own, r_lon, r_lat, r_cor],
        [pltpu.VMEM((2,) + latent.shape, BF), pltpu.SemaphoreType.DMA((8,))],
        hbm_outs=[(latent.shape, BF)] * 2,
        smem=0,
        us=30,
    )

    b_half, copies = call(
        spread_kernel,
        [((256, 128), BF)],
        [across_z(copies)],
        [pltpu.VMEM((256, 256), BF), pltpu.SemaphoreType.DMA((4,))],
        smem=0,
        hbm_outs=[((4, 256, 256), BF)],
    )
    mine = across_y(copies).reshape(1024, 256)
    b_other = swapped(b_half, 1, 0)
    grad_bias, done = call(
        bias_out_kernel,
        [(bias_table.shape, F32), TOKEN],
        [info, b_half, b_other],
        [pltpu.VMEM((512, 128), F32), pltpu.VMEM((16, 3312), F32)],
        after=[placed],
    )

    (g_mine,) = call(
        gain_kernel, [((8, 512), F32)], [info, mine, w_qkv], after=[done], us=30
    )
    g_parts = [g_mine, swapped(g_mine, 1, 0), other_group(g_mine), other_group_and_core(g_mine)]
    done, grad_wqkv, grad_wout = call(
        weights_kernel,
        [TOKEN],
        [info, mine, swapped(mine, 1, 0)],
        [pltpu.VMEM((6, 256, 256), F32), pltpu.VMEM((256, 512), F32), pltpu.SemaphoreType.DMA((8,))],
        hbm_outs=[((3, 512, 256), F32), ((256, 512), F32)],
        us=2,
    )
    (grad_gain,) = call(
        gain_sum_kernel, [((1, 512), F32)], [*g_parts, gain], smem=0, after=[done]
    )
    grad_gain = grad_gain.reshape(512)
    return output, grad_latent, grad_gain, grad_wqkv, grad_wout, grad_bias


def solution(mesh):
    specs = (
        P("lon", "lat", None, None),
        P("lon", "lat", None, None),
        P(),
        P(None, None, "tp"),
        P("tp", None),
        P("lat", None, "tp", None),
    )
    return jax.shard_map(on_device, mesh=mesh, in_specs=specs, out_specs=specs, check_vma=False)
```

```python
import jax
import jax.numpy as jnp
import numpy as np
from jax import lax
from jax.experimental import pallas as pl
from jax.experimental.pallas import tpu as pltpu
from jax.sharding import PartitionSpec as P

BF = jnp.bfloat16
F32 = jnp.float32
WTOK = 144
OFFS = 23
PAIRS = 16 * WTOK + 8
ROOM = 192 + 8
NT = (((1,), (1,)), ((), ()))
TN = (((0,), (0,)), ((), ()))


def section_row(lon, lat, lev):
    if lat < 6:
        return (lon >= 6) * 144 + (lon % 6 * 6 + lat) * 4 + lev
    return (lat >= 9) * 144 + (lon >= 6) * 72 + (lon % 6 * 3 + lat % 3) * 4 + lev


def placement():
    place = np.zeros((2, 288, 288), np.float32)
    for a in range(2):
        for b in range(2):
            for p in range(12):
                for s in range(2):
                    for r in range(6):
                        row = b * WTOK + p * 12 + s * 6 + r
                        place[a, row, section_row(p, a * 6 + r, (b * 2 + s + 1) % 4)] = 1
    return place


def offset_order():
    order = np.zeros((276, 276), np.float32)
    for rs in range(12):
        for k in range(OFFS):
            order[rs * OFFS + k, k * 12 + rs] = 1
    return order


TO_WINDOW = placement()
ORDER = offset_order()


def dot(a, b, dims=(((1,), (0,)), ((), ()))):
    return lax.dot_general(a, b, dims, preferred_element_type=F32)


def call(body, outs, args, scratch=(), smem=1, after=(), us=1, mib=16, hbm=(), hbm_outs=()):
    vmem, far = pl.BlockSpec(memory_space=pltpu.VMEM), pl.BlockSpec(memory_space=pltpu.HBM)
    n = len(args)
    m = n + len(hbm)

    def kernel(*refs):
        body(*refs[:m], *refs[m + len(after) :])

    return pl.pallas_call(
        kernel,
        out_shape=[jax.ShapeDtypeStruct(s, t) for s, t in [*outs, *hbm_outs]],
        in_specs=[pl.BlockSpec(memory_space=pltpu.SMEM)] * smem
        + [vmem] * (n - smem)
        + [far] * len(hbm)
        + [pl.BlockSpec(memory_space=pl.ANY)] * len(after),
        out_specs=[vmem] * len(outs) + [far] * len(hbm_outs),
        scratch_shapes=list(scratch),
        compiler_params=pltpu.CompilerParams(vmem_limit_bytes=mib * 1024 * 1024),
        cost_estimate=pl.CostEstimate(flops=int(us * 1e9), bytes_accessed=0, transcendentals=0),
    )(*args, *hbm, *after)


TOKEN = ((8, 128), F32)


LOW_LON, LOW_LAT, HIGH_LON, MID_LAT, HIGH_LAT = slice(0, 6), slice(0, 3), slice(6, 12), slice(3, 9), slice(9, 12)
PLACES = (
    ((HIGH_LON, MID_LAT), (HIGH_LON, HIGH_LAT)),
    ((LOW_LON, MID_LAT), (LOW_LON, HIGH_LAT)),
    ((HIGH_LON, LOW_LAT),),
    ((LOW_LON, LOW_LAT),),
)


def flat(tile):
    return tile.reshape(-1, tile.shape[-1])


def sent(copies, source, target, sem):
    copies.append(pltpu.make_async_copy(source, target, sem))
    copies[-1].start()


def finish(copies):
    for copy in copies:
        copy.wait()


def halo_kernel(latent, cot, o_lon, o_lat, o_cor, tiles, h_lon, h_lat, h_cor, in_sems, out_sems):
    arrived, copies = [], []
    for first in (0, 3, 6, 9):
        for j, grid in enumerate((latent, cot)):
            rows = pl.ds(first, 3)
            sent(arrived, grid.at[rows], tiles.at[j, rows], in_sems.at[len(arrived)])
    finish(arrived[:4])
    for places, held, ref in ((PLACES[1], h_lon, o_lon), (PLACES[3], h_cor, o_cor), (PLACES[2], h_lat, o_lat)):
        if held is h_lat:
            finish(arrived[4:])
        for j in range(2):
            held[j] = jnp.concatenate([flat(tiles[j, lon, lat]) for lon, lat in places], 0)
            sent(copies, held.at[j], ref.at[j], out_sems.at[len(copies)])
    finish(copies)


def bias_kernel(info, table, order, w_out, bias, w_copy, raw, entries, t0, t1, t2):
    w_copy[...] = w_out[...]
    flat = table[...].reshape(16, 3312)
    for s_t in range(2):
        for s_u in range(2):
            for r_t in range(6):
                at = ((s_t * 2 + s_u) * 6 + r_t) * 138
                row = (s_t * 6 + r_t) * 16
                raw[row : row + 16, s_u * 138 : s_u * 138 + 138] = flat[:, at : at + 138]
    full = raw[...]
    high = full.astype(BF)
    rest = full - high.astype(F32)
    mid = rest.astype(BF)
    low = (rest - mid.astype(F32)).astype(BF)
    wide = dot(low, order[...]) + dot(mid, order[...]) + dot(high, order[...])
    t0[0:192, :] = wide[:, 0:128]
    t1[0:192, :] = wide[:, 128:256]
    t2[0:192, 0:20] = wide[:, 256:276]
    for i in range(16):
        at, rows = pl.ds(i, 12, stride=16), slice(i * 12, i * 12 + 12)
        entries[rows, 0:128] = t0[at, :]
        entries[rows, 128:256] = t1[at, :]
        entries[rows, 256:276] = t2[at, :][:, 0:20]
    row = lax.broadcasted_iota(jnp.int32, (192, WTOK), 0)
    col = lax.broadcasted_iota(jnp.int32, (192, WTOK), 1)
    rs_t, rs_u, which = row % 12, col % 12, row // 12
    s_t, s_u = (rs_t >= 6).astype(jnp.int32), (rs_u >= 6).astype(jnp.int32)
    edge_t = (rs_t - s_t * 6 >= 3).astype(jnp.int32)
    edge_u = (rs_u - s_u * 6 >= 3).astype(jnp.int32)
    last_lat = (which >= 8).astype(jnp.int32) * info[0]
    last_lev = ((which % 8) >= 4).astype(jnp.int32)
    barred = (last_lat * (edge_t - edge_u) != 0) | (last_lev * (s_t - s_u) != 0)
    for p in range(12):
        at = jnp.where(barred, -jnp.inf, entries[0:192, (11 - p) * 12 : (11 - p) * 12 + WTOK])
        for i in range(16):
            bias[i * WTOK + p * 12 : i * WTOK + p * 12 + 12, :] = at[i * 12 : i * 12 + 12]


def main_kernel(info, latent, cotangent, lon, lat, cor, place, gain, w_qkv, w_out, bias,
                keep, send, o_ds, att_s, gq_s, gk_s, gv_s, joined):
    def gathered(which):
        grid = (latent, cotangent)[which]
        beside = lon[which].astype(F32)
        parts = (flat(grid[HIGH_LON, MID_LAT]), beside[0:144], flat(grid[HIGH_LON, HIGH_LAT]), beside[144:216])
        start = 0
        for rows in (*parts, lat[which], cor[which]):
            joined[start : start + rows.shape[0], :] = rows.astype(F32)
            start += rows.shape[0]
        rows = joined[...].astype(BF)
        return jnp.concatenate([dot(place[a], rows[a * 288 : (a + 1) * 288]) for a in range(2)], 0)

    values = gathered(0)
    cot = gathered(1).astype(BF)
    shifted = values - jnp.mean(values, -1, keepdims=True)
    normed = shifted * lax.rsqrt(jnp.mean(shifted * shifted, -1, keepdims=True) + 1e-05)
    hidden = (normed * gain[...]).astype(BF)
    q, k, v = [dot(hidden, w_qkv[j]).astype(BF) for j in range(3)]
    down = dot(cot, w_out[...], NT).astype(BF)
    head = lax.broadcasted_iota(jnp.int32, (WTOK, 256), 1) // 64

    def stacked(rows):
        return jnp.concatenate([jnp.where(head == h, rows, jnp.zeros_like(rows)) for h in range(4)], 0)

    def unstacked(rows):
        total = jnp.zeros((WTOK, 256), F32)
        for h in range(4):
            total = jnp.where(head == h, rows[h * WTOK : (h + 1) * WTOK], total)
        return total

    for w in range(4):
        rows = slice(w * WTOK, (w + 1) * WTOK)
        four = slice(w * 576, (w + 1) * 576)
        qs, ds_ = stacked(q[rows]), stacked(down[rows])
        scores = dot(qs, k[rows], NT) * 0.125 + bias[four, :]
        exps = jnp.exp(scores - jnp.max(scores, -1, keepdims=True))
        probs = exps / jnp.sum(exps, -1, keepdims=True)
        probs_low = probs.astype(BF)
        att_s[rows, :] = unstacked(dot(probs_low, v[rows])).astype(BF)
        dp = dot(ds_, v[rows], NT)
        gv_s[rows, :] = dot(probs_low, ds_, TN).astype(BF)
        grad = probs * (dp - jnp.sum(dp * probs, -1, keepdims=True))
        o_ds[four, :] = grad
        grad_low = grad.astype(BF)
        gq_s[rows, :] = unstacked(dot(grad_low, k[rows]) * 0.125).astype(BF)
        gk_s[rows, :] = (dot(grad_low, qs, TN) * 0.125).astype(BF)

    att, gq, gk, gv = att_s[...], gq_s[...], gk_s[...], gv_s[...]
    wo = dot(att, cot, TN)
    first = [dot(hidden, gq, TN), dot(hidden, gk, TN)]
    second = [dot(hidden, gv, TN), jnp.concatenate([wo[:, :256], wo[:, 256:]], 0)]
    core = info[1]
    for j in range(2):
        rows = slice(j * 512, (j + 1) * 512)
        keep[rows, :] = jnp.where(core == 0, first[j], second[j])
        send[rows, :] = jnp.where(core == 0, second[j], first[j]).astype(BF)

def terms_kernel(att, gq, gk, gv, w_qkv, back, terms):
    hid_part = dot(gq[...], w_qkv[0], NT) + dot(gk[...], w_qkv[1], NT) + dot(gv[...], w_qkv[2], NT)
    hid_part = hid_part.astype(BF)
    for a in range(2):
        rows = slice(a * 288, (a + 1) * 288)
        terms[rows, 0:256] = dot(back[a], att[rows, :]).astype(BF)
        terms[rows, 256:768] = dot(back[a], hid_part[rows]).astype(BF)


def core_sum_kernel(keep, recv, total, held, sems):
    copies = []
    for k in range(4):
        rows = slice(k * 256, (k + 1) * 256)
        held[k] = (keep[rows, :] + recv[rows, :].astype(F32)).astype(BF)
        sent(copies, held.at[k], total.at[k], sems.at[k])
    finish(copies)


def y_sum_kernel(parts, b_keep, b_recv, message, held, sems):
    copies = []
    for j in range(8):
        rows = slice(j * 32, (j + 1) * 32)
        total = parts[0, rows, :].astype(F32)
        for k in range(1, 4):
            total = total + parts[k, rows, :].astype(F32)
        held[j, :, 0:256] = total.astype(BF)
        held[j, :, 256:384] = (b_keep[rows, :].astype(F32) + b_recv[rows, :].astype(F32)).astype(BF)
        sent(copies, held.at[j], message.at[j], sems.at[j])
    finish(copies)


def z_sum_kernel(parts, mine, bias):
    total = parts[0].astype(F32)
    for j in range(1, 8):
        total = total + parts[j].astype(F32)
    mine[...] = total[:, 0:256].astype(BF)
    bias[...] = total[:, 256:384].astype(BF)


def x_sum_kernel(mine, recv, bias, out, held, sems):
    held[:, 0:256] = (mine[...].astype(F32) + recv[...].astype(F32)).astype(BF)
    held[:, 256:384] = bias[...]
    copies = []
    for j in range(8):
        sent(copies, held, out.at[j], sems.at[j])
    finish(copies)


def pair_kernel(terms, others, w_out, w_other, o_own, o_lon, o_lat, o_cor, token):
    token[...] = jnp.zeros_like(token)
    out = dot(terms[:, 0:256], w_out[...]).astype(BF).astype(F32)
    out = out + dot(others[:, 0:256], w_other[...]).astype(BF).astype(F32)
    hid = terms[:, 256:768].astype(F32) + others[:, 256:768].astype(F32)
    for j, rows in enumerate((out, hid)):
        o_own[j] = jnp.concatenate([rows[0:144], rows[288:360]], 0).astype(BF)
        o_lon[j] = jnp.concatenate([rows[144:288], rows[360:432]], 0).astype(BF)
        o_lat[j] = rows[432:504].astype(BF)
        o_cor[j] = rows[504:576].astype(BF)


def spread_kernel(parts, b_half, out, held, sems):
    for j in range(8):
        rows = slice(j * 32, (j + 1) * 32)
        held[rows, :] = parts[j, :, 0:256]
        b_half[rows, :] = parts[j, :, 256:384]
    copies = []
    for k in range(4):
        sent(copies, held, out.at[k], sems.at[k])
    finish(copies)


def gain_kernel(info, mine, w_qkv, out):
    rows = mine[...].astype(F32)
    w0, w1, w2 = [w_qkv[j].astype(F32) for j in range(3)]
    total = jnp.where(info[1] == 0, rows[:512] * w0 + rows[512:] * w1, rows[:512] * w2)
    total = total[:, 0:128] + total[:, 128:256]
    high = total.astype(BF)
    low = (total - high.astype(F32)).astype(BF)
    ones = jnp.ones((8, 128), BF)
    out[...] = dot(ones, high, NT) + dot(ones, low, NT)


def gain_sum_kernel(mine, other, mine_tp, other_tp, gain, out):
    total = (mine[0:1, :] + other[0:1, :]) + (mine_tp[0:1, :] + other_tp[0:1, :])
    out[...] = total / gain[...]


def bias_out_kernel(info, mine, other, grad_bias, token, rows, flat):
    token[...] = jnp.zeros_like(token)
    rows[0:256, :] = jnp.where(info[1] == 0, mine[...], other[...]).astype(F32)
    rows[256:512, :] = jnp.where(info[1] == 0, other[...], mine[...]).astype(F32)
    for s_t in range(2):
        for j in range(12):
            at = (s_t * 12 + j) * 138
            flat[:, at : at + 115] = rows[pl.ds(s_t * 16 + j, 16, stride=32), :][:, 0:115]
            last = rows[pl.ds(s_t * 16 + 12 + j // 3, 16, stride=32), :]
            flat[:, at + 115 : at + 138] = last[:, j % 3 * 23 : j % 3 * 23 + 23]
    grad_bias[...] = flat[...].reshape(grad_bias.shape)


def weights_kernel(info, mine, other, token, wqkv, wout, held, held_out, sems):
    token[...] = jnp.zeros_like(token)
    first = jnp.where(info[1] == 0, mine[...], other[...]).astype(F32)
    second = jnp.where(info[1] == 0, other[...], mine[...]).astype(F32)
    copies = []
    for k in range(6):
        rows = pl.ds(k % 2 * 256, 256)
        half = first if k < 4 else second
        held[k] = half[k % 4 * 256 : (k % 4 + 1) * 256]
        copies.append(pltpu.make_async_copy(held.at[k], wqkv.at[k // 2, rows], sems.at[k]))
        copies[-1].start()
    held_out[:, 0:256] = second[512:768]
    held_out[:, 256:512] = second[768:]
    for k in range(2):
        rows = pl.ds(k * 128, 128)
        copies.append(pltpu.make_async_copy(held_out.at[rows], wout.at[rows], sems.at[6 + k]))
        copies[-1].start()
    for copy in copies:
        copy.wait()


def bias_grad_kernel(info, ds, order, keep, send, part, entries, packed, *ends):
    entries[...] = jnp.zeros_like(entries)
    for p in range(12):
        for i in range(16):
            part[i * 12 : i * 12 + 12, :] = ds[i * WTOK + p * 12 : i * WTOK + p * 12 + 12, :]
        at = slice((11 - p) * 12, (11 - p) * 12 + WTOK)
        entries[:, at] = entries[:, at] + part[0:192, :]
    total = entries[...].astype(BF)
    packed[...] = jnp.zeros_like(packed)
    for s_u in range(2):
        rows = dot(total, order[s_u], NT)
        for half in range(32):
            at = half * 16 + s_u * 6
            packed[at : at + 6, 0:115] = rows[half * 6 : half * 6 + 6, 0:115]
        for q in range(3):
            last = ends[s_u * 3 + q]
            last[...] = jnp.zeros_like(last)
            last[:, q * 23 : q * 23 + 23] = rows[:, 115:138]
    for k in range(4):
        row = jnp.zeros((32, 128), F32)
        for q in range(3):
            s_u, r_t = (k * 3 + q) // 6, (k * 3 + q) % 6
            row = row + ends[s_u * 3 + q][pl.ds(r_t, 32, stride=6), :]
        packed[pl.ds(12 + k, 32, stride=16), :] = row
    mine, other = packed[0:256, :], packed[256:512, :]
    keep[...] = jnp.where(info[1] == 0, mine, other).astype(BF)
    send[...] = jnp.where(info[1] == 0, other, mine).astype(BF)


def final_kernel(latent, cot, gain, own, lon, lat, cor, token, output, grad, held, sems):
    token[...] = jnp.zeros_like(token)
    copies = []
    for k in (1, 3, 0, 2):
        ref = (own, lon, lat, cor)[k]
        out_terms, hid_terms = ref[0].astype(F32), ref[1].astype(F32)
        start = 0
        for by_lon, by_lat in PLACES[k]:
            tile = latent[by_lon, by_lat]
            values = flat(tile).astype(F32)
            rows = slice(start, start + values.shape[0])
            start += values.shape[0]
            held[0, by_lon, by_lat] = (values + out_terms[rows]).astype(BF).reshape(tile.shape)
            shifted = values - jnp.mean(values, -1, keepdims=True)
            inv_std = lax.rsqrt(jnp.mean(shifted * shifted, -1, keepdims=True) + 1e-05)
            normed = shifted * inv_std
            scaled = hid_terms[rows] * gain[...]
            inner = scaled - jnp.mean(scaled, -1, keepdims=True) - normed * jnp.mean(scaled * normed, -1, keepdims=True)
            above = flat(cot[by_lon, by_lat]).astype(F32)
            held[1, by_lon, by_lat] = (above + inv_std * inner).astype(BF).reshape(tile.shape)
        if k >= 2:
            for j, ref in enumerate((output, grad)):
                for first in (0, 3):
                    rows = pl.ds(first + (6 if k == 2 else 0), 3)
                    sent(copies, held.at[j, rows], ref.at[rows], sems.at[len(copies)])
    finish(copies)


def moved(value, by_lon, by_lat):
    n_lon, n_lat = lax.axis_size("lon"), lax.axis_size("lat")
    flip = 1 if by_lat else 0
    pairs = [
        ((i * n_lat + j) * 2 + k, ((i + by_lon) % n_lon * n_lat + (j + by_lat) % n_lat) * 2 + (k ^ flip))
        for i in range(n_lon)
        for j in range(n_lat)
        for k in range(2)
    ]
    return lax.ppermute(value, ("lon", "lat", "tp"), pairs)


def swapped(value, lon_bits, lat_bits):
    n_lon, n_lat = lax.axis_size("lon"), lax.axis_size("lat")
    pairs = [(i * n_lat + j, (i ^ lon_bits) * n_lat + (j ^ lat_bits)) for i in range(n_lon) for j in range(n_lat)]
    return lax.ppermute(value, ("lon", "lat"), pairs)


def across_y(value):
    n_lat = lax.axis_size("lat")
    groups = [list(range(x, n_lat, 2)) for x in range(2)]
    return lax.all_to_all(value, "lat", 0, 0, axis_index_groups=groups)


def across_z(value):
    n_lon = lax.axis_size("lon")
    groups = [list(range(core, n_lon, 2)) for core in range(2)]
    return lax.all_to_all(value, "lon", 0, 0, axis_index_groups=groups)


def other_group(value):
    return lax.ppermute(value, "tp", [(0, 1), (1, 0)])


def other_group_and_core(value):
    n_lon = lax.axis_size("lon")
    return lax.ppermute(value, ("lon", "tp"), [(i * 2 + j, (i ^ 1) * 2 + (j ^ 1)) for i in range(n_lon) for j in range(2)])


def on_device(latent, cotangent, ln_gain, w_qkv, w_out, bias_table):
    place, back = jnp.asarray(TO_WINDOW, BF), jnp.asarray(TO_WINDOW.transpose(0, 2, 1), BF)
    order = jnp.asarray(ORDER, BF)
    order_halves = jnp.asarray(ORDER.reshape(2, 138, 276), BF)
    i_lon, i_lat = lax.axis_index("lon"), lax.axis_index("lat")
    last = (i_lat == lax.axis_size("lat") - 1).astype(jnp.int32)
    core = i_lon % 2
    info = jnp.stack([last, core]).astype(jnp.int32)
    gain = ln_gain.reshape(1, 512)

    part = lambda n: ((2, n, 512), BF)
    halos = [part(216), part(72), part(72)]
    s_lon, s_lat, s_cor = call(
        halo_kernel,
        [],
        [],
        [pltpu.VMEM((2,) + latent.shape, BF)]
        + [pltpu.VMEM(shape, BF) for shape, _ in halos]
        + [pltpu.SemaphoreType.DMA((8,)), pltpu.SemaphoreType.DMA((6,))],
        smem=0,
        mib=60,
        hbm=[latent, cotangent],
        hbm_outs=halos,
    )
    in_lon, in_lat, in_cor = moved(s_lon, -1, 0), moved(s_lat, 0, -1), moved(s_cor, -1, -1)

    bias, w_copy = call(
        bias_kernel,
        [((PAIRS, WTOK), F32), (w_out.shape, BF)],
        [info, bias_table, order, w_out],
        [pltpu.VMEM((192, 276), F32), pltpu.VMEM((ROOM, 276), F32)] + [pltpu.VMEM((256, 128), F32)] * 3,
        us=2,
    )
    w_other = other_group(w_copy)

    keep, send, ds, att, gq, gk, gv = call(
        main_kernel,
        [((1024, 256), F32), ((1024, 256), BF), ((PAIRS, WTOK), F32)] + [((576, 256), BF)] * 4,
        [info, latent, cotangent, in_lon, in_lat, in_cor, place, gain, w_qkv, w_out, bias],
        [pltpu.VMEM((576, 512), F32)],
        us=9,
        mib=32,
    )
    recv = swapped(send, 1, 0)
    (terms,) = call(terms_kernel, [((576, 768), BF)], [att, gq, gk, gv, w_qkv, back], smem=0, after=[w_other], us=2)
    others = other_group(terms)
    own, s_lon, s_lat, s_cor, paired = call(
        pair_kernel, [part(216)] + halos + [TOKEN], [terms, others, w_out, w_other], smem=0, us=30
    )

    (total,) = call(
        core_sum_kernel,
        [],
        [keep, recv],
        [pltpu.VMEM((4, 256, 256), BF), pltpu.SemaphoreType.DMA((4,))],
        smem=0,
        after=[terms],
        us=0.5,
        hbm_outs=[((4, 256, 256), BF)],
    )
    parts = across_y(total)
    b_keep, b_send = call(
        bias_grad_kernel,
        [((256, 128), BF)] * 2,
        [info, ds, order_halves],
        [pltpu.VMEM((ROOM, WTOK), F32), pltpu.VMEM((192, 276), F32), pltpu.VMEM((512, 128), F32)]
        + [pltpu.VMEM((192, 128), F32)] * 6,
        us=2.5,
    )
    b_recv = swapped(b_send, 1, 0)
    (message,) = call(
        y_sum_kernel,
        [],
        [parts, b_keep, b_recv],
        [pltpu.VMEM((8, 32, 384), BF), pltpu.SemaphoreType.DMA((8,))],
        smem=0,
        hbm_outs=[((8, 32, 384), BF)],
    )
    x_mine, b_sum = call(
        z_sum_kernel, [((32, 256), BF), ((32, 128), BF)], [across_z(message)], smem=0, after=[paired], us=1
    )
    (copies,) = call(
        x_sum_kernel,
        [],
        [x_mine, swapped(x_mine, 0, 1), b_sum],
        [pltpu.VMEM((32, 384), BF), pltpu.SemaphoreType.DMA((8,))],
        smem=0,
        hbm_outs=[((8, 32, 384), BF)],
    )
    r_lon, r_lat, r_cor = moved(s_lon, 1, 0), moved(s_lat, 0, 1), moved(s_cor, 1, 1)

    placed, output, grad_latent = call(
        final_kernel,
        [TOKEN],
        [latent, cotangent, gain, own, r_lon, r_lat, r_cor],
        [pltpu.VMEM((2,) + latent.shape, BF), pltpu.SemaphoreType.DMA((8,))],
        hbm_outs=[(latent.shape, BF)] * 2,
        smem=0,
        us=30,
    )

    b_half, copies = call(
        spread_kernel,
        [((256, 128), BF)],
        [across_z(copies)],
        [pltpu.VMEM((256, 256), BF), pltpu.SemaphoreType.DMA((4,))],
        smem=0,
        hbm_outs=[((4, 256, 256), BF)],
    )
    mine = across_y(copies).reshape(1024, 256)
    b_other = swapped(b_half, 1, 0)
    grad_bias, done = call(
        bias_out_kernel,
        [(bias_table.shape, F32), TOKEN],
        [info, b_half, b_other],
        [pltpu.VMEM((512, 128), F32), pltpu.VMEM((16, 3312), F32)],
        after=[placed],
    )

    (g_mine,) = call(
        gain_kernel, [((8, 512), F32)], [info, mine, w_qkv], after=[done], us=30
    )
    g_parts = [g_mine, swapped(g_mine, 1, 0), other_group(g_mine), other_group_and_core(g_mine)]
    done, grad_wqkv, grad_wout = call(
        weights_kernel,
        [TOKEN],
        [info, mine, swapped(mine, 1, 0)],
        [pltpu.VMEM((6, 256, 256), F32), pltpu.VMEM((256, 512), F32), pltpu.SemaphoreType.DMA((8,))],
        hbm_outs=[((3, 512, 256), F32), ((256, 512), F32)],
        us=2,
    )
    (grad_gain,) = call(
        gain_sum_kernel, [((1, 512), F32)], [*g_parts, gain], smem=0, after=[done]
    )
    grad_gain = grad_gain.reshape(512)
    return output, grad_latent, grad_gain, grad_wqkv, grad_wout, grad_bias


def solution(mesh):
    specs = (
        P("lon", "lat", None, None),
        P("lon", "lat", None, None),
        P(),
        P(None, None, "tp"),
        P("tp", None),
        P("lat", None, "tp", None),
    )
    return jax.shard_map(on_device, mesh=mesh, in_specs=specs, out_specs=specs, check_vma=False)
```
